32 devices in a mesh: phase: 4 (over y, x), dp: 4 (over z), mp: 2 (over core).
Axes of the slice: x: 2, y: 2, z: 4, core: 2. Of those that a mesh axis runs over, the one named last changes fastest.
Arguments:
- text_rows: bfloat16 [512, 4096], P('dp', 'mp'), may hold values from -6 to 6
- image_rows: bfloat16 [8, 128, 1280], P('dp', ('phase', 'mp')), may hold values from -6 to 6
- tile_counts: int32 [8], P('dp'), may hold values from 1 to 4
- text_lengths: int32 [8], P('dp'), may hold values from 1 to 64
- sample_image: int32 [8], P('dp'), may hold values from 0 to 1
- norm_gain: float32 [4, 4096], P('phase'), may hold values from 0.5 to 2
- query_weight: bfloat16 [4, 4096, 1024], P('phase', 'dp', 'mp'), may hold values from -0.09375 to 0.09375
- keyval_weight: bfloat16 [4, 1280, 2, 256], P('phase', None, 'mp'), may hold values from -0.15625 to 0.15625
- output_weight: bfloat16 [4, 1024, 4096], P('phase', 'dp', 'mp'), may hold values from -0.1875 to 0.1875
- cross_gate: float32 [4], P('phase'), may hold values from -1.5 to 1.5
Outputs:
- section_states: bfloat16 [4, 512, 4096], P('phase', 'dp', 'mp')
The draws below stay inside these ranges and needn't reach their ends.
All inputs are finite; a program needn't handle non-finite values.
Results may differ from the reference program's by a relative error of at most 0.014.
Values may be sent and summed in bfloat16 or wider, within the bound.
No kernel may reach another device: no remote copies, remote signals or barrier semaphores. Data moves between devices by JAX's collectives and lax.ppermute only.
A program may use at most 64 MiB of HBM per device.

```python
import math
import jax
import jax.numpy as jnp
from jax import lax

D = 4096
HD = 128
HQ_DEV = 4
VD = 1280
TROWS = 32
MAXT = 4
SAMP = 2
TXT = 64
KVH = 2
HQ = 8
SECTIONS = 4
IMGS = 8
TOKENS = 512


def touch_ends(result, own_key, least, high):
    dims = result.shape
    index_at = [jax.random.randint(jax.random.fold_in(own_key, axis), (), 0, dims[axis]) for axis in range(len(dims))]
    result = result.at[tuple(index_at)].set(least)
    longest = dims.index(max(dims))
    index_at[longest] = (index_at[longest] + 1) % dims[longest]
    return result.at[tuple(index_at)].set(high)


def level_of(own_key, shape, split, low, high):
    def one(dim, blocks):
        steps = jax.random.uniform(jax.random.fold_in(jax.random.fold_in(own_key, 6), dim), (blocks,), jnp.float32, low / len(split), high / len(split))
        return jnp.repeat(jnp.exp(steps), shape[dim] // blocks).reshape((-1,) + (1,) * (len(shape) - dim - 1))

    factor_of = one(*split[0])
    for cut in split[1:]:
        factor_of = factor_of * one(*cut)
    return factor_of


def centred(stream_key, shape, spread, reach, shards=(), kind=jnp.bfloat16):
    drawn = spread * jax.random.normal(stream_key, shape, jnp.float32)
    if shards:
        drawn = drawn * level_of(stream_key, shape, shards, -0.22, 0.18)
    return jnp.clip(drawn, -reach, reach).astype(kind)


def setup_inputs(seed: int = 0) -> dict:
    key_of = jax.random.split(jax.random.key(seed), 11)
    text_rows = centred(key_of[0], (TOKENS, D), 1.0, 6.0, ((0, 4), (1, 2)))
    image_rows = centred(key_of[1], (IMGS, MAXT * TROWS, VD), 1.0, 6.0, ((0, 4), (1, 8)))
    tile_counts = touch_ends(jax.random.randint(key_of[2], (IMGS,), 1, MAXT + 1), jax.random.fold_in(key_of[2], 1), 1, MAXT).astype(jnp.int32)
    text_lengths = touch_ends(jax.random.randint(key_of[3], (IMGS,), 1, TXT + 1), jax.random.fold_in(key_of[3], 1), 1, TXT).astype(jnp.int32)
    sample_image = touch_ends(jax.random.randint(key_of[4], (IMGS,), 0, SAMP), jax.random.fold_in(key_of[4], 1), 0, SAMP - 1).astype(jnp.int32)
    norm_gain = jnp.clip(jnp.exp(math.log(2.0) - 1.3862944 * jax.random.uniform(key_of[5], (SECTIONS, D), jnp.float32) ** level_of(key_of[5], (SECTIONS, D), ((0, 4),), -0.2, 0.2)), 0.5, 2.0)
    query_weight = centred(key_of[6], (SECTIONS, D, HQ * HD), D ** -0.5, 0.09375, ((0, 4), (1, 4), (2, 2)))
    keyval_weight = centred(key_of[7], (SECTIONS, VD, KVH, 2 * HD), VD ** -0.5, 0.15625, ((0, 4), (2, 2)))
    output_weight = centred(key_of[8], (SECTIONS, HQ * HD, D), (HQ * HD) ** -0.5, 0.1875, ((0, 4), (1, 4), (2, 2)))
    cross_gate = jnp.clip(jax.random.uniform(key_of[9], (SECTIONS,), jnp.float32, -1.5, 1.5) * level_of(key_of[9], (SECTIONS,), ((0, 4),), -0.4, 0.0), -1.5, 1.5)
    return dict(text_rows=text_rows, image_rows=image_rows, tile_counts=tile_counts, text_lengths=text_lengths, sample_image=sample_image, norm_gain=norm_gain, query_weight=query_weight, keyval_weight=keyval_weight, output_weight=output_weight, cross_gate=cross_gate)


epsilon = 1e-05

def attend(operands):
    queries, keyval, allowed = operands
    key_part = jnp.repeat(keyval[..., :HD], HQ_DEV, axis=1).astype(jnp.float32)
    value_part = jnp.repeat(keyval[..., HD:], HQ_DEV, axis=1).astype(jnp.float32)
    scores = jnp.einsum('rhd,khd->hrk', queries.astype(jnp.float32), key_part) * float(HD) ** (-0.5)
    weighted = jnp.exp(scores) * allowed[None]
    weights = (weighted / lax.optimization_barrier(jnp.sum(weighted, axis=-1, keepdims=True))).astype(jnp.bfloat16)
    context = jnp.einsum('hrk,khd->rhd', weights.astype(jnp.float32), value_part).astype(jnp.bfloat16)
    return context.reshape(queries.shape[0], -1)

def reference(text_rows, image_rows, tile_counts, text_lengths, sample_image, norm_gain, query_weight, keyval_weight, output_weight, cross_gate):
    owners = IMGS // SAMP
    own_rows = SAMP * TXT
    key_count = MAXT * TROWS
    positions = jnp.arange(TOKENS, dtype=jnp.int32)
    live = (positions % TXT < jnp.repeat(text_lengths, TXT)).astype(jnp.float32)
    key_index = jnp.arange(SAMP * key_count, dtype=jnp.int32)
    key_image = key_index // key_count
    tiles_own = tile_counts.reshape(owners, SAMP)
    key_valid = (key_index % key_count)[None, :] < tiles_own[:, key_image] * TROWS
    row_sample = jnp.arange(own_rows, dtype=jnp.int32) // TXT
    row_image = sample_image.reshape(owners, SAMP)[:, row_sample]
    allowed = ((row_image[:, :, None] == key_image[None, None, :]) & key_valid[:, None, :]).astype(jnp.float32)
    carried = text_rows
    states = []
    for section in range(SECTIONS):
        widened = carried.astype(jnp.float32)
        mean_square = lax.optimization_barrier(jnp.mean(widened * widened, axis=-1, keepdims=True))
        normed = (widened * lax.rsqrt(mean_square + epsilon) * norm_gain[section]).astype(jnp.bfloat16)
        queries = jnp.dot(normed, query_weight[section], preferred_element_type=jnp.float32).astype(jnp.bfloat16)
        keyval = jnp.dot(image_rows.reshape(-1, VD), keyval_weight[section].reshape(VD, -1), preferred_element_type=jnp.float32).astype(jnp.bfloat16)
        keyval = keyval.reshape(owners, SAMP * key_count, KVH, 2 * HD)
        context = lax.map(attend, (queries.reshape(owners, own_rows, HQ, HD), keyval, allowed))
        attended = jnp.dot(context.reshape(TOKENS, HQ * HD), output_weight[section], preferred_element_type=jnp.float32)
        carried = (carried.astype(jnp.float32) + live[:, None] * jnp.tanh(cross_gate[section]) * attended).astype(jnp.bfloat16)
        states.append(carried)
    return jnp.stack(states)
```

```python
import jax
import jax.numpy as jnp
from jax import lax
from jax.sharding import PartitionSpec as P

HD = 128
HQ_DEV = 4
TROWS = 32
SAMP = 2
TXT = 64
LANES = 128

epsilon = 1e-05


def place_query_weight(query_weight, norm_gain, phases):
    depth, width = query_weight.shape[1:]
    gain = lax.dynamic_slice_in_dim(norm_gain[0], lax.axis_index("dp") * depth, depth, 0)
    scaled = (query_weight[0].astype(jnp.float32) * gain[:, None]).astype(jnp.bfloat16)
    scaled = scaled.reshape(phases, depth // phases, width)
    return lax.all_to_all(scaled, "phase", 0, 0, tiled=True)


def place_output_weight(output_weight, phases, dps):
    mixed = lax.all_to_all(output_weight[0], "mp", 0, 1, tiled=True)
    rows, width = mixed.shape
    feats = width // (phases * dps)
    mixed = mixed.reshape(rows, dps, phases, feats).transpose(2, 1, 0, 3)
    mixed = mixed.reshape(phases * dps, rows, feats)
    mixed = lax.all_to_all(mixed, ("phase", "dp"), 0, 0, tiled=True)
    mixed = lax.all_gather(mixed, "mp", axis=1, tiled=True)
    return mixed.reshape(phases, -1, feats)


def place_text(text_rows, phases, dps, mps):
    rows, width = text_rows.shape
    feats = width * mps // (phases * dps)
    split = text_rows.reshape(rows, dps // mps, phases, feats)
    mine = lax.dynamic_index_in_dim(split, lax.axis_index("phase"), 2, keepdims=False)
    mine = lax.all_gather(mine, "mp", axis=1, tiled=True)
    mine = lax.all_to_all(mine.transpose(1, 0, 2), "dp", 0, 0, tiled=True)
    return mine.reshape(dps * rows, feats)


def return_states(states, phases, dps, mps):
    rows, feats = states.shape[2:]
    share = rows // mps
    mine = lax.dynamic_slice_in_dim(states, lax.axis_index("mp") * share, share, 2)
    mine = mine.reshape(phases * dps, share, feats)
    mine = lax.all_to_all(mine, ("phase", "dp"), 0, 0, tiled=True)
    mine = mine.reshape(phases, dps, share, feats).transpose(2, 1, 0, 3)
    return lax.all_to_all(mine.reshape(share, -1), "mp", 1, 0, tiled=True)


def on_device(
    text_rows,
    image_rows,
    tile_counts,
    text_lengths,
    sample_image,
    norm_gain,
    query_weight,
    keyval_weight,
    output_weight,
    cross_gate,
):
    phases, dps, mps = (lax.axis_size(name) for name in ("phase", "dp", "mp"))
    width = norm_gain.shape[1]
    own_rows = text_rows.shape[0]
    part_rows = own_rows // phases
    head_width = query_weight.shape[2]

    carried = place_text(text_rows, phases, dps, mps)
    wq = place_query_weight(query_weight, norm_gain, phases)
    images = lax.all_gather(image_rows, ("phase", "mp"), axis=1, tiled=True)
    key_count = images.shape[1]
    keyval = jnp.einsum(
        "srv,vc->src", images, keyval_weight[0, :, 0, :], preferred_element_type=jnp.float32
    ).reshape(SAMP * key_count, 2 * HD)
    factor = jnp.concatenate(
        [jnp.ones((HD,), jnp.float32), jnp.broadcast_to(jnp.tanh(cross_gate), (HD,))]
    )
    keyval = (keyval * factor[None, :]).astype(jnp.bfloat16)
    keyval = lax.all_gather(keyval, "phase", axis=0, tiled=False)
    wo = place_output_weight(output_weight, phases, dps)

    key_index = jnp.arange(SAMP * key_count, dtype=jnp.int32)
    key_image = key_index // key_count
    key_pick = (key_image[:, None] == jnp.arange(SAMP, dtype=jnp.int32)[None, :]).astype(jnp.int32)
    key_valid = key_index % key_count < jnp.sum(key_pick * tile_counts[None, :], axis=1) * TROWS
    row_index = lax.axis_index("phase") * part_rows + jnp.arange(part_rows, dtype=jnp.int32)
    row_pick = ((row_index // TXT)[:, None] == jnp.arange(SAMP, dtype=jnp.int32)[None, :]).astype(
        jnp.int32
    )
    row_image = jnp.sum(row_pick * sample_image[None, :], axis=1)
    row_length = jnp.sum(row_pick * text_lengths[None, :], axis=1)
    live = (row_index % TXT < row_length).astype(jnp.float32)
    allowed = ((row_image[:, None] == key_image[None, :]) & key_valid[None, :]).astype(jnp.float32)
    scale = float(HD) ** (-0.5)

    states = []
    for section in range(phases):
        widened = carried.astype(jnp.float32)
        squares = jnp.sum(widened * widened, axis=-1, keepdims=True)
        squares_high = squares.astype(jnp.bfloat16)
        squares_low = (squares - squares_high.astype(jnp.float32)).astype(jnp.bfloat16)
        partial = jnp.dot(carried, wq[section], preferred_element_type=jnp.float32).astype(
            jnp.bfloat16
        )
        lane = jnp.arange(LANES)[None, :]
        extra = jnp.where(lane == 0, squares_high, jnp.where(lane == 1, squares_low, 0)).astype(
            jnp.bfloat16
        )
        packed = jnp.concatenate([partial, extra], axis=1)
        packed = packed.reshape(dps, phases, part_rows, head_width + LANES).transpose(1, 0, 2, 3)
        packed = packed.reshape(phases * dps, part_rows, head_width + LANES)
        packed = lax.all_to_all(packed, ("phase", "dp"), 0, 0, tiled=True)
        summed = jnp.sum(packed.astype(jnp.float32), axis=0)
        mean_square = (summed[:, head_width] + summed[:, head_width + 1]) / width
        inverse = lax.rsqrt(mean_square + epsilon) * scale
        queries = (summed[:, :head_width] * inverse[:, None]).astype(jnp.bfloat16)
        queries = queries.reshape(part_rows, HQ_DEV, HD)
        scores = jnp.einsum(
            "rhd,kd->hrk", queries, keyval[section, :, :HD], preferred_element_type=jnp.float32
        )
        weighted = jnp.exp(scores) * allowed[None]
        weights = (weighted / jnp.sum(weighted, axis=-1, keepdims=True)).astype(jnp.bfloat16)
        context = jnp.einsum(
            "hrk,kd->rhd", weights, keyval[section, :, HD:], preferred_element_type=jnp.float32
        )
        context = (context * live[:, None, None]).astype(jnp.bfloat16)
        context = context.reshape(part_rows, head_width)
        context = lax.all_gather(context, ("dp", "phase"), axis=0, tiled=True)
        context = lax.all_gather(context, "mp", axis=1, tiled=True)
        attended = jnp.dot(context, wo[section], preferred_element_type=jnp.float32)
        carried = (widened + attended).astype(jnp.bfloat16)
        states.append(carried.reshape(dps, own_rows, -1))
    return return_states(jnp.stack(states), phases, dps, mps)[None]


def solution(mesh):
    placed = (
        P("dp", "mp"),
        P("dp", ("phase", "mp"), None),
        P("dp"),
        P("dp"),
        P("dp"),
        P("phase", None),
        P("phase", "dp", "mp"),
        P("phase", None, "mp", None),
        P("phase", "dp", "mp"),
        P("phase"),
    )
    return jax.shard_map(
        on_device, mesh=mesh, in_specs=placed, out_specs=P("phase", "dp", "mp"), check_vma=False
    )
```

```python
import jax
import jax.numpy as jnp
from jax import lax
from jax.sharding import PartitionSpec as P

HD = 128
HQ_DEV = 4
TROWS = 32
SAMP = 2
TXT = 64
LANES = 128

epsilon = 1e-05


def over_phases(block):
    return lax.all_to_all(block, "phase", 0, 0, tiled=True)


def place_query_weight(query_weight, norm_gain, phases):
    depth, width = query_weight.shape[1:]
    gain = lax.dynamic_slice_in_dim(norm_gain[0], lax.axis_index("dp") * depth, depth, 0)
    scaled = (query_weight[0].astype(jnp.float32) * gain[:, None]).astype(jnp.bfloat16)
    return over_phases(scaled.reshape(phases, depth // phases, width))


def place_output_weight(output_weight, phases, slots, feats):
    rows = output_weight.shape[1]
    split = output_weight.reshape(rows, slots, phases, feats).transpose(2, 0, 1, 3)
    return over_phases(split.reshape(phases, rows, slots * feats))


def on_device(
    text_rows,
    image_rows,
    tile_counts,
    text_lengths,
    sample_image,
    norm_gain,
    query_weight,
    keyval_weight,
    output_weight,
    cross_gate,
):
    phases, dps, mps = (lax.axis_size(name) for name in ("phase", "dp", "mp"))
    phase_index = lax.axis_index("phase")
    width = norm_gain.shape[1]
    own_rows = text_rows.shape[0]
    part_rows = own_rows // phases
    head_width = query_weight.shape[2]
    feats = width // (phases * dps)
    slots = dps // mps

    wq = place_query_weight(query_weight, norm_gain, phases)
    wo = place_output_weight(output_weight, phases, slots, feats)

    def spread(own_part):
        return lax.all_gather(own_part, "mp", axis=1, tiled=True)

    own = text_rows.reshape(own_rows, slots, phases, feats)
    own = lax.dynamic_index_in_dim(own, phase_index, 2, keepdims=False)
    own = own.reshape(own_rows, slots * feats)
    carried = spread(own)

    images = lax.all_gather(image_rows, ("phase", "mp"), axis=1, tiled=True)
    key_count = images.shape[1]
    keyval = jnp.einsum(
        "srv,vc->src", images, keyval_weight[0, :, 0, :], preferred_element_type=jnp.float32
    )
    factor = jnp.concatenate(
        [jnp.ones((HD,), jnp.float32), jnp.broadcast_to(jnp.tanh(cross_gate), (HD,))]
    )
    keyval = (keyval * factor).astype(jnp.bfloat16)
    samples = [(phase * part_rows) // TXT for phase in range(phases)]
    picked = [lax.dynamic_index_in_dim(keyval, sample_image[b], 0, keepdims=False) for b in samples]
    keyval = over_phases(jnp.stack(picked))

    own_sample = (phase_index * part_rows) // TXT
    tiles = lax.dynamic_index_in_dim(
        tile_counts,
        lax.dynamic_index_in_dim(sample_image, own_sample, 0, keepdims=False),
        0,
        keepdims=False,
    )
    length = lax.dynamic_index_in_dim(text_lengths, own_sample, 0, keepdims=False)
    valid = (jnp.arange(key_count, dtype=jnp.int32) < tiles * TROWS).astype(jnp.float32)
    position = (phase_index * part_rows + jnp.arange(part_rows, dtype=jnp.int32)) % TXT
    live = (position < length).astype(jnp.float32)
    scale = float(HD) ** (-0.5)
    lane = jnp.arange(LANES)[None, :]

    states = []
    for section in range(phases):
        wq_full = lax.all_gather(wq[section], "dp", axis=0, tiled=True)
        wo_full = lax.all_gather(wo[section], "dp", axis=0, tiled=True)
        widened = carried.astype(jnp.float32)
        squares = jnp.sum(widened * widened, axis=-1, keepdims=True)
        squares_high = squares.astype(jnp.bfloat16)
        squares_low = (squares - squares_high.astype(jnp.float32)).astype(jnp.bfloat16)
        partial = jnp.dot(carried, wq_full, preferred_element_type=jnp.float32).astype(jnp.bfloat16)
        extra = jnp.where(lane == 0, squares_high, jnp.where(lane == 1, squares_low, 0)).astype(
            jnp.bfloat16
        )
        packed = jnp.concatenate([partial, extra], axis=1)
        packed = over_phases(packed.reshape(phases, part_rows, head_width + LANES))
        summed = jnp.sum(packed.astype(jnp.float32), axis=0)
        mean_square = (summed[:, head_width] + summed[:, head_width + 1]) / width
        inverse = lax.rsqrt(mean_square + epsilon) * scale
        queries = (summed[:, :head_width] * inverse[:, None]).astype(jnp.bfloat16)
        queries = queries.reshape(part_rows, HQ_DEV, HD)
        scores = jnp.einsum(
            "rhd,kd->hrk", queries, keyval[section, :, :HD], preferred_element_type=jnp.float32
        )
        weighted = jnp.exp(scores) * valid
        weights = (weighted / jnp.sum(weighted, axis=-1, keepdims=True)).astype(jnp.bfloat16)
        context = jnp.einsum(
            "hrk,kd->rhd", weights, keyval[section, :, HD:], preferred_element_type=jnp.float32
        )
        context = (context * live[:, None, None]).astype(jnp.bfloat16)
        context = context.reshape(1, part_rows, head_width)
        context = over_phases(jnp.broadcast_to(context, (phases, part_rows, head_width)))
        context = spread(context.reshape(own_rows, head_width))
        attended = jnp.dot(context, wo_full, preferred_element_type=jnp.float32)
        own = (own.astype(jnp.float32) + attended).astype(jnp.bfloat16)
        states.append(own)
        if section + 1 < phases:
            carried = spread(own)
    result = over_phases(jnp.stack(states)).reshape(phases, own_rows, slots, feats)
    return result.transpose(1, 2, 0, 3).reshape(1, own_rows, -1)


def solution(mesh):
    placed = (
        P("dp", "mp"),
        P("dp", ("phase", "mp"), None),
        P("dp"),
        P("dp"),
        P("dp"),
        P("phase", None),
        P("phase", "dp", "mp"),
        P("phase", None, "mp", None),
        P("phase", "dp", "mp"),
        P("phase"),
    )
    return jax.shard_map(
        on_device, mesh=mesh, in_specs=placed, out_specs=P("phase", "dp", "mp"), check_vma=False
    )
```

```python
import functools

import jax
import jax.numpy as jnp
import numpy as np
from jax import lax
from jax.experimental import pallas as pl
from jax.experimental.pallas import tpu as pltpu
from jax.sharding import Mesh
from jax.sharding import PartitionSpec as P

HD = 128
HQ_DEV = 4
TROWS = 32
SAMP = 2
TXT = 64
LANES = 128
PAIR = 2

PHASE = ("far", "near")
GROUP = ("far", "near", "side")

epsilon = 1e-05
VMEM = pl.BlockSpec(memory_space=pltpu.VMEM)


def cost(flops, bytes_accessed, transcendentals=0):
    return pl.CostEstimate(
        flops=flops, bytes_accessed=bytes_accessed, transcendentals=transcendentals
    )


def query_kernel(x_ref, weight_ref, packed_ref):
    halves, depth = weight_ref.shape[0], weight_ref.shape[2]
    total = jnp.zeros((x_ref.shape[0], weight_ref.shape[3]), jnp.float32)
    squares = jnp.zeros((x_ref.shape[0], 1), jnp.float32)
    for half in range(halves):
        part = x_ref[:, half * depth : (half + 1) * depth]
        total += jnp.dot(part, weight_ref[half, 0], preferred_element_type=jnp.float32)
        wide = part.astype(jnp.float32)
        squares += jnp.sum(wide * wide, axis=-1, keepdims=True)
    high = squares.astype(jnp.bfloat16).astype(jnp.float32)
    lane = lax.broadcasted_iota(jnp.int32, (x_ref.shape[0], LANES), 1)
    extra = jnp.where(lane == 0, high, jnp.where(lane == 1, squares - high, 0.0))
    packed_ref[:, : total.shape[1]] = total.astype(jnp.bfloat16)
    packed_ref[:, total.shape[1] :] = extra.astype(jnp.bfloat16)


def project_queries(x, weights, slot):
    rows = x.shape[0]
    halves, _, depth, width = weights.shape
    return pl.pallas_call(
        query_kernel,
        grid=(1,),
        out_shape=jax.ShapeDtypeStruct((rows, width + LANES), jnp.bfloat16),
        in_specs=[
            pl.BlockSpec(x.shape, lambda i: (0, 0)),
            pl.BlockSpec((halves, 1, depth, width), lambda i: (0, slot, 0, 0)),
        ],
        out_specs=pl.BlockSpec((rows, width + LANES), lambda i: (0, 0)),
        cost_estimate=cost(2 * rows * halves * depth * width, 2 * halves * depth * width),
    )(x, weights)


def attend_kernel(width, packed_ref, keyval_ref, valid_ref, live_ref, context_ref):
    sources, rows, columns = packed_ref.shape
    heads = (columns - LANES) // HD
    summed = packed_ref[0].astype(jnp.float32)
    for source in range(1, sources):
        summed += packed_ref[source].astype(jnp.float32)
    squares = summed[:, heads * HD : heads * HD + 1] + summed[:, heads * HD + 1 : heads * HD + 2]
    inverse = lax.rsqrt(squares / width + epsilon) * (float(HD) ** (-0.5))
    queries = jnp.concatenate(
        [summed[:, head * HD : (head + 1) * HD] * inverse for head in range(heads)], axis=0
    ).astype(jnp.bfloat16)
    keys = keyval_ref[0, :, :HD]
    values = keyval_ref[0, :, HD:]
    scores = lax.dot_general(
        queries, keys, (((1,), (1,)), ((), ())), preferred_element_type=jnp.float32
    )
    weighted = jnp.exp(scores) * valid_ref[...]
    weights = (weighted / jnp.sum(weighted, axis=-1, keepdims=True)).astype(jnp.bfloat16)
    context = jnp.dot(weights, values, preferred_element_type=jnp.float32)
    for head in range(heads):
        part = context[head * rows : (head + 1) * rows] * live_ref[...]
        context_ref[:, head * HD : (head + 1) * HD] = part.astype(jnp.bfloat16)


def attend(packed, keyval, valid, live, section, width):
    sources, rows, columns = packed.shape
    keys = keyval.shape[1]
    heads = (columns - LANES) // HD
    return pl.pallas_call(
        functools.partial(attend_kernel, width),
        grid=(1,),
        out_shape=jax.ShapeDtypeStruct((rows, heads * HD), jnp.bfloat16),
        in_specs=[
            pl.BlockSpec(packed.shape, lambda i: (0, 0, 0)),
            pl.BlockSpec((1, keys, 2 * HD), lambda i: (section, 0, 0)),
            pl.BlockSpec(valid.shape, lambda i: (0, 0)),
            pl.BlockSpec(live.shape, lambda i: (0, 0)),
        ],
        out_specs=pl.BlockSpec((rows, heads * HD), lambda i: (0, 0)),
        cost_estimate=cost(4 * heads * rows * keys * HD, packed.size * 2, heads * rows * keys),
    )(packed, keyval, valid, live)


def output_kernel(context_ref, weight_ref, own_ref, result_ref):
    halves, width = weight_ref.shape[0], weight_ref.shape[3]
    total = own_ref[...].astype(jnp.float32)
    for half in range(halves):
        total += lax.dot_general(
            context_ref[:, half * width : (half + 1) * width],
            weight_ref[half, 0],
            (((1,), (1,)), ((), ())),
            preferred_element_type=jnp.float32,
        )
    result_ref[...] = total.astype(jnp.bfloat16)


def project_output(context, weights, slot, own):
    halves, _, columns, width = weights.shape
    return pl.pallas_call(
        output_kernel,
        grid=(1,),
        out_shape=jax.ShapeDtypeStruct(own.shape, jnp.bfloat16),
        in_specs=[
            pl.BlockSpec(context.shape, lambda i: (0, 0)),
            pl.BlockSpec((halves, 1, columns, width), lambda i: (0, slot, 0, 0)),
            pl.BlockSpec(own.shape, lambda i: (0, 0)),
        ],
        out_specs=pl.BlockSpec(own.shape, lambda i: (0, 0)),
        cost_estimate=cost(2 * context.size * columns, 2 * halves * columns * width),
    )(context, weights, own)


def exchange(block, axes):
    return lax.all_to_all(block, axes, 0, 0, tiled=True)


def on_device(
    text_rows,
    image_rows,
    tile_counts,
    text_lengths,
    sample_image,
    norm_gain,
    query_weight,
    keyval_weight,
    output_weight,
    cross_gate,
):
    halves, mps = lax.axis_size("half"), lax.axis_size("mp")
    phases = lax.axis_size("far") * lax.axis_size("near")
    dps = halves * PAIR
    phase_index = lax.axis_index(PHASE)
    dp_index = lax.axis_index(("half", "side"))
    width = norm_gain.shape[1]
    own_rows = text_rows.shape[0]
    part_rows = own_rows // phases
    depth, head_width = query_weight.shape[1:]
    feats = depth // phases
    slots = dps // mps // PAIR
    core_feats = slots * feats

    gain = lax.dynamic_slice_in_dim(norm_gain[0], dp_index * depth, depth, 0)
    wq = (query_weight[0].astype(jnp.float32) * gain[:, None]).astype(jnp.bfloat16)
    wq = exchange(wq.reshape(phases, feats, head_width), PHASE)
    context_part = output_weight.shape[1]
    wo = output_weight.reshape(context_part, slots, PAIR, phases, feats)
    wo = wo.transpose(3, 2, 1, 4, 0).reshape(phases * PAIR, core_feats, context_part)
    wo = exchange(wo, GROUP).reshape(phases, PAIR, core_feats, context_part)
    wo = wo.transpose(0, 2, 1, 3).reshape(phases, core_feats, PAIR * context_part)

    def gather_weights(*parts):
        return lax.all_gather(jnp.stack(parts), "half", axis=0, tiled=False)

    def spread(own_part):
        return lax.all_gather(own_part, "mp", axis=1, tiled=True)

    own = text_rows.reshape(own_rows, slots, PAIR, phases, feats)
    own = lax.dynamic_index_in_dim(own, phase_index, 3, keepdims=False)
    own = own.transpose(2, 0, 1, 3).reshape(PAIR, own_rows, core_feats)
    own = exchange(own, "side").reshape(PAIR, phases, part_rows, core_feats)
    own = own.transpose(1, 0, 2, 3).reshape(PAIR * own_rows, core_feats)
    carried = spread(own)

    images = lax.all_gather(image_rows, PHASE + ("mp",), axis=1, tiled=True)
    key_count = images.shape[1]
    keyval = jnp.einsum(
        "srv,vc->src", images, keyval_weight[0, :, 0, :], preferred_element_type=jnp.float32
    )
    factor = jnp.concatenate(
        [jnp.ones((HD,), jnp.float32), jnp.broadcast_to(jnp.tanh(cross_gate), (HD,))]
    )
    keyval = (keyval * factor).astype(jnp.bfloat16)
    samples = [(phase * part_rows) // TXT for phase in range(phases)]
    picked = [lax.dynamic_index_in_dim(keyval, sample_image[b], 0, keepdims=False) for b in samples]
    keyval = exchange(jnp.stack(picked), PHASE)

    own_sample = (phase_index * part_rows) // TXT
    image = lax.dynamic_index_in_dim(sample_image, own_sample, 0, keepdims=False)
    tiles = lax.dynamic_index_in_dim(tile_counts, image, 0, keepdims=False)
    length = lax.dynamic_index_in_dim(text_lengths, own_sample, 0, keepdims=False)
    valid = (jnp.arange(key_count, dtype=jnp.int32) < tiles * TROWS).astype(jnp.float32)[None, :]
    position = (phase_index * part_rows + jnp.arange(part_rows, dtype=jnp.int32)) % TXT
    live = (position < length).astype(jnp.float32)[:, None]

    weights = [gather_weights(wq[0])]
    for section in range(phases - 2):
        weights.append(gather_weights(wo[section], wq[section + 1]))
    weights.append(gather_weights(wo[phases - 2], wq[phases - 1], wo[phases - 1]))

    states = []
    for section in range(phases):
        packed = project_queries(carried, weights[section], 0 if section == 0 else 1)
        packed = exchange(packed.reshape(phases * PAIR, part_rows, head_width + LANES), GROUP)
        context = attend(packed, keyval, valid, live, section, width)
        for axis in ("side", "near", "far"):
            context = lax.all_gather(context, axis, axis=0, tiled=True)
        context = spread(context)
        last = section + 1 == phases
        own = project_output(context, weights[section if last else section + 1], 2 if last else 0, own)
        states.append(own)
        if not last:
            carried = spread(own)
    result = jnp.stack(states).reshape(phases, phases, PAIR, part_rows, core_feats)
    result = result.transpose(0, 2, 1, 3, 4).reshape(phases * PAIR, own_rows, core_feats)
    result = exchange(result, GROUP).reshape(phases, PAIR, own_rows, slots, feats)
    return result.transpose(2, 3, 1, 0, 4).reshape(1, own_rows, -1)


def solution(mesh):
    phases, dps, mps = (mesh.shape[name] for name in ("phase", "dp", "mp"))
    sizes = (phases // PAIR, PAIR, dps // PAIR, PAIR, mps)
    parts = Mesh(np.reshape(mesh.devices, sizes), ("far", "near", "half", "side", "mp"))
    dp = ("half", "side")
    placed = (
        P(dp, "mp"),
        P(dp, PHASE + ("mp",), None),
        P(dp),
        P(dp),
        P(dp),
        P(PHASE, None),
        P(PHASE, dp, "mp"),
        P(PHASE, None, "mp", None),
        P(PHASE, dp, "mp"),
        P(PHASE),
    )
    return jax.shard_map(
        on_device, mesh=parts, in_specs=placed, out_specs=P(PHASE, dp, "mp"), check_vma=False
    )
```

```python
import functools

import jax
import jax.numpy as jnp
from jax import lax
from jax.experimental import pallas as pl
from jax.experimental.pallas import tpu as pltpu
from jax.sharding import PartitionSpec as P

HD = 128
HQ_DEV = 4
TROWS = 32
SAMP = 2
TXT = 64
LANES = 128

epsilon = 1e-05
IN_VMEM = pl.BlockSpec(memory_space=pltpu.VMEM)
IN_SMEM = pl.BlockSpec(memory_space=pltpu.SMEM)
LIMIT = pltpu.CompilerParams(vmem_limit_bytes=24 * 2**20)


def cost(flops, bytes_accessed, transcendentals=0):
    return pl.CostEstimate(
        flops=flops, bytes_accessed=bytes_accessed, transcendentals=transcendentals
    )


def keyval_kernel(samples, choice_ref, gate_ref, images_ref, weight_ref, result_ref, held):
    count, keys, depth = images_ref.shape
    factor = jnp.tanh(jnp.full((1, HD), gate_ref[0], jnp.float32))
    for image in range(count):
        both = jnp.dot(images_ref[image], weight_ref[...], preferred_element_type=jnp.float32)
        held[image, :, :HD] = both[:, :HD].astype(jnp.bfloat16)
        held[image, :, HD:] = (both[:, HD:] * factor).astype(jnp.bfloat16)
    for slot, sample in enumerate(samples):
        result_ref[slot] = held[choice_ref[sample]]


def project_keyval(samples, choice, gate, images, weight):
    count, keys, depth = images.shape
    return pl.pallas_call(
        functools.partial(keyval_kernel, samples),
        out_shape=jax.ShapeDtypeStruct((len(samples), keys, 2 * HD), jnp.bfloat16),
        in_specs=[IN_SMEM, IN_SMEM, IN_VMEM, IN_VMEM],
        out_specs=IN_VMEM,
        scratch_shapes=[pltpu.VMEM((count, keys, 2 * HD), jnp.bfloat16)],
        compiler_params=LIMIT,
        cost_estimate=cost(4 * count * keys * depth * HD, 2 * images.size + 2 * weight.size),
    )(choice, gate, images, weight)


def query_kernel(slot, x_ref, weight_ref, packed_ref):
    parts, _, depth, width = weight_ref.shape
    total = jnp.zeros((x_ref.shape[0], width), jnp.float32)
    squares = jnp.zeros((x_ref.shape[0], 1), jnp.float32)
    for part in range(parts):
        block = x_ref[:, part * depth : (part + 1) * depth]
        total += jnp.dot(block, weight_ref[part, slot], preferred_element_type=jnp.float32)
        wide = block.astype(jnp.float32)
        squares += jnp.sum(wide * wide, axis=-1, keepdims=True)
    high = squares.astype(jnp.bfloat16).astype(jnp.float32)
    lane = lax.broadcasted_iota(jnp.int32, (x_ref.shape[0], LANES), 1)
    extra = jnp.where(lane == 0, high, jnp.where(lane == 1, squares - high, 0.0))
    packed_ref[:, :width] = total.astype(jnp.bfloat16)
    packed_ref[:, width:] = extra.astype(jnp.bfloat16)


def project_queries(x, weights, slot):
    rows = x.shape[0]
    parts, _, depth, width = weights.shape
    return pl.pallas_call(
        functools.partial(query_kernel, slot),
        out_shape=jax.ShapeDtypeStruct((rows, width + LANES), jnp.bfloat16),
        in_specs=[IN_VMEM, IN_VMEM],
        out_specs=IN_VMEM,
        compiler_params=LIMIT,
        cost_estimate=cost(2 * rows * parts * depth * width, 2 * parts * depth * width),
    )(x, weights)


def attend_kernel(
    width, section, place_ref, choice_ref, tiles_ref, length_ref, packed_ref, keyval_ref, result_ref
):
    sources, rows, columns = packed_ref.shape
    heads = (columns - LANES) // HD
    keys = keyval_ref.shape[1]
    first = place_ref[0] * rows
    sample = first // TXT
    key = lax.broadcasted_iota(jnp.int32, (1, keys), 1)
    valid = jnp.where(key < tiles_ref[choice_ref[sample]] * TROWS, 1.0, 0.0)
    position = first - sample * TXT + lax.broadcasted_iota(jnp.int32, (rows, 1), 0)
    live = jnp.where(position < length_ref[sample], 1.0, 0.0)
    summed = packed_ref[0].astype(jnp.float32)
    for source in range(1, sources):
        summed += packed_ref[source].astype(jnp.float32)
    squares = summed[:, heads * HD : heads * HD + 1] + summed[:, heads * HD + 1 : heads * HD + 2]
    inverse = lax.rsqrt(squares / width + epsilon) * (float(HD) ** (-0.5))
    queries = jnp.concatenate(
        [summed[:, head * HD : (head + 1) * HD] * inverse for head in range(heads)], axis=0
    ).astype(jnp.bfloat16)
    scores = lax.dot_general(
        queries,
        keyval_ref[section, :, :HD],
        (((1,), (1,)), ((), ())),
        preferred_element_type=jnp.float32,
    )
    weighted = jnp.exp(scores) * valid
    weights = (weighted / jnp.sum(weighted, axis=-1, keepdims=True)).astype(jnp.bfloat16)
    context = jnp.dot(weights, keyval_ref[section, :, HD:], preferred_element_type=jnp.float32)
    for head in range(heads):
        part = (context[head * rows : (head + 1) * rows] * live).astype(jnp.bfloat16)
        for target in range(sources):
            result_ref[target, :, head * HD : (head + 1) * HD] = part


def attend(place, choice, tiles, lengths, packed, keyval, section, width):
    sources, rows, columns = packed.shape
    keys = keyval.shape[1]
    heads = (columns - LANES) // HD
    return pl.pallas_call(
        functools.partial(attend_kernel, width, section),
        out_shape=jax.ShapeDtypeStruct((sources, rows, heads * HD), jnp.bfloat16),
        in_specs=[IN_SMEM, IN_SMEM, IN_SMEM, IN_SMEM, IN_VMEM, IN_VMEM],
        out_specs=IN_VMEM,
        compiler_params=LIMIT,
        cost_estimate=cost(4 * heads * rows * keys * HD, packed.size * 2, heads * rows * keys),
    )(place, choice, tiles, lengths, packed, keyval)


def output_kernel(slot, context_ref, weight_ref, own_ref, result_ref):
    parts, _, depth, _ = weight_ref.shape
    total = own_ref[...].astype(jnp.float32)
    for part in range(parts):
        total += jnp.dot(
            context_ref[:, part * depth : (part + 1) * depth],
            weight_ref[part, slot],
            preferred_element_type=jnp.float32,
        )
    result_ref[...] = total.astype(jnp.bfloat16)


def project_output(context, weights, slot, own):
    rows, depth = context.shape
    columns = own.shape[1]
    if weights.shape[2:] != (depth // weights.shape[0], columns):
        weights = weights[:, slot].reshape(weights.shape[0], 1, -1, columns)
        slot = 0
    return pl.pallas_call(
        functools.partial(output_kernel, slot),
        out_shape=jax.ShapeDtypeStruct(own.shape, jnp.bfloat16),
        in_specs=[IN_VMEM, IN_VMEM, IN_VMEM],
        out_specs=IN_VMEM,
        compiler_params=LIMIT,
        cost_estimate=cost(2 * rows * depth * columns, 2 * depth * columns),
    )(context, weights, own)


def over_phases(block):
    return lax.all_to_all(block, "phase", 0, 0, tiled=True)


def on_device(
    text_rows,
    image_rows,
    tile_counts,
    text_lengths,
    sample_image,
    norm_gain,
    query_weight,
    keyval_weight,
    output_weight,
    cross_gate,
):
    phases, dps, mps = (lax.axis_size(name) for name in ("phase", "dp", "mp"))
    phase_index = lax.axis_index("phase")
    width = norm_gain.shape[1]
    own_rows = text_rows.shape[0]
    part_rows = own_rows // phases
    depth, head_width = query_weight.shape[1:]
    feats = depth // phases
    slots = dps // mps
    core_feats = slots * feats

    gain = lax.dynamic_slice_in_dim(norm_gain[0], lax.axis_index("dp") * depth, depth, 0)
    wq = (query_weight[0].astype(jnp.float32) * gain[:, None]).astype(jnp.bfloat16)
    wq = over_phases(wq.reshape(phases, feats, head_width))
    context_part = output_weight.shape[1]
    wo = output_weight.reshape(context_part, slots, phases, feats).transpose(2, 0, 1, 3)
    wo = over_phases(wo.reshape(phases, context_part, core_feats))
    wo = wo.reshape(phases, feats, head_width)

    def gather_weights(*parts):
        return lax.all_gather(jnp.stack(parts), "dp", axis=0, tiled=False)

    def spread(own_part):
        return lax.all_gather(own_part, "mp", axis=1, tiled=True)

    own = text_rows.reshape(own_rows, slots, phases, feats)
    own = lax.dynamic_index_in_dim(own, phase_index, 2, keepdims=False)
    own = own.reshape(own_rows, core_feats)
    carried = spread(own)

    samples = [(phase * part_rows) // TXT for phase in range(phases)]
    images = lax.all_gather(image_rows, ("phase", "mp"), axis=1, tiled=True)
    keyval = project_keyval(samples, sample_image, cross_gate, images, keyval_weight[0, :, 0, :])
    keyval = over_phases(keyval)
    place = jnp.full((1,), phase_index, jnp.int32)

    weights = [gather_weights(wq[0])]
    for section in range(phases - 1):
        weights.append(gather_weights(wo[section], wq[section + 1]))
    weights.append(gather_weights(wo[phases - 1]))

    states = []
    for section in range(phases):
        packed = project_queries(carried, weights[section], 0 if section == 0 else 1)
        packed = over_phases(packed.reshape(phases, part_rows, head_width + LANES))
        context = attend(
            place, sample_image, tile_counts, text_lengths, packed, keyval, section, width
        )
        context = spread(over_phases(context).reshape(own_rows, head_width))
        own = project_output(context, weights[section + 1], 0, own)
        states.append(own)
        if section + 1 < phases:
            carried = spread(own)
    result = over_phases(jnp.stack(states)).reshape(phases, own_rows, slots, feats)
    return result.transpose(1, 2, 0, 3).reshape(1, own_rows, -1)


def solution(mesh):
    placed = (
        P("dp", "mp"),
        P("dp", ("phase", "mp"), None),
        P("dp"),
        P("dp"),
        P("dp"),
        P("phase", None),
        P("phase", "dp", "mp"),
        P("phase", None, "mp", None),
        P("phase", "dp", "mp"),
        P("phase"),
    )
    return jax.shard_map(
        on_device, mesh=mesh, in_specs=placed, out_specs=P("phase", "dp", "mp"), check_vma=False
    )
```

```python
import functools

import jax
import jax.numpy as jnp
from jax import lax
from jax.experimental import pallas as pl
from jax.experimental.pallas import tpu as pltpu
from jax.sharding import PartitionSpec as P

HD = 128
HQ_DEV = 4
TROWS = 32
SAMP = 2
TXT = 64
LANES = 128

epsilon = 1e-05
IN_VMEM = pl.BlockSpec(memory_space=pltpu.VMEM)
IN_SMEM = pl.BlockSpec(memory_space=pltpu.SMEM)
LIMIT = pltpu.CompilerParams(vmem_limit_bytes=24 * 2**20)


def cost(flops, bytes_accessed, transcendentals=0):
    return pl.CostEstimate(
        flops=flops, bytes_accessed=bytes_accessed, transcendentals=transcendentals
    )


def keyval_kernel(samples, choice_ref, gate_ref, images_ref, weight_ref, result_ref, held):
    count, keys, depth = images_ref.shape
    factor = jnp.tanh(jnp.full((1, HD), gate_ref[0], jnp.float32))
    for image in range(count):
        both = jnp.dot(images_ref[image], weight_ref[...], preferred_element_type=jnp.float32)
        held[image, :, :HD] = both[:, :HD].astype(jnp.bfloat16)
        held[image, :, HD:] = (both[:, HD:] * factor).astype(jnp.bfloat16)
    for slot, sample in enumerate(samples):
        result_ref[slot] = held[choice_ref[sample]]


def project_keyval(samples, choice, gate, images, weight):
    count, keys, depth = images.shape
    return pl.pallas_call(
        functools.partial(keyval_kernel, samples),
        out_shape=jax.ShapeDtypeStruct((len(samples), keys, 2 * HD), jnp.bfloat16),
        in_specs=[IN_SMEM, IN_SMEM, IN_VMEM, IN_VMEM],
        out_specs=IN_VMEM,
        scratch_shapes=[pltpu.VMEM((count, keys, 2 * HD), jnp.bfloat16)],
        compiler_params=LIMIT,
        cost_estimate=cost(4 * count * keys * depth * HD, 2 * images.size + 2 * weight.size),
    )(choice, gate, images, weight)


def query_kernel(slot, x_ref, weight_ref, packed_ref):
    parts, _, depth, width = weight_ref.shape
    total = jnp.zeros((x_ref.shape[0], width), jnp.float32)
    squares = jnp.zeros((x_ref.shape[0], 1), jnp.float32)
    for part in range(parts):
        block = x_ref[:, part * depth : (part + 1) * depth]
        total += jnp.dot(block, weight_ref[part, slot], preferred_element_type=jnp.float32)
        wide = block.astype(jnp.float32)
        squares += jnp.sum(wide * wide, axis=-1, keepdims=True)
    high = squares.astype(jnp.bfloat16).astype(jnp.float32)
    lane = lax.broadcasted_iota(jnp.int32, (x_ref.shape[0], LANES), 1)
    extra = jnp.where(lane == 0, high, jnp.where(lane == 1, squares - high, 0.0))
    packed_ref[:, :width] = total.astype(jnp.bfloat16)
    packed_ref[:, width:] = extra.astype(jnp.bfloat16)


def project_queries(x, weights, slot):
    rows = x.shape[0]
    parts, _, depth, width = weights.shape
    return pl.pallas_call(
        functools.partial(query_kernel, slot),
        out_shape=jax.ShapeDtypeStruct((rows, width + LANES), jnp.bfloat16),
        in_specs=[IN_VMEM, IN_VMEM],
        out_specs=IN_VMEM,
        compiler_params=LIMIT,
        cost_estimate=cost(2 * rows * parts * depth * width, 2 * parts * depth * width),
    )(x, weights)


def sum_kernel(partial_ref, result_ref):
    sources, _, columns = partial_ref.shape
    edge = columns - LANES
    total = partial_ref[0].astype(jnp.float32)
    for source in range(1, sources):
        total += partial_ref[source].astype(jnp.float32)
    squares = total[:, edge : edge + 1] + total[:, edge + 1 : edge + 2]
    high = squares.astype(jnp.bfloat16).astype(jnp.float32)
    lane = lax.broadcasted_iota(jnp.int32, (total.shape[0], LANES), 1)
    extra = jnp.where(lane == 0, high, jnp.where(lane == 1, squares - high, 0.0))
    result_ref[:, :edge] = total[:, :edge].astype(jnp.bfloat16)
    result_ref[:, edge:] = extra.astype(jnp.bfloat16)


def sum_partials(partial):
    return pl.pallas_call(
        sum_kernel,
        out_shape=jax.ShapeDtypeStruct(partial.shape[1:], jnp.bfloat16),
        in_specs=[IN_VMEM],
        out_specs=IN_VMEM,
        compiler_params=LIMIT,
        cost_estimate=cost(partial.size, 2 * partial.size),
    )(partial)


def attend_kernel(
    width, section, place_ref, choice_ref, tiles_ref, length_ref, packed_ref, keyval_ref, result_ref
):
    sources, rows, columns = packed_ref.shape
    heads = (columns - LANES) // HD
    keys = keyval_ref.shape[1]
    first = place_ref[0] * rows
    sample = first // TXT
    key = lax.broadcasted_iota(jnp.int32, (1, keys), 1)
    valid = jnp.where(key < tiles_ref[choice_ref[sample]] * TROWS, 1.0, 0.0)
    position = first - sample * TXT + lax.broadcasted_iota(jnp.int32, (rows, 1), 0)
    live = jnp.where(position < length_ref[sample], 1.0, 0.0)
    summed = packed_ref[0].astype(jnp.float32)
    for source in range(1, sources):
        summed += packed_ref[source].astype(jnp.float32)
    squares = summed[:, heads * HD : heads * HD + 1] + summed[:, heads * HD + 1 : heads * HD + 2]
    inverse = lax.rsqrt(squares / width + epsilon) * (float(HD) ** (-0.5))
    queries = jnp.concatenate(
        [summed[:, head * HD : (head + 1) * HD] * inverse for head in range(heads)], axis=0
    ).astype(jnp.bfloat16)
    scores = lax.dot_general(
        queries,
        keyval_ref[section, :, :HD],
        (((1,), (1,)), ((), ())),
        preferred_element_type=jnp.float32,
    )
    weighted = jnp.exp(scores) * valid
    weights = (weighted / jnp.sum(weighted, axis=-1, keepdims=True)).astype(jnp.bfloat16)
    context = jnp.dot(weights, keyval_ref[section, :, HD:], preferred_element_type=jnp.float32)
    for head in range(heads):
        part = (context[head * rows : (head + 1) * rows] * live).astype(jnp.bfloat16)
        for target in range(result_ref.shape[0]):
            result_ref[target, :, head * HD : (head + 1) * HD] = part


def attend(place, choice, tiles, lengths, packed, keyval, section, width):
    sources, rows, columns = packed.shape
    sections, keys, _ = keyval.shape
    heads = (columns - LANES) // HD
    return pl.pallas_call(
        functools.partial(attend_kernel, width, section),
        out_shape=jax.ShapeDtypeStruct((sections, rows, heads * HD), jnp.bfloat16),
        in_specs=[IN_SMEM, IN_SMEM, IN_SMEM, IN_SMEM, IN_VMEM, IN_VMEM],
        out_specs=IN_VMEM,
        compiler_params=LIMIT,
        cost_estimate=cost(4 * heads * rows * keys * HD, packed.size * 2, heads * rows * keys),
    )(place, choice, tiles, lengths, packed, keyval)


def output_kernel(slot, context_ref, weight_ref, own_ref, result_ref):
    parts, _, depth, _ = weight_ref.shape
    total = own_ref[...].astype(jnp.float32)
    for part in range(parts):
        total += jnp.dot(
            context_ref[:, part * depth : (part + 1) * depth],
            weight_ref[part, slot],
            preferred_element_type=jnp.float32,
        )
    result_ref[...] = total.astype(jnp.bfloat16)


def project_output(context, weights, slot, own):
    rows, depth = context.shape
    columns = own.shape[1]
    if weights.shape[2:] != (depth // weights.shape[0], columns):
        weights = weights[:, slot].reshape(weights.shape[0], 1, -1, columns)
        slot = 0
    return pl.pallas_call(
        functools.partial(output_kernel, slot),
        out_shape=jax.ShapeDtypeStruct(own.shape, jnp.bfloat16),
        in_specs=[IN_VMEM, IN_VMEM, IN_VMEM],
        out_specs=IN_VMEM,
        compiler_params=LIMIT,
        cost_estimate=cost(2 * rows * depth * columns, 2 * depth * columns),
    )(context, weights, own)


def over_phases(block):
    return lax.all_to_all(block, "phase", 0, 0, tiled=True)


def on_device(
    text_rows,
    image_rows,
    tile_counts,
    text_lengths,
    sample_image,
    norm_gain,
    query_weight,
    keyval_weight,
    output_weight,
    cross_gate,
):
    phases, dps, mps = (lax.axis_size(name) for name in ("phase", "dp", "mp"))
    phase_index = lax.axis_index("phase")
    width = norm_gain.shape[1]
    own_rows = text_rows.shape[0]
    part_rows = own_rows // phases
    depth, head_width = query_weight.shape[1:]
    feats = depth // phases
    slots = dps // mps
    core_feats = slots * feats

    context_part = output_weight.shape[1]
    wo = output_weight.reshape(context_part, slots, phases, feats).transpose(2, 0, 1, 3)
    wo = over_phases(wo.reshape(phases, context_part, core_feats))
    gain = lax.dynamic_slice_in_dim(norm_gain[0], lax.axis_index("dp") * depth, depth, 0)
    wq = (query_weight[0].astype(jnp.float32) * gain[:, None]).astype(jnp.bfloat16)
    wo, wq = lax.optimization_barrier((wo, wq))
    wq = over_phases(wq.reshape(phases, feats, head_width))
    wo = wo.reshape(phases, feats, head_width)

    def gather_weights(*parts):
        return lax.all_gather(jnp.stack(parts), "dp", axis=0, tiled=False)

    def spread(own_part):
        return lax.all_gather(own_part, "mp", axis=1, tiled=True)

    own = text_rows.reshape(own_rows, slots, phases, feats)
    own = lax.dynamic_index_in_dim(own, phase_index, 2, keepdims=False)
    own = own.reshape(own_rows, core_feats)
    carried = spread(own)

    samples = [(phase * part_rows) // TXT for phase in range(phases)]
    images = lax.all_gather(image_rows, ("phase", "mp"), axis=1, tiled=True)
    keyval = project_keyval(samples, sample_image, cross_gate, images, keyval_weight[0, :, 0, :])
    keyval = over_phases(keyval)
    place = jnp.full((1,), phase_index, jnp.int32)

    items = [(kind, section) for section in range(1, phases) for kind in ("query", "out")]
    groups = [[("out", 0)], items[:3]] + [items[i : i + 2] for i in range(3, len(items), 2)]
    gathered = {}
    for group in groups:
        parts = [(wo if kind == "out" else wq)[section] for kind, section in group]
        block = gather_weights(*parts)
        gathered.update({item: (block, slot) for slot, item in enumerate(group)})

    rows = carried.reshape(own_rows, dps, feats).transpose(1, 0, 2)
    rows = lax.all_to_all(rows, "dp", 0, 0, tiled=True)
    rows = rows.reshape(dps, phases, part_rows, feats).transpose(1, 0, 2, 3)
    packed = project_queries(rows.reshape(dps * own_rows, feats), wq[None], 0)
    packed = over_phases(packed.reshape(phases, dps * part_rows, head_width + LANES))
    packed = sum_partials(packed).reshape(dps, part_rows, head_width + LANES)
    packed = lax.all_to_all(packed, "dp", 0, 0, tiled=True)

    states = []
    for section in range(phases):
        if section:
            carried = spread(own)
            packed = project_queries(carried, *gathered["query", section])
            packed = over_phases(packed.reshape(phases, part_rows, head_width + LANES))
        context = attend(
            place, sample_image, tile_counts, text_lengths, packed, keyval, section, width
        )
        context = spread(over_phases(context).reshape(own_rows, head_width))
        own = project_output(context, *gathered["out", section], own)
        states.append(own)
    result = over_phases(jnp.stack(states)).reshape(phases, own_rows, slots, feats)
    return result.transpose(1, 2, 0, 3).reshape(1, own_rows, -1)


def solution(mesh):
    placed = (
        P("dp", "mp"),
        P("dp", ("phase", "mp"), None),
        P("dp"),
        P("dp"),
        P("dp"),
        P("phase", None),
        P("phase", "dp", "mp"),
        P("phase", None, "mp", None),
        P("phase", "dp", "mp"),
        P("phase"),
    )
    return jax.shard_map(
        on_device, mesh=mesh, in_specs=placed, out_specs=P("phase", "dp", "mp"), check_vma=False
    )
```

```python
import functools

import jax
import jax.numpy as jnp
from jax import lax
from jax.experimental import pallas as pl
from jax.experimental.pallas import tpu as pltpu
from jax.sharding import PartitionSpec as P

HD = 128
HQ_DEV = 4
TROWS = 32
SAMP = 2
TXT = 64
LANES = 128

epsilon = 1e-05
IN_VMEM = pl.BlockSpec(memory_space=pltpu.VMEM)
IN_SMEM = pl.BlockSpec(memory_space=pltpu.SMEM)
LIMIT = pltpu.CompilerParams(vmem_limit_bytes=24 * 2**20)


def cost(flops, bytes_accessed, transcendentals=0):
    return pl.CostEstimate(
        flops=flops, bytes_accessed=bytes_accessed, transcendentals=transcendentals
    )


def keyval_kernel(samples, choice_ref, gate_ref, images_ref, weight_ref, result_ref, held):
    count, keys, depth = images_ref.shape
    factor = jnp.tanh(jnp.full((1, HD), gate_ref[0], jnp.float32))
    for image in range(count):
        both = jnp.dot(images_ref[image], weight_ref[...], preferred_element_type=jnp.float32)
        held[image, :, :HD] = both[:, :HD].astype(jnp.bfloat16)
        held[image, :, HD:] = (both[:, HD:] * factor).astype(jnp.bfloat16)
    for slot, sample in enumerate(samples):
        result_ref[slot] = held[choice_ref[sample]]


def project_keyval(samples, choice, gate, images, weight):
    count, keys, depth = images.shape
    return pl.pallas_call(
        functools.partial(keyval_kernel, samples),
        out_shape=jax.ShapeDtypeStruct((len(samples), keys, 2 * HD), jnp.bfloat16),
        in_specs=[IN_SMEM, IN_SMEM, IN_VMEM, IN_VMEM],
        out_specs=IN_VMEM,
        scratch_shapes=[pltpu.VMEM((count, keys, 2 * HD), jnp.bfloat16)],
        compiler_params=LIMIT,
        cost_estimate=cost(4 * count * keys * depth * HD, 2 * images.size + 2 * weight.size),
    )(choice, gate, images, weight)


def query_kernel(slot, x_ref, weight_ref, packed_ref):
    parts, _, depth, width = weight_ref.shape
    total = jnp.zeros((x_ref.shape[0], width), jnp.float32)
    squares = jnp.zeros((x_ref.shape[0], 1), jnp.float32)
    for part in range(parts):
        block = x_ref[:, part * depth : (part + 1) * depth]
        total += jnp.dot(block, weight_ref[part, slot], preferred_element_type=jnp.float32)
        wide = block.astype(jnp.float32)
        squares += jnp.sum(wide * wide, axis=-1, keepdims=True)
    high = squares.astype(jnp.bfloat16).astype(jnp.float32)
    lane = lax.broadcasted_iota(jnp.int32, (x_ref.shape[0], LANES), 1)
    extra = jnp.where(lane == 0, high, jnp.where(lane == 1, squares - high, 0.0))
    packed_ref[:, :width] = total.astype(jnp.bfloat16)
    packed_ref[:, width:] = extra.astype(jnp.bfloat16)


def project_queries(x, weights, slot):
    rows = x.shape[0]
    parts, _, depth, width = weights.shape
    return pl.pallas_call(
        functools.partial(query_kernel, slot),
        out_shape=jax.ShapeDtypeStruct((rows, width + LANES), jnp.bfloat16),
        in_specs=[IN_VMEM, IN_VMEM],
        out_specs=IN_VMEM,
        compiler_params=LIMIT,
        cost_estimate=cost(2 * rows * parts * depth * width, 2 * parts * depth * width),
    )(x, weights)


def attend_kernel(
    width, section, place_ref, choice_ref, tiles_ref, length_ref, packed_ref, keyval_ref, result_ref
):
    sources, rows, columns = packed_ref.shape
    heads = (columns - LANES) // HD
    keys = keyval_ref.shape[1]
    first = place_ref[0] * rows
    sample = first // TXT
    key = lax.broadcasted_iota(jnp.int32, (1, keys), 1)
    valid = jnp.where(key < tiles_ref[choice_ref[sample]] * TROWS, 1.0, 0.0)
    position = first - sample * TXT + lax.broadcasted_iota(jnp.int32, (rows, 1), 0)
    live = jnp.where(position < length_ref[sample], 1.0, 0.0)
    summed = packed_ref[0].astype(jnp.float32)
    for source in range(1, sources):
        summed += packed_ref[source].astype(jnp.float32)
    squares = summed[:, heads * HD : heads * HD + 1] + summed[:, heads * HD + 1 : heads * HD + 2]
    inverse = lax.rsqrt(squares / width + epsilon) * (float(HD) ** (-0.5))
    queries = jnp.concatenate(
        [summed[:, head * HD : (head + 1) * HD] * inverse for head in range(heads)], axis=0
    ).astype(jnp.bfloat16)
    scores = lax.dot_general(
        queries,
        keyval_ref[section, :, :HD],
        (((1,), (1,)), ((), ())),
        preferred_element_type=jnp.float32,
    )
    weighted = jnp.exp(scores) * valid
    weights = (weighted / jnp.sum(weighted, axis=-1, keepdims=True)).astype(jnp.bfloat16)
    context = jnp.dot(weights, keyval_ref[section, :, HD:], preferred_element_type=jnp.float32)
    for head in range(heads):
        part = (context[head * rows : (head + 1) * rows] * live).astype(jnp.bfloat16)
        for target in range(result_ref.shape[0]):
            result_ref[target, :, head * HD : (head + 1) * HD] = part


def attend(place, choice, tiles, lengths, packed, keyval, section, width):
    sources, rows, columns = packed.shape
    keys = keyval.shape[1]
    heads = (columns - LANES) // HD
    return pl.pallas_call(
        functools.partial(attend_kernel, width, section),
        out_shape=jax.ShapeDtypeStruct((sources, rows, heads * HD), jnp.bfloat16),
        in_specs=[IN_SMEM, IN_SMEM, IN_SMEM, IN_SMEM, IN_VMEM, IN_VMEM],
        out_specs=IN_VMEM,
        compiler_params=LIMIT,
        cost_estimate=cost(4 * heads * rows * keys * HD, packed.size * 2, heads * rows * keys),
    )(place, choice, tiles, lengths, packed, keyval)


def output_kernel(slot, context_ref, weight_ref, own_ref, result_ref):
    parts, _, depth, _ = weight_ref.shape
    total = own_ref[...].astype(jnp.float32)
    for part in range(parts):
        total += jnp.dot(
            context_ref[:, part * depth : (part + 1) * depth],
            weight_ref[part, slot],
            preferred_element_type=jnp.float32,
        )
    result_ref[...] = total.astype(jnp.bfloat16)


def project_output(context, weights, slot, own):
    rows, depth = context.shape
    columns = own.shape[1]
    return pl.pallas_call(
        functools.partial(output_kernel, slot),
        out_shape=jax.ShapeDtypeStruct(own.shape, jnp.bfloat16),
        in_specs=[IN_VMEM, IN_VMEM, IN_VMEM],
        out_specs=IN_VMEM,
        compiler_params=LIMIT,
        cost_estimate=cost(2 * rows * depth * columns, 2 * depth * columns),
    )(context, weights, own)


def exchange(block, axes):
    return lax.all_to_all(block, axes, 0, 0, tiled=True)


def on_device(
    text_rows,
    image_rows,
    tile_counts,
    text_lengths,
    sample_image,
    norm_gain,
    query_weight,
    keyval_weight,
    output_weight,
    cross_gate,
):
    phases, dps, mps = (lax.axis_size(name) for name in ("phase", "dp", "mp"))
    phase_index = lax.axis_index("phase")
    width = norm_gain.shape[1]
    own_rows = text_rows.shape[0]
    part_rows = own_rows // phases
    depth, head_width = query_weight.shape[1:]
    slots = dps // mps
    piece = depth // mps
    context_part = output_weight.shape[1]

    def spread(own_part):
        return lax.all_gather(own_part, "mp", axis=1, tiled=True)

    gain = lax.dynamic_slice_in_dim(norm_gain[0], lax.axis_index("dp") * depth, depth, 0)
    wq = (query_weight[0].astype(jnp.float32) * gain[:, None]).astype(jnp.bfloat16)
    wq = lax.all_gather(wq, "phase", axis=0, tiled=False)[None]

    wo = output_weight.reshape(context_part, slots, mps, piece).transpose(2, 0, 1, 3)
    wo = exchange(wo, "mp").transpose(0, 2, 1, 3).reshape(dps, context_part, piece)
    wo = exchange(wo, "dp").reshape(dps * context_part, piece)
    wo = lax.all_gather(wo, "phase", axis=0, tiled=False)[None]

    mine = lax.dynamic_slice_in_dim(text_rows, phase_index * part_rows, part_rows, 0)
    mine = spread(mine).reshape(part_rows, dps, depth).transpose(1, 0, 2)
    carried = exchange(mine, "dp").reshape(dps * part_rows, depth)
    own = lax.dynamic_slice_in_dim(carried, lax.axis_index("mp") * piece, piece, 1)

    samples = [(phase * part_rows) // TXT for phase in range(phases)]
    images = lax.all_gather(image_rows, ("phase", "mp"), axis=1, tiled=True)
    keyval = project_keyval(samples, sample_image, cross_gate, images, keyval_weight[0, :, 0, :])
    keyval = exchange(keyval, "phase")
    place = jnp.full((1,), phase_index, jnp.int32)

    states = []
    for section in range(phases):
        if section:
            carried = spread(own)
        packed = project_queries(carried, wq, section)
        packed = exchange(packed.reshape(dps, part_rows, head_width + LANES), "dp")
        context = attend(
            place, sample_image, tile_counts, text_lengths, packed, keyval, section, width
        )
        context = spread(exchange(context, "dp").reshape(dps * part_rows, head_width))
        own = project_output(context, wo, section, own)
        states.append(own)
    result = jnp.stack(states).reshape(phases * dps, part_rows, piece)
    result = exchange(result, ("phase", "dp")).reshape(phases, mps, slots, part_rows, piece)
    result = exchange(result.transpose(1, 0, 2, 3, 4), "mp")
    return result.transpose(1, 3, 2, 0, 4).reshape(1, own_rows, -1)


def solution(mesh):
    placed = (
        P("dp", "mp"),
        P("dp", ("phase", "mp"), None),
        P("dp"),
        P("dp"),
        P("dp"),
        P("phase", None),
        P("phase", "dp", "mp"),
        P("phase", None, "mp", None),
        P("phase", "dp", "mp"),
        P("phase"),
    )
    return jax.shard_map(
        on_device, mesh=mesh, in_specs=placed, out_specs=P("phase", "dp", "mp"), check_vma=False
    )
```

```python
import functools

import jax
import jax.numpy as jnp
from jax import lax
from jax.experimental import pallas as pl
from jax.experimental.pallas import tpu as pltpu
from jax.sharding import PartitionSpec as P

HD = 128
HQ_DEV = 4
TROWS = 32
SAMP = 2
TXT = 64
LANES = 128

epsilon = 1e-05
IN_VMEM = pl.BlockSpec(memory_space=pltpu.VMEM)
IN_SMEM = pl.BlockSpec(memory_space=pltpu.SMEM)
LIMIT = pltpu.CompilerParams(vmem_limit_bytes=24 * 2**20)


def cost(flops, bytes_accessed, transcendentals=0):
    return pl.CostEstimate(
        flops=flops, bytes_accessed=bytes_accessed, transcendentals=transcendentals
    )


def keyval_kernel(samples, choice_ref, gate_ref, images_ref, weight_ref, result_ref, held):
    count, keys, depth = images_ref.shape
    factor = jnp.tanh(jnp.full((1, HD), gate_ref[0], jnp.float32))
    for image in range(count):
        both = jnp.dot(images_ref[image], weight_ref[...], preferred_element_type=jnp.float32)
        held[image, :, :HD] = both[:, :HD].astype(jnp.bfloat16)
        held[image, :, HD:] = (both[:, HD:] * factor).astype(jnp.bfloat16)
    for slot, sample in enumerate(samples):
        result_ref[slot] = held[choice_ref[sample]]


def project_keyval(samples, choice, gate, images, weight):
    count, keys, depth = images.shape
    return pl.pallas_call(
        functools.partial(keyval_kernel, samples),
        out_shape=jax.ShapeDtypeStruct((len(samples), keys, 2 * HD), jnp.bfloat16),
        in_specs=[IN_SMEM, IN_SMEM, IN_VMEM, IN_VMEM],
        out_specs=IN_VMEM,
        scratch_shapes=[pltpu.VMEM((count, keys, 2 * HD), jnp.bfloat16)],
        compiler_params=LIMIT,
        cost_estimate=cost(4 * count * keys * depth * HD, 2 * images.size + 2 * weight.size),
    )(choice, gate, images, weight)


def query_kernel(slot, x_ref, weight_ref, packed_ref):
    parts, _, depth, width = weight_ref.shape
    total = jnp.zeros((x_ref.shape[0], width), jnp.float32)
    squares = jnp.zeros((x_ref.shape[0], 1), jnp.float32)
    for part in range(parts):
        block = x_ref[:, part * depth : (part + 1) * depth]
        total += jnp.dot(block, weight_ref[part, slot], preferred_element_type=jnp.float32)
        wide = block.astype(jnp.float32)
        squares += jnp.sum(wide * wide, axis=-1, keepdims=True)
    high = squares.astype(jnp.bfloat16).astype(jnp.float32)
    lane = lax.broadcasted_iota(jnp.int32, (x_ref.shape[0], LANES), 1)
    extra = jnp.where(lane == 0, high, jnp.where(lane == 1, squares - high, 0.0))
    packed_ref[:, :width] = total.astype(jnp.bfloat16)
    packed_ref[:, width:] = extra.astype(jnp.bfloat16)


def project_queries(x, weights, slot):
    rows = x.shape[0]
    parts, _, depth, width = weights.shape
    return pl.pallas_call(
        functools.partial(query_kernel, slot),
        out_shape=jax.ShapeDtypeStruct((rows, width + LANES), jnp.bfloat16),
        in_specs=[IN_VMEM, IN_VMEM],
        out_specs=IN_VMEM,
        compiler_params=LIMIT,
        cost_estimate=cost(2 * rows * parts * depth * width, 2 * parts * depth * width),
    )(x, weights)


def attend_kernel(
    width, section, place_ref, choice_ref, tiles_ref, length_ref, packed_ref, keyval_ref, result_ref
):
    sources, rows, columns = packed_ref.shape
    heads = (columns - LANES) // HD
    keys = keyval_ref.shape[1]
    first = place_ref[0] * rows
    sample = first // TXT
    key = lax.broadcasted_iota(jnp.int32, (1, keys), 1)
    valid = jnp.where(key < tiles_ref[choice_ref[sample]] * TROWS, 1.0, 0.0)
    position = first - sample * TXT + lax.broadcasted_iota(jnp.int32, (rows, 1), 0)
    live = jnp.where(position < length_ref[sample], 1.0, 0.0)
    summed = packed_ref[0].astype(jnp.float32)
    for source in range(1, sources):
        summed += packed_ref[source].astype(jnp.float32)
    squares = summed[:, heads * HD : heads * HD + 1] + summed[:, heads * HD + 1 : heads * HD + 2]
    inverse = lax.rsqrt(squares / width + epsilon) * (float(HD) ** (-0.5))
    queries = jnp.concatenate(
        [summed[:, head * HD : (head + 1) * HD] * inverse for head in range(heads)], axis=0
    ).astype(jnp.bfloat16)
    scores = lax.dot_general(
        queries,
        keyval_ref[section, :, :HD],
        (((1,), (1,)), ((), ())),
        preferred_element_type=jnp.float32,
    )
    weighted = jnp.exp(scores) * valid
    weights = (weighted / jnp.sum(weighted, axis=-1, keepdims=True)).astype(jnp.bfloat16)
    context = jnp.dot(weights, keyval_ref[section, :, HD:], preferred_element_type=jnp.float32)
    for head in range(heads):
        part = (context[head * rows : (head + 1) * rows] * live).astype(jnp.bfloat16)
        for target in range(result_ref.shape[0]):
            result_ref[target, :, head * HD : (head + 1) * HD] = part


def attend(place, choice, tiles, lengths, packed, keyval, section, width):
    sources, rows, columns = packed.shape
    keys = keyval.shape[1]
    heads = (columns - LANES) // HD
    return pl.pallas_call(
        functools.partial(attend_kernel, width, section),
        out_shape=jax.ShapeDtypeStruct((sources, rows, heads * HD), jnp.bfloat16),
        in_specs=[IN_SMEM, IN_SMEM, IN_SMEM, IN_SMEM, IN_VMEM, IN_VMEM],
        out_specs=IN_VMEM,
        compiler_params=LIMIT,
        cost_estimate=cost(4 * heads * rows * keys * HD, packed.size * 2, heads * rows * keys),
    )(place, choice, tiles, lengths, packed, keyval)


def output_kernel(slot, context_ref, weight_ref, own_ref, result_ref):
    parts, _, depth, _ = weight_ref.shape
    total = own_ref[...].astype(jnp.float32)
    for part in range(parts):
        total += jnp.dot(
            context_ref[:, part * depth : (part + 1) * depth],
            weight_ref[part, slot],
            preferred_element_type=jnp.float32,
        )
    result_ref[...] = total.astype(jnp.bfloat16)


def project_output(context, weights, slot, own):
    rows, depth = context.shape
    columns = own.shape[1]
    if weights.shape[2:] != (depth // weights.shape[0], columns):
        weights = weights[:, slot].reshape(weights.shape[0], 1, -1, columns)
        slot = 0
    return pl.pallas_call(
        functools.partial(output_kernel, slot),
        out_shape=jax.ShapeDtypeStruct(own.shape, jnp.bfloat16),
        in_specs=[IN_VMEM, IN_VMEM, IN_VMEM],
        out_specs=IN_VMEM,
        compiler_params=LIMIT,
        cost_estimate=cost(2 * rows * depth * columns, 2 * depth * columns),
    )(context, weights, own)


def exchange(block, axes):
    return lax.all_to_all(block, axes, 0, 0, tiled=True)


def on_device(
    text_rows,
    image_rows,
    tile_counts,
    text_lengths,
    sample_image,
    norm_gain,
    query_weight,
    keyval_weight,
    output_weight,
    cross_gate,
):
    phases, dps, mps = (lax.axis_size(name) for name in ("phase", "dp", "mp"))
    phase_index = lax.axis_index("phase")
    width = norm_gain.shape[1]
    own_rows = text_rows.shape[0]
    part_rows = own_rows // phases
    depth, head_width = query_weight.shape[1:]
    slots = dps // mps
    piece = depth // mps
    context_part = output_weight.shape[1]

    def spread(own_part):
        return lax.all_gather(own_part, "mp", axis=1, tiled=True)

    gain = lax.dynamic_slice_in_dim(norm_gain[0], lax.axis_index("dp") * depth, depth, 0)
    wq = (query_weight[0].astype(jnp.float32) * gain[:, None]).astype(jnp.bfloat16)
    wq = exchange(wq.reshape(phases, depth // phases, head_width), "phase")

    wo = output_weight.reshape(context_part, slots, mps, piece).transpose(2, 0, 1, 3)
    wo = exchange(wo, "mp").transpose(0, 2, 1, 3).reshape(dps, context_part, piece)
    wo = exchange(wo, "dp").reshape(phases, dps * context_part // phases, piece)

    mine = lax.dynamic_slice_in_dim(text_rows, phase_index * part_rows, part_rows, 0)
    mine = spread(mine).reshape(part_rows, dps, depth).transpose(1, 0, 2)
    carried = exchange(mine, "dp").reshape(dps * part_rows, depth)
    own = lax.dynamic_slice_in_dim(carried, lax.axis_index("mp") * piece, piece, 1)

    samples = [(phase * part_rows) // TXT for phase in range(phases)]
    images = lax.all_gather(image_rows, ("phase", "mp"), axis=1, tiled=True)
    keyval = project_keyval(samples, sample_image, cross_gate, images, keyval_weight[0, :, 0, :])
    place = jnp.full((1,), phase_index, jnp.int32)

    wo, keyval, carried = lax.optimization_barrier((wo, keyval, carried))
    wo = exchange(wo, "phase").reshape(wq.shape)
    keyval = exchange(keyval, "phase")

    items = [(kind, section) for section in range(1, phases) for kind in ("query", "out")]
    groups = [[("query", 0), ("query", 1)], [("out", 0)]]
    groups += [items[i : i + 2] for i in range(1, len(items), 2)]
    gathered = {}
    for group in groups:
        parts = [(wo if kind == "out" else wq)[section] for kind, section in group]
        block = lax.all_gather(jnp.stack(parts), "phase", axis=0, tiled=False)
        gathered.update({item: (block, slot) for slot, item in enumerate(group)})

    states = []
    for section in range(phases):
        if section:
            carried = spread(own)
        packed = project_queries(carried, *gathered["query", section])
        packed = exchange(packed.reshape(dps, part_rows, head_width + LANES), "dp")
        context = attend(
            place, sample_image, tile_counts, text_lengths, packed, keyval, section, width
        )
        context = spread(exchange(context, "dp").reshape(dps * part_rows, head_width))
        own = project_output(context, *gathered["out", section], own)
        states.append(own)
    result = jnp.stack(states).reshape(phases * dps, part_rows, piece)
    result = exchange(result, ("phase", "dp")).reshape(phases, mps, slots, part_rows, piece)
    result = exchange(result.transpose(1, 0, 2, 3, 4), "mp")
    return result.transpose(1, 3, 2, 0, 4).reshape(1, own_rows, -1)


def solution(mesh):
    placed = (
        P("dp", "mp"),
        P("dp", ("phase", "mp"), None),
        P("dp"),
        P("dp"),
        P("dp"),
        P("phase", None),
        P("phase", "dp", "mp"),
        P("phase", None, "mp", None),
        P("phase", "dp", "mp"),
        P("phase"),
    )
    return jax.shard_map(
        on_device, mesh=mesh, in_specs=placed, out_specs=P("phase", "dp", "mp"), check_vma=False
    )
```

```python
import functools

import jax
import jax.numpy as jnp
from jax import lax
from jax.experimental import pallas as pl
from jax.experimental.pallas import tpu as pltpu
from jax.sharding import PartitionSpec as P

HD = 128
HQ_DEV = 4
TROWS = 32
SAMP = 2
TXT = 64
LANES = 128

epsilon = 1e-05
IN_VMEM = pl.BlockSpec(memory_space=pltpu.VMEM)
IN_PLACE = pl.BlockSpec(memory_space=pl.ANY)
IN_SMEM = pl.BlockSpec(memory_space=pltpu.SMEM)
LIMIT = pltpu.CompilerParams(vmem_limit_bytes=24 * 2**20)


def cost(flops, bytes_accessed, transcendentals=0):
    return pl.CostEstimate(
        flops=flops, bytes_accessed=bytes_accessed, transcendentals=transcendentals
    )


def keyval_kernel(samples, choice_ref, gate_ref, images_ref, weight_ref, result_ref, held):
    count, keys, depth = images_ref.shape
    factor = jnp.tanh(jnp.full((1, HD), gate_ref[0], jnp.float32))
    for image in range(count):
        both = jnp.dot(images_ref[image], weight_ref[...], preferred_element_type=jnp.float32)
        held[image, :, :HD] = both[:, :HD].astype(jnp.bfloat16)
        held[image, :, HD:] = (both[:, HD:] * factor).astype(jnp.bfloat16)
    for slot, sample in enumerate(samples):
        result_ref[slot] = held[choice_ref[sample]]


def project_keyval(samples, choice, gate, images, weight):
    count, keys, depth = images.shape
    return pl.pallas_call(
        functools.partial(keyval_kernel, samples),
        out_shape=jax.ShapeDtypeStruct((len(samples), keys, 2 * HD), jnp.bfloat16),
        in_specs=[IN_SMEM, IN_SMEM, IN_VMEM, IN_VMEM],
        out_specs=IN_VMEM,
        scratch_shapes=[pltpu.VMEM((count, keys, 2 * HD), jnp.bfloat16)],
        compiler_params=LIMIT,
        cost_estimate=cost(4 * count * keys * depth * HD, 2 * images.size + 2 * weight.size),
    )(choice, gate, images, weight)


def start_fetch(distance, blocks, held, sems):
    half = held.shape[0] // 2
    own, near, far, first, second = blocks
    for step, whole in enumerate((own, near, far)):

        @pl.when(distance == step)
        def _():
            pltpu.make_async_copy(whole.at[:half], held.at[:half], sems.at[0]).start()
            pltpu.make_async_copy(whole.at[half:], held.at[half:], sems.at[1]).start()

    @pl.when(distance == 3)
    def _():
        pltpu.make_async_copy(first, held.at[:half], sems.at[0]).start()
        pltpu.make_async_copy(second, held.at[half:], sems.at[1]).start()


def wait_fetch(blocks, held, sems):
    half = held.shape[0] // 2
    pltpu.make_async_copy(blocks[3], held.at[:half], sems.at[0]).wait()
    pltpu.make_async_copy(blocks[4], held.at[half:], sems.at[1]).wait()


def query_kernel(section, place_ref, x_ref, *refs):
    *blocks, packed_ref, held, sems = refs
    start_fetch(place_ref[0] ^ section, blocks, held, sems)
    wide = x_ref[...].astype(jnp.float32)
    squares = jnp.sum(wide * wide, axis=-1, keepdims=True)
    high = squares.astype(jnp.bfloat16).astype(jnp.float32)
    lane = lax.broadcasted_iota(jnp.int32, (x_ref.shape[0], LANES), 1)
    extra = jnp.where(lane == 0, high, jnp.where(lane == 1, squares - high, 0.0))
    width = held.shape[1]
    packed_ref[:, width:] = extra.astype(jnp.bfloat16)
    wait_fetch(blocks, held, sems)
    total = jnp.dot(x_ref[...], held[...], preferred_element_type=jnp.float32)
    packed_ref[:, :width] = total.astype(jnp.bfloat16)


def project_queries(place, x, blocks, section):
    rows = x.shape[0]
    depth, width = blocks[0].shape
    return pl.pallas_call(
        functools.partial(query_kernel, section),
        out_shape=jax.ShapeDtypeStruct((rows, width + LANES), jnp.bfloat16),
        in_specs=[IN_SMEM, IN_VMEM] + [IN_PLACE] * len(blocks),
        out_specs=IN_VMEM,
        scratch_shapes=[
            pltpu.VMEM((depth, width), jnp.bfloat16),
            pltpu.SemaphoreType.DMA((2,)),
        ],
        compiler_params=LIMIT,
        cost_estimate=cost(2 * rows * depth * width, 2 * depth * width),
    )(place, x, *blocks)


def attend_kernel(
    width, section, place_ref, choice_ref, tiles_ref, length_ref, packed_ref, keyval_ref, result_ref
):
    sources, rows, columns = packed_ref.shape
    heads = (columns - LANES) // HD
    keys = keyval_ref.shape[1]
    first = place_ref[0] * rows
    sample = first // TXT
    key = lax.broadcasted_iota(jnp.int32, (1, keys), 1)
    valid = jnp.where(key < tiles_ref[choice_ref[sample]] * TROWS, 1.0, 0.0)
    position = first - sample * TXT + lax.broadcasted_iota(jnp.int32, (rows, 1), 0)
    live = jnp.where(position < length_ref[sample], 1.0, 0.0)
    summed = packed_ref[0].astype(jnp.float32)
    for source in range(1, sources):
        summed += packed_ref[source].astype(jnp.float32)
    squares = summed[:, heads * HD : heads * HD + 1] + summed[:, heads * HD + 1 : heads * HD + 2]
    inverse = lax.rsqrt(squares / width + epsilon) * (float(HD) ** (-0.5))
    queries = jnp.concatenate(
        [summed[:, head * HD : (head + 1) * HD] * inverse for head in range(heads)], axis=0
    ).astype(jnp.bfloat16)
    scores = lax.dot_general(
        queries,
        keyval_ref[section, :, :HD],
        (((1,), (1,)), ((), ())),
        preferred_element_type=jnp.float32,
    )
    weighted = jnp.exp(scores) * valid
    weights = (weighted / jnp.sum(weighted, axis=-1, keepdims=True)).astype(jnp.bfloat16)
    context = jnp.dot(weights, keyval_ref[section, :, HD:], preferred_element_type=jnp.float32)
    for head in range(heads):
        part = (context[head * rows : (head + 1) * rows] * live).astype(jnp.bfloat16)
        for target in range(result_ref.shape[0]):
            result_ref[target, :, head * HD : (head + 1) * HD] = part


def attend(place, choice, tiles, lengths, packed, keyval, section, width):
    sources, rows, columns = packed.shape
    keys = keyval.shape[1]
    heads = (columns - LANES) // HD
    return pl.pallas_call(
        functools.partial(attend_kernel, width, section),
        out_shape=jax.ShapeDtypeStruct((sources, rows, heads * HD), jnp.bfloat16),
        in_specs=[IN_SMEM, IN_SMEM, IN_SMEM, IN_SMEM, IN_VMEM, IN_VMEM],
        out_specs=IN_VMEM,
        compiler_params=LIMIT,
        cost_estimate=cost(4 * heads * rows * keys * HD, packed.size * 2, heads * rows * keys),
    )(place, choice, tiles, lengths, packed, keyval)


def output_kernel(section, place_ref, context_ref, own_ref, *refs):
    *blocks, result_ref, held, sems = refs
    start_fetch(place_ref[0] ^ section, blocks, held, sems)
    total = own_ref[...].astype(jnp.float32)
    wait_fetch(blocks, held, sems)
    total += jnp.dot(context_ref[...], held[...], preferred_element_type=jnp.float32)
    result_ref[...] = total.astype(jnp.bfloat16)


def project_output(place, context, own, blocks, section):
    rows, depth = context.shape
    columns = own.shape[1]
    return pl.pallas_call(
        functools.partial(output_kernel, section),
        out_shape=jax.ShapeDtypeStruct(own.shape, jnp.bfloat16),
        in_specs=[IN_SMEM, IN_VMEM, IN_VMEM] + [IN_PLACE] * len(blocks),
        out_specs=IN_VMEM,
        scratch_shapes=[
            pltpu.VMEM((depth, columns), jnp.bfloat16),
            pltpu.SemaphoreType.DMA((2,)),
        ],
        compiler_params=LIMIT,
        cost_estimate=cost(2 * rows * depth * columns, 2 * depth * columns),
    )(place, context, own, *blocks)


def bring(block):
    phases = lax.axis_size("phase")
    half = block.shape[0] // 2

    def shift(part, distance):
        return lax.ppermute(part, "phase", [(i, i ^ distance) for i in range(phases)])

    near, far = shift(block, 1), shift(block, 2)
    return block, near, far, shift(far[:half], 1), shift(near[half:], 2)


def exchange(block, axes):
    return lax.all_to_all(block, axes, 0, 0, tiled=True)


def on_device(
    text_rows,
    image_rows,
    tile_counts,
    text_lengths,
    sample_image,
    norm_gain,
    query_weight,
    keyval_weight,
    output_weight,
    cross_gate,
):
    phases, dps, mps = (lax.axis_size(name) for name in ("phase", "dp", "mp"))
    phase_index = lax.axis_index("phase")
    width = norm_gain.shape[1]
    own_rows = text_rows.shape[0]
    part_rows = own_rows // phases
    depth, head_width = query_weight.shape[1:]
    slots = dps // mps
    piece = depth // mps
    context_part = output_weight.shape[1]

    def spread(own_part):
        return lax.all_gather(own_part, "mp", axis=1, tiled=True)

    gain = lax.dynamic_slice_in_dim(norm_gain[0], lax.axis_index("dp") * depth, depth, 0)
    wq = (query_weight[0].astype(jnp.float32) * gain[:, None]).astype(jnp.bfloat16)
    wq = bring(wq)

    wo = output_weight.reshape(context_part, slots, mps, piece).transpose(2, 0, 1, 3)
    wo = exchange(wo, "mp").transpose(0, 2, 1, 3).reshape(dps, context_part, piece)
    wo = bring(exchange(wo, "dp").reshape(dps * context_part, piece))

    mine = lax.dynamic_slice_in_dim(text_rows, phase_index * part_rows, part_rows, 0)
    mine = spread(mine).reshape(part_rows, dps, depth).transpose(1, 0, 2)
    carried = exchange(mine, "dp").reshape(dps * part_rows, depth)
    own = lax.dynamic_slice_in_dim(carried, lax.axis_index("mp") * piece, piece, 1)

    samples = [(phase * part_rows) // TXT for phase in range(phases)]
    images = lax.all_gather(image_rows, ("phase", "mp"), axis=1, tiled=True)
    keyval = project_keyval(samples, sample_image, cross_gate, images, keyval_weight[0, :, 0, :])
    keyval = exchange(keyval, "phase")
    place = jnp.full((1,), phase_index, jnp.int32)

    states = []
    for section in range(phases):
        if section:
            carried = spread(own)
        packed = project_queries(place, carried, wq, section)
        packed = exchange(packed.reshape(dps, part_rows, head_width + LANES), "dp")
        context = attend(
            place, sample_image, tile_counts, text_lengths, packed, keyval, section, width
        )
        context = spread(exchange(context, "dp").reshape(dps * part_rows, head_width))
        own = project_output(place, context, own, wo, section)
        states.append(own)
    result = jnp.stack(states).reshape(phases * dps, part_rows, piece)
    result = exchange(result, ("phase", "dp")).reshape(phases, mps, slots, part_rows, piece)
    result = exchange(result.transpose(1, 0, 2, 3, 4), "mp")
    return result.transpose(1, 3, 2, 0, 4).reshape(1, own_rows, -1)


def solution(mesh):
    placed = (
        P("dp", "mp"),
        P("dp", ("phase", "mp"), None),
        P("dp"),
        P("dp"),
        P("dp"),
        P("phase", None),
        P("phase", "dp", "mp"),
        P("phase", None, "mp", None),
        P("phase", "dp", "mp"),
        P("phase"),
    )
    return jax.shard_map(
        on_device, mesh=mesh, in_specs=placed, out_specs=P("phase", "dp", "mp"), check_vma=False
    )
```

```python
import functools

import jax
import jax.numpy as jnp
from jax import lax
from jax.experimental import pallas as pl
from jax.experimental.pallas import tpu as pltpu
from jax.sharding import PartitionSpec as P

HD = 128
HQ_DEV = 4
TROWS = 32
SAMP = 2
TXT = 64
LANES = 128

epsilon = 1e-05
IN_VMEM = pl.BlockSpec(memory_space=pltpu.VMEM)
IN_SMEM = pl.BlockSpec(memory_space=pltpu.SMEM)
LIMIT = pltpu.CompilerParams(vmem_limit_bytes=24 * 2**20)


def cost(flops, bytes_accessed, transcendentals=0):
    return pl.CostEstimate(
        flops=flops, bytes_accessed=bytes_accessed, transcendentals=transcendentals
    )


def keyval_kernel(samples, choice_ref, gate_ref, images_ref, weight_ref, result_ref, held):
    phases, count = images_ref.shape[:2]
    factor = jnp.tanh(jnp.full((1, HD), gate_ref[0], jnp.float32))
    for image in range(count):
        rows = jnp.concatenate([images_ref[phase, image] for phase in range(phases)], axis=0)
        both = jnp.dot(rows, weight_ref[...], preferred_element_type=jnp.float32)
        held[image, :, :HD] = both[:, :HD].astype(jnp.bfloat16)
        held[image, :, HD:] = (both[:, HD:] * factor).astype(jnp.bfloat16)
    for slot, sample in enumerate(samples):
        result_ref[slot] = held[choice_ref[sample]]


def project_keyval(samples, choice, gate, images, weight):
    phases, count, rows, depth = images.shape
    keys = phases * rows
    return pl.pallas_call(
        functools.partial(keyval_kernel, samples),
        out_shape=jax.ShapeDtypeStruct((len(samples), keys, 2 * HD), jnp.bfloat16),
        in_specs=[IN_SMEM, IN_SMEM, IN_VMEM, IN_VMEM],
        out_specs=IN_VMEM,
        scratch_shapes=[pltpu.VMEM((count, keys, 2 * HD), jnp.bfloat16)],
        compiler_params=LIMIT,
        cost_estimate=cost(4 * count * keys * depth * HD, 2 * images.size + 2 * weight.size),
    )(choice, gate, images, weight)


def multiply(distance, x_ref, blocks, finish):
    for step in range(len(blocks) // 2):

        @pl.when(distance == step)
        def _():
            first, second = blocks[2 * step : 2 * step + 2]
            half = first.shape[0]
            total = jnp.dot(x_ref[:, :half], first[...], preferred_element_type=jnp.float32)
            total += jnp.dot(x_ref[:, half:], second[...], preferred_element_type=jnp.float32)
            finish(total)


def query_kernel(section, place_ref, x_ref, *refs):
    *blocks, packed_ref = refs
    width = blocks[0].shape[1]
    wide = x_ref[...].astype(jnp.float32)
    squares = jnp.sum(wide * wide, axis=-1, keepdims=True)
    high = squares.astype(jnp.bfloat16).astype(jnp.float32)
    lane = lax.broadcasted_iota(jnp.int32, (x_ref.shape[0], LANES), 1)
    extra = jnp.where(lane == 0, high, jnp.where(lane == 1, squares - high, 0.0))
    packed_ref[:, width:] = extra.astype(jnp.bfloat16)

    def finish(total):
        packed_ref[:, :width] = total.astype(jnp.bfloat16)

    multiply(place_ref[0] ^ section, x_ref, blocks, finish)


def project_queries(place, x, blocks, section):
    rows, depth = x.shape
    width = blocks[0].shape[1]
    return pl.pallas_call(
        functools.partial(query_kernel, section),
        out_shape=jax.ShapeDtypeStruct((rows, width + LANES), jnp.bfloat16),
        in_specs=[IN_SMEM, IN_VMEM] + [IN_VMEM] * len(blocks),
        out_specs=IN_VMEM,
        compiler_params=LIMIT,
        cost_estimate=cost(2 * rows * depth * width, 2 * depth * width),
    )(place, x, *blocks)


def attend_kernel(
    width, section, place_ref, choice_ref, tiles_ref, length_ref, packed_ref, keyval_ref, result_ref
):
    sources, rows, columns = packed_ref.shape
    heads = (columns - LANES) // HD
    keys = keyval_ref.shape[1]
    first = place_ref[0] * rows
    sample = first // TXT
    key = lax.broadcasted_iota(jnp.int32, (1, keys), 1)
    valid = jnp.where(key < tiles_ref[choice_ref[sample]] * TROWS, 1.0, 0.0)
    position = first - sample * TXT + lax.broadcasted_iota(jnp.int32, (rows, 1), 0)
    live = jnp.where(position < length_ref[sample], 1.0, 0.0)
    summed = packed_ref[0].astype(jnp.float32)
    for source in range(1, sources):
        summed += packed_ref[source].astype(jnp.float32)
    squares = summed[:, heads * HD : heads * HD + 1] + summed[:, heads * HD + 1 : heads * HD + 2]
    inverse = lax.rsqrt(squares / width + epsilon) * (float(HD) ** (-0.5))
    queries = jnp.concatenate(
        [summed[:, head * HD : (head + 1) * HD] * inverse for head in range(heads)], axis=0
    ).astype(jnp.bfloat16)
    scores = lax.dot_general(
        queries,
        keyval_ref[section, :, :HD],
        (((1,), (1,)), ((), ())),
        preferred_element_type=jnp.float32,
    )
    weighted = jnp.exp(scores) * valid
    weights = (weighted / jnp.sum(weighted, axis=-1, keepdims=True)).astype(jnp.bfloat16)
    context = jnp.dot(weights, keyval_ref[section, :, HD:], preferred_element_type=jnp.float32)
    for head in range(heads):
        part = (context[head * rows : (head + 1) * rows] * live).astype(jnp.bfloat16)
        for target in range(result_ref.shape[0]):
            result_ref[target, :, head * HD : (head + 1) * HD] = part


def attend(place, choice, tiles, lengths, packed, keyval, section, width):
    sources, rows, columns = packed.shape
    keys = keyval.shape[1]
    heads = (columns - LANES) // HD
    return pl.pallas_call(
        functools.partial(attend_kernel, width, section),
        out_shape=jax.ShapeDtypeStruct((sources, rows, heads * HD), jnp.bfloat16),
        in_specs=[IN_SMEM, IN_SMEM, IN_SMEM, IN_SMEM, IN_VMEM, IN_VMEM],
        out_specs=IN_VMEM,
        compiler_params=LIMIT,
        cost_estimate=cost(4 * heads * rows * keys * HD, packed.size * 2, heads * rows * keys),
    )(place, choice, tiles, lengths, packed, keyval)


def output_kernel(section, place_ref, context_ref, own_ref, *refs):
    *blocks, result_ref = refs

    def finish(total):
        result_ref[...] = (own_ref[...].astype(jnp.float32) + total).astype(jnp.bfloat16)

    multiply(place_ref[0] ^ section, context_ref, blocks, finish)


def project_output(place, context, own, blocks, section):
    rows, depth = context.shape
    columns = own.shape[1]
    return pl.pallas_call(
        functools.partial(output_kernel, section),
        out_shape=jax.ShapeDtypeStruct(own.shape, jnp.bfloat16),
        in_specs=[IN_SMEM, IN_VMEM, IN_VMEM] + [IN_VMEM] * len(blocks),
        out_specs=IN_VMEM,
        compiler_params=LIMIT,
        cost_estimate=cost(2 * rows * depth * columns, 2 * depth * columns),
    )(place, context, own, *blocks)


def bring(first, second):
    phases = lax.axis_size("phase")

    def shift(part, distance):
        return lax.ppermute(part, "phase", [(i, i ^ distance) for i in range(phases)])

    near_first, far_first = shift(first, 1), shift(first, 2)
    near_second, far_second = shift(second, 1), shift(second, 2)
    across = shift(far_first, 1), shift(near_second, 2)
    return first, second, near_first, near_second, far_first, far_second, *across


def exchange(block, axes):
    return lax.all_to_all(block, axes, 0, 0, tiled=True)


def on_device(
    text_rows,
    image_rows,
    tile_counts,
    text_lengths,
    sample_image,
    norm_gain,
    query_weight,
    keyval_weight,
    output_weight,
    cross_gate,
):
    phases, dps, mps = (lax.axis_size(name) for name in ("phase", "dp", "mp"))
    phase_index = lax.axis_index("phase")
    width = norm_gain.shape[1]
    own_rows = text_rows.shape[0]
    part_rows = own_rows // phases
    depth, head_width = query_weight.shape[1:]
    slots = dps // mps
    piece = depth // mps
    context_part = output_weight.shape[1]

    def spread(own_part):
        return lax.all_gather(own_part, "mp", axis=1, tiled=True)

    images = jnp.broadcast_to(image_rows[None], (phases,) + image_rows.shape)
    images = lax.all_gather(exchange(images, "phase"), "mp", axis=2, tiled=True)

    wo = output_weight.reshape(context_part, slots, mps, piece).transpose(2, 1, 0, 3)
    wo = exchange(wo, "mp").reshape(dps, context_part, piece)
    wo = exchange(wo, "dp")
    middle = dps // 2
    wo = bring(wo[:middle].reshape(-1, piece), wo[middle:].reshape(-1, piece))

    gain = lax.dynamic_slice_in_dim(norm_gain[0], lax.axis_index("dp") * depth, depth, 0)
    middle = depth // 2
    wq = bring(
        *[
            (query_weight[0, rows].astype(jnp.float32) * gain[rows, None]).astype(jnp.bfloat16)
            for rows in (slice(0, middle), slice(middle, depth))
        ]
    )

    mine = lax.dynamic_slice_in_dim(text_rows, phase_index * part_rows, part_rows, 0)
    mine = spread(mine).reshape(part_rows, dps, depth).transpose(1, 0, 2)
    carried = exchange(mine, "dp").reshape(dps * part_rows, depth)
    own = lax.dynamic_slice_in_dim(carried, lax.axis_index("mp") * piece, piece, 1)

    samples = [(phase * part_rows) // TXT for phase in range(phases)]
    keyval = project_keyval(samples, sample_image, cross_gate, images, keyval_weight[0, :, 0, :])
    keyval = exchange(keyval, "phase")
    place = jnp.full((1,), phase_index, jnp.int32)

    states = []
    for section in range(phases):
        if section:
            carried = spread(own)
        packed = project_queries(place, carried, wq, section)
        packed = exchange(packed.reshape(dps, part_rows, head_width + LANES), "dp")
        context = attend(
            place, sample_image, tile_counts, text_lengths, packed, keyval, section, width
        )
        context = spread(exchange(context, "dp").reshape(dps * part_rows, head_width))
        own = project_output(place, context, own, wo, section)
        states.append(own)
    result = jnp.stack(states).reshape(phases * dps, part_rows, piece)
    result = exchange(result, ("phase", "dp")).reshape(phases, mps, slots, part_rows, piece)
    result = exchange(result.transpose(1, 0, 2, 3, 4), "mp")
    return result.transpose(1, 3, 2, 0, 4).reshape(1, own_rows, -1)


def solution(mesh):
    placed = (
        P("dp", "mp"),
        P("dp", ("phase", "mp"), None),
        P("dp"),
        P("dp"),
        P("dp"),
        P("phase", None),
        P("phase", "dp", "mp"),
        P("phase", None, "mp", None),
        P("phase", "dp", "mp"),
        P("phase"),
    )
    return jax.shard_map(
        on_device, mesh=mesh, in_specs=placed, out_specs=P("phase", "dp", "mp"), check_vma=False
    )
```

```python
import functools

import jax
import jax.numpy as jnp
from jax import lax
from jax.experimental import pallas as pl
from jax.experimental.pallas import tpu as pltpu
from jax.sharding import PartitionSpec as P

HD = 128
HQ_DEV = 4
TROWS = 32
SAMP = 2
TXT = 64
LANES = 128

epsilon = 1e-05
IN_VMEM = pl.BlockSpec(memory_space=pltpu.VMEM)
IN_PLACE = pl.BlockSpec(memory_space=pl.ANY)
IN_SMEM = pl.BlockSpec(memory_space=pltpu.SMEM)
LIMIT = pltpu.CompilerParams(vmem_limit_bytes=24 * 2**20)


def cost(flops, bytes_accessed, transcendentals=0):
    return pl.CostEstimate(
        flops=flops, bytes_accessed=bytes_accessed, transcendentals=transcendentals
    )


def keyval_kernel(samples, choice_ref, gate_ref, images_ref, weight_ref, result_ref, held):
    phases, count = images_ref.shape[:2]
    factor = jnp.tanh(jnp.full((1, HD), gate_ref[0], jnp.float32))
    for image in range(count):
        rows = jnp.concatenate([images_ref[phase, image] for phase in range(phases)], axis=0)
        both = jnp.dot(rows, weight_ref[...], preferred_element_type=jnp.float32)
        held[image, :, :HD] = both[:, :HD].astype(jnp.bfloat16)
        held[image, :, HD:] = (both[:, HD:] * factor).astype(jnp.bfloat16)
    for slot, sample in enumerate(samples):
        result_ref[slot] = held[choice_ref[sample]]


def project_keyval(samples, choice, gate, images, weight):
    phases, count, rows, depth = images.shape
    keys = phases * rows
    return pl.pallas_call(
        functools.partial(keyval_kernel, samples),
        out_shape=jax.ShapeDtypeStruct((len(samples), keys, 2 * HD), jnp.bfloat16),
        in_specs=[IN_SMEM, IN_SMEM, IN_VMEM, IN_VMEM],
        out_specs=IN_VMEM,
        scratch_shapes=[pltpu.VMEM((count, keys, 2 * HD), jnp.bfloat16)],
        compiler_params=LIMIT,
        cost_estimate=cost(4 * count * keys * depth * HD, 2 * images.size + 2 * weight.size),
    )(choice, gate, images, weight)


def start_copy(distance, blocks, target, sems):
    half = target.shape[0] // 2
    for step in range(len(blocks) // 2):

        @pl.when(distance == step)
        def _():
            pltpu.make_async_copy(blocks[2 * step], target.at[:half], sems.at[0]).start()
            pltpu.make_async_copy(blocks[2 * step + 1], target.at[half:], sems.at[1]).start()


def wait_copy(blocks, target, sems):
    half = target.shape[0] // 2
    pltpu.make_async_copy(blocks[0], target.at[:half], sems.at[0]).wait()
    pltpu.make_async_copy(blocks[1], target.at[half:], sems.at[1]).wait()


def arrange_kernel(sections, place_ref, *refs):
    blocks, targets, sems = refs[: -len(sections) - 1], refs[-len(sections) - 1 : -1], refs[-1]
    for step, section in enumerate(sections):
        start_copy(place_ref[0] ^ section, blocks, targets[step], sems.at[step])
    for step in range(len(sections)):
        wait_copy(blocks, targets[step], sems.at[step])


def arrange(place, blocks, sections):
    half, columns = blocks[0].shape
    whole = jax.ShapeDtypeStruct((2 * half, columns), jnp.bfloat16)
    return pl.pallas_call(
        functools.partial(arrange_kernel, sections),
        out_shape=[whole] * len(sections),
        in_specs=[IN_SMEM] + [IN_PLACE] * len(blocks),
        out_specs=[IN_PLACE] * len(sections),
        scratch_shapes=[pltpu.SemaphoreType.DMA((len(sections), 2))],
        compiler_params=LIMIT,
        cost_estimate=cost(0, 8 * half * columns * len(sections)),
    )(place, *blocks)


def query_kernel(section, place_ref, x_ref, *refs):
    if section is None:
        weight_ref, packed_ref = refs
    else:
        *blocks, packed_ref, weight_ref, sems = refs
        start_copy(place_ref[0] ^ section, blocks, weight_ref, sems)
    width = weight_ref.shape[1]
    wide = x_ref[...].astype(jnp.float32)
    squares = jnp.sum(wide * wide, axis=-1, keepdims=True)
    high = squares.astype(jnp.bfloat16).astype(jnp.float32)
    lane = lax.broadcasted_iota(jnp.int32, (x_ref.shape[0], LANES), 1)
    extra = jnp.where(lane == 0, high, jnp.where(lane == 1, squares - high, 0.0))
    packed_ref[:, width:] = extra.astype(jnp.bfloat16)
    if section is not None:
        wait_copy(blocks, weight_ref, sems)
    total = jnp.dot(x_ref[...], weight_ref[...], preferred_element_type=jnp.float32)
    packed_ref[:, :width] = total.astype(jnp.bfloat16)


def output_kernel(section, place_ref, context_ref, own_ref, *refs):
    if section is None:
        weight_ref, result_ref = refs
    else:
        *blocks, result_ref, weight_ref, sems = refs
        start_copy(place_ref[0] ^ section, blocks, weight_ref, sems)
        wait_copy(blocks, weight_ref, sems)
    total = own_ref[...].astype(jnp.float32)
    total += jnp.dot(context_ref[...], weight_ref[...], preferred_element_type=jnp.float32)
    result_ref[...] = total.astype(jnp.bfloat16)


def project(kernel, place, operands, weights, section, columns):
    rows = operands[0].shape[0]
    fetch = section is not None
    depth = weights[0].shape[0] * (2 if fetch else 1)
    width = weights[0].shape[1]
    scratch = [pltpu.VMEM((depth, width), jnp.bfloat16), pltpu.SemaphoreType.DMA((2,))]
    return pl.pallas_call(
        functools.partial(kernel, section),
        out_shape=jax.ShapeDtypeStruct((rows, columns), jnp.bfloat16),
        in_specs=[IN_SMEM]
        + [IN_VMEM] * len(operands)
        + [IN_PLACE if fetch else IN_VMEM] * len(weights),
        out_specs=IN_VMEM,
        scratch_shapes=scratch if fetch else [],
        compiler_params=LIMIT,
        cost_estimate=cost(2 * rows * depth * width, 2 * depth * width),
    )(place, *operands, *weights)


def attend_kernel(
    width, section, place_ref, choice_ref, tiles_ref, length_ref, packed_ref, keyval_ref, result_ref
):
    sources, rows, columns = packed_ref.shape
    heads = (columns - LANES) // HD
    keys = keyval_ref.shape[1]
    first = place_ref[0] * rows
    sample = first // TXT
    key = lax.broadcasted_iota(jnp.int32, (1, keys), 1)
    valid = jnp.where(key < tiles_ref[choice_ref[sample]] * TROWS, 1.0, 0.0)
    position = first - sample * TXT + lax.broadcasted_iota(jnp.int32, (rows, 1), 0)
    live = jnp.where(position < length_ref[sample], 1.0, 0.0)
    summed = packed_ref[0].astype(jnp.float32)
    for source in range(1, sources):
        summed += packed_ref[source].astype(jnp.float32)
    squares = summed[:, heads * HD : heads * HD + 1] + summed[:, heads * HD + 1 : heads * HD + 2]
    inverse = lax.rsqrt(squares / width + epsilon) * (float(HD) ** (-0.5))
    queries = jnp.concatenate(
        [summed[:, head * HD : (head + 1) * HD] * inverse for head in range(heads)], axis=0
    ).astype(jnp.bfloat16)
    scores = lax.dot_general(
        queries,
        keyval_ref[section, :, :HD],
        (((1,), (1,)), ((), ())),
        preferred_element_type=jnp.float32,
    )
    weighted = jnp.exp(scores) * valid
    weights = (weighted / jnp.sum(weighted, axis=-1, keepdims=True)).astype(jnp.bfloat16)
    context = jnp.dot(weights, keyval_ref[section, :, HD:], preferred_element_type=jnp.float32)
    for head in range(heads):
        part = (context[head * rows : (head + 1) * rows] * live).astype(jnp.bfloat16)
        for target in range(result_ref.shape[0]):
            result_ref[target, :, head * HD : (head + 1) * HD] = part


def attend(place, choice, tiles, lengths, packed, keyval, section, width):
    sources, rows, columns = packed.shape
    keys = keyval.shape[1]
    heads = (columns - LANES) // HD
    return pl.pallas_call(
        functools.partial(attend_kernel, width, section),
        out_shape=jax.ShapeDtypeStruct((sources, rows, heads * HD), jnp.bfloat16),
        in_specs=[IN_SMEM, IN_SMEM, IN_SMEM, IN_SMEM, IN_VMEM, IN_VMEM],
        out_specs=IN_VMEM,
        compiler_params=LIMIT,
        cost_estimate=cost(4 * heads * rows * keys * HD, packed.size * 2, heads * rows * keys),
    )(place, choice, tiles, lengths, packed, keyval)


def assemble_kernel(received_ref, result_ref):
    cores, phases, slots, rows, piece = received_ref.shape
    for phase in range(phases):
        for slot in range(slots):
            for core in range(cores):
                column = (slot * cores + core) * piece
                result_ref[0, phase * rows : (phase + 1) * rows, column : column + piece] = (
                    received_ref[core, phase, slot]
                )


def assemble(received):
    cores, phases, slots, rows, piece = received.shape
    return pl.pallas_call(
        assemble_kernel,
        out_shape=jax.ShapeDtypeStruct((1, phases * rows, slots * cores * piece), received.dtype),
        in_specs=[IN_VMEM],
        out_specs=IN_VMEM,
        compiler_params=LIMIT,
        cost_estimate=cost(0, 4 * received.size),
    )(received)


def bring(first, second):
    phases = lax.axis_size("phase")

    def shift(part, distance):
        return lax.ppermute(part, "phase", [(i, i ^ distance) for i in range(phases)])

    near_first, far_first = shift(first, 1), shift(first, 2)
    near_second, far_second = shift(second, 1), shift(second, 2)
    across = shift(far_first, 1), shift(near_second, 2)
    return first, second, near_first, near_second, far_first, far_second, *across


def exchange(block, axes):
    return lax.all_to_all(block, axes, 0, 0, tiled=True)


def on_device(
    text_rows,
    image_rows,
    tile_counts,
    text_lengths,
    sample_image,
    norm_gain,
    query_weight,
    keyval_weight,
    output_weight,
    cross_gate,
):
    phases, dps, mps = (lax.axis_size(name) for name in ("phase", "dp", "mp"))
    phase_index = lax.axis_index("phase")
    width = norm_gain.shape[1]
    own_rows = text_rows.shape[0]
    part_rows = own_rows // phases
    depth, head_width = query_weight.shape[1:]
    slots = dps // mps
    piece = depth // mps
    context_part = output_weight.shape[1]

    def spread(own_part):
        return lax.all_gather(own_part, "mp", axis=1, tiled=True)

    wo = output_weight.reshape(context_part, slots, mps, piece).transpose(2, 1, 0, 3)
    wo = exchange(wo.reshape(mps, slots * context_part, piece), "mp")
    wo = exchange(wo.reshape(dps, context_part, piece), "dp")
    middle = dps // 2
    wo = bring(wo[:middle].reshape(-1, piece), wo[middle:].reshape(-1, piece))

    gain = lax.dynamic_slice_in_dim(norm_gain[0], lax.axis_index("dp") * depth, depth, 0)
    middle = depth // 2
    wq = bring(
        *[
            (query_weight[0, rows].astype(jnp.float32) * gain[rows, None]).astype(jnp.bfloat16)
            for rows in (slice(0, middle), slice(middle, depth))
        ]
    )

    image_rows, _ = lax.optimization_barrier((image_rows, wq[2]))
    images = jnp.broadcast_to(image_rows[None], (phases,) + image_rows.shape)
    images = lax.all_gather(exchange(images, "phase"), "mp", axis=2, tiled=True)

    mine = lax.dynamic_slice_in_dim(text_rows, phase_index * part_rows, part_rows, 0)
    mine = spread(mine).reshape(part_rows, dps, depth).transpose(1, 0, 2)
    carried = exchange(mine, "dp").reshape(dps * part_rows, depth)
    own = lax.dynamic_slice_in_dim(carried, lax.axis_index("mp") * piece, piece, 1)

    samples = [(phase * part_rows) // TXT for phase in range(phases)]
    keyval = project_keyval(samples, sample_image, cross_gate, images, keyval_weight[0, :, 0, :])
    keyval = exchange(keyval, "phase")
    place = jnp.full((1,), phase_index, jnp.int32)

    later = range(1, phases)
    wq_later, wo_later = arrange(place, wq, later), arrange(place, wo, later)
    packed_width = head_width + LANES
    states = []
    for section in range(phases):
        if section == 0:
            packed = project(query_kernel, place, [carried], wq, 0, packed_width)
        else:
            carried = spread(own)
            weights = [wq_later[section - 1]]
            packed = project(query_kernel, place, [carried], weights, None, packed_width)
        packed = exchange(packed.reshape(dps, part_rows, packed_width), "dp")
        context = attend(
            place, sample_image, tile_counts, text_lengths, packed, keyval, section, width
        )
        context = spread(exchange(context, "dp").reshape(dps * part_rows, head_width))
        if section == 0:
            own = project(output_kernel, place, [context, own], wo, 0, piece)
        else:
            weights = [wo_later[section - 1]]
            own = project(output_kernel, place, [context, own], weights, None, piece)
        states.append(own)
    result = jnp.stack(states).reshape(phases * dps, part_rows, piece)
    result = exchange(result, ("phase", "dp")).reshape(phases, mps, slots, part_rows, piece)
    return assemble(exchange(result.transpose(1, 0, 2, 3, 4), "mp"))


def solution(mesh):
    placed = (
        P("dp", "mp"),
        P("dp", ("phase", "mp"), None),
        P("dp"),
        P("dp"),
        P("dp"),
        P("phase", None),
        P("phase", "dp", "mp"),
        P("phase", None, "mp", None),
        P("phase", "dp", "mp"),
        P("phase"),
    )
    return jax.shard_map(
        on_device, mesh=mesh, in_specs=placed, out_specs=P("phase", "dp", "mp"), check_vma=False
    )
```

```python
import functools

import jax
import jax.numpy as jnp
from jax import lax
from jax.experimental import pallas as pl
from jax.experimental.pallas import tpu as pltpu
from jax.sharding import PartitionSpec as P

HD = 128
HQ_DEV = 4
TROWS = 32
SAMP = 2
TXT = 64
LANES = 128

epsilon = 1e-05
IN_VMEM = pl.BlockSpec(memory_space=pltpu.VMEM)
IN_PLACE = pl.BlockSpec(memory_space=pl.ANY)
IN_SMEM = pl.BlockSpec(memory_space=pltpu.SMEM)
LIMIT = pltpu.CompilerParams(vmem_limit_bytes=24 * 2**20)


def cost(flops, bytes_accessed, transcendentals=0):
    return pl.CostEstimate(
        flops=flops, bytes_accessed=bytes_accessed, transcendentals=transcendentals
    )


def keyval_kernel(samples, choice_ref, gate_ref, images_ref, weight_ref, result_ref, held):
    phases, count = images_ref.shape[:2]
    factor = jnp.tanh(jnp.full((1, HD), gate_ref[0], jnp.float32))
    for image in range(count):
        rows = jnp.concatenate([images_ref[phase, image] for phase in range(phases)], axis=0)
        both = jnp.dot(rows, weight_ref[...], preferred_element_type=jnp.float32)
        held[image, :, :HD] = both[:, :HD].astype(jnp.bfloat16)
        held[image, :, HD:] = (both[:, HD:] * factor).astype(jnp.bfloat16)
    for slot, sample in enumerate(samples):
        result_ref[slot] = held[choice_ref[sample]]


def project_keyval(samples, choice, gate, images, weight):
    phases, count, rows, depth = images.shape
    keys = phases * rows
    return pl.pallas_call(
        functools.partial(keyval_kernel, samples),
        out_shape=jax.ShapeDtypeStruct((len(samples), keys, 2 * HD), jnp.bfloat16),
        in_specs=[IN_SMEM, IN_SMEM, IN_VMEM, IN_VMEM],
        out_specs=IN_VMEM,
        scratch_shapes=[pltpu.VMEM((count, keys, 2 * HD), jnp.bfloat16)],
        compiler_params=LIMIT,
        cost_estimate=cost(4 * count * keys * depth * HD, 2 * images.size + 2 * weight.size),
    )(choice, gate, images, weight)


def start_copy(distance, blocks, target, sems):
    half = target.shape[0] // 2
    for step in range(len(blocks) // 2):

        @pl.when(distance == step)
        def _():
            pltpu.make_async_copy(blocks[2 * step], target.at[:half], sems.at[0]).start()
            pltpu.make_async_copy(blocks[2 * step + 1], target.at[half:], sems.at[1]).start()


def wait_copy(blocks, target, sems):
    half = target.shape[0] // 2
    pltpu.make_async_copy(blocks[0], target.at[:half], sems.at[0]).wait()
    pltpu.make_async_copy(blocks[1], target.at[half:], sems.at[1]).wait()


def arrange_kernel(sections, place_ref, *refs):
    blocks, targets, sems = refs[: -len(sections) - 1], refs[-len(sections) - 1 : -1], refs[-1]
    for step, section in enumerate(sections):
        start_copy(place_ref[0] ^ section, blocks, targets[step], sems.at[step])
    for step in range(len(sections)):
        wait_copy(blocks, targets[step], sems.at[step])


def arrange(place, blocks, sections):
    half, columns = blocks[0].shape
    whole = jax.ShapeDtypeStruct((2 * half, columns), jnp.bfloat16)
    return pl.pallas_call(
        functools.partial(arrange_kernel, sections),
        out_shape=[whole] * len(sections),
        in_specs=[IN_SMEM] + [IN_PLACE] * len(blocks),
        out_specs=[IN_PLACE] * len(sections),
        scratch_shapes=[pltpu.SemaphoreType.DMA((len(sections), 2))],
        compiler_params=LIMIT,
        cost_estimate=cost(0, 8 * half * columns * len(sections)),
    )(place, *blocks)


def query_kernel(section, place_ref, x_ref, *refs):
    if section is None:
        weight_ref, packed_ref = refs
    else:
        *blocks, packed_ref, weight_ref, sems = refs
        start_copy(place_ref[0] ^ section, blocks, weight_ref, sems)
    width = weight_ref.shape[1]
    wide = x_ref[...].astype(jnp.float32)
    squares = jnp.sum(wide * wide, axis=-1, keepdims=True)
    high = squares.astype(jnp.bfloat16).astype(jnp.float32)
    lane = lax.broadcasted_iota(jnp.int32, (x_ref.shape[0], LANES), 1)
    extra = jnp.where(lane == 0, high, jnp.where(lane == 1, squares - high, 0.0))
    packed_ref[:, width:] = extra.astype(jnp.bfloat16)
    if section is not None:
        wait_copy(blocks, weight_ref, sems)
    total = jnp.dot(x_ref[...], weight_ref[...], preferred_element_type=jnp.float32)
    packed_ref[:, :width] = total.astype(jnp.bfloat16)


def output_kernel(section, place_ref, context_ref, own_ref, *refs):
    if section is None:
        weight_ref, result_ref = refs
    else:
        *blocks, result_ref, weight_ref, sems = refs
        start_copy(place_ref[0] ^ section, blocks, weight_ref, sems)
        wait_copy(blocks, weight_ref, sems)
    total = own_ref[...].astype(jnp.float32)
    total += jnp.dot(context_ref[...], weight_ref[...], preferred_element_type=jnp.float32)
    result_ref[...] = total.astype(jnp.bfloat16)


def project(kernel, place, operands, weights, section, columns):
    rows = operands[0].shape[0]
    fetch = section is not None
    depth = weights[0].shape[0] * (2 if fetch else 1)
    width = weights[0].shape[1]
    scratch = [pltpu.VMEM((depth, width), jnp.bfloat16), pltpu.SemaphoreType.DMA((2,))]
    return pl.pallas_call(
        functools.partial(kernel, section),
        out_shape=jax.ShapeDtypeStruct((rows, columns), jnp.bfloat16),
        in_specs=[IN_SMEM]
        + [IN_VMEM] * len(operands)
        + [IN_PLACE if fetch else IN_VMEM] * len(weights),
        out_specs=IN_VMEM,
        scratch_shapes=scratch if fetch else [],
        compiler_params=LIMIT,
        cost_estimate=cost(2 * rows * depth * width, 2 * depth * width),
    )(place, *operands, *weights)


def attend_kernel(
    width, section, place_ref, choice_ref, tiles_ref, length_ref, packed_ref, keyval_ref, result_ref
):
    sources, rows, columns = packed_ref.shape
    heads = (columns - LANES) // HD
    keys = keyval_ref.shape[1]
    first = place_ref[0] * rows
    sample = first // TXT
    key = lax.broadcasted_iota(jnp.int32, (1, keys), 1)
    valid = jnp.where(key < tiles_ref[choice_ref[sample]] * TROWS, 1.0, 0.0)
    position = first - sample * TXT + lax.broadcasted_iota(jnp.int32, (rows, 1), 0)
    live = jnp.where(position < length_ref[sample], 1.0, 0.0)
    summed = packed_ref[0].astype(jnp.float32)
    for source in range(1, sources):
        summed += packed_ref[source].astype(jnp.float32)
    squares = summed[:, heads * HD : heads * HD + 1] + summed[:, heads * HD + 1 : heads * HD + 2]
    inverse = lax.rsqrt(squares / width + epsilon) * (float(HD) ** (-0.5))
    queries = jnp.concatenate(
        [summed[:, head * HD : (head + 1) * HD] * inverse for head in range(heads)], axis=0
    ).astype(jnp.bfloat16)
    scores = lax.dot_general(
        queries,
        keyval_ref[section, :, :HD],
        (((1,), (1,)), ((), ())),
        preferred_element_type=jnp.float32,
    )
    weighted = jnp.exp(scores) * valid
    weights = (weighted / jnp.sum(weighted, axis=-1, keepdims=True)).astype(jnp.bfloat16)
    context = jnp.dot(weights, keyval_ref[section, :, HD:], preferred_element_type=jnp.float32)
    for head in range(heads):
        part = (context[head * rows : (head + 1) * rows] * live).astype(jnp.bfloat16)
        for target in range(result_ref.shape[0]):
            result_ref[target, :, head * HD : (head + 1) * HD] = part


def attend(place, choice, tiles, lengths, packed, keyval, section, width):
    sources, rows, columns = packed.shape
    keys = keyval.shape[1]
    heads = (columns - LANES) // HD
    return pl.pallas_call(
        functools.partial(attend_kernel, width, section),
        out_shape=jax.ShapeDtypeStruct((sources, rows, heads * HD), jnp.bfloat16),
        in_specs=[IN_SMEM, IN_SMEM, IN_SMEM, IN_SMEM, IN_VMEM, IN_VMEM],
        out_specs=IN_VMEM,
        compiler_params=LIMIT,
        cost_estimate=cost(4 * heads * rows * keys * HD, packed.size * 2, heads * rows * keys),
    )(place, choice, tiles, lengths, packed, keyval)


def assemble_kernel(received_ref, result_ref):
    cores, phases, slots, rows, piece = received_ref.shape
    for phase in range(phases):
        for slot in range(slots):
            for core in range(cores):
                column = (slot * cores + core) * piece
                result_ref[0, phase * rows : (phase + 1) * rows, column : column + piece] = (
                    received_ref[core, phase, slot]
                )


def assemble(received):
    cores, phases, slots, rows, piece = received.shape
    return pl.pallas_call(
        assemble_kernel,
        out_shape=jax.ShapeDtypeStruct((1, phases * rows, slots * cores * piece), received.dtype),
        in_specs=[IN_VMEM],
        out_specs=IN_VMEM,
        compiler_params=LIMIT,
        cost_estimate=cost(0, 4 * received.size),
    )(received)


def bring(first, second):
    phases = lax.axis_size("phase")

    def shift(part, distance):
        return lax.ppermute(part, "phase", [(i, i ^ distance) for i in range(phases)])

    near_first, far_first = shift(first, 1), shift(first, 2)
    near_second, far_second = shift(second, 1), shift(second, 2)
    across = shift(far_first, 1), shift(near_second, 2)
    return first, second, near_first, near_second, far_first, far_second, *across


def exchange(block, axes):
    return lax.all_to_all(block, axes, 0, 0, tiled=True)


def on_device(
    text_rows,
    image_rows,
    tile_counts,
    text_lengths,
    sample_image,
    norm_gain,
    query_weight,
    keyval_weight,
    output_weight,
    cross_gate,
):
    phases, dps, mps = (lax.axis_size(name) for name in ("phase", "dp", "mp"))
    phase_index = lax.axis_index("phase")
    width = norm_gain.shape[1]
    own_rows = text_rows.shape[0]
    part_rows = own_rows // phases
    depth, head_width = query_weight.shape[1:]
    slots = dps // mps
    piece = depth // mps
    context_part = output_weight.shape[1]

    def spread(own_part):
        return lax.all_gather(own_part, "mp", axis=1, tiled=True)

    images = jnp.broadcast_to(image_rows[None], (phases,) + image_rows.shape)
    images = exchange(images, "phase")
    gain = lax.dynamic_slice_in_dim(norm_gain[0], lax.axis_index("dp") * depth, depth, 0)
    middle = depth // 2
    wq = [
        (query_weight[0, rows].astype(jnp.float32) * gain[rows, None]).astype(jnp.bfloat16)
        for rows in (slice(0, middle), slice(middle, depth))
    ]
    wo = output_weight.reshape(context_part, slots, mps, piece).transpose(2, 1, 0, 3)
    wo = wo.reshape(mps, slots * context_part, piece)
    images, wq, wo, text_rows = lax.optimization_barrier((images, wq, wo, text_rows))
    wq = bring(*wq)
    wo = exchange(exchange(wo, "mp").reshape(dps, context_part, piece), "dp")

    samples = [(phase * part_rows) // TXT for phase in range(phases)]
    images = lax.all_gather(images, "mp", axis=2, tiled=True)
    keyval = project_keyval(samples, sample_image, cross_gate, images, keyval_weight[0, :, 0, :])
    keyval, wo = lax.optimization_barrier((keyval, wo))
    keyval = exchange(keyval, "phase")
    middle = dps // 2
    wo = bring(wo[:middle].reshape(-1, piece), wo[middle:].reshape(-1, piece))

    mine = lax.dynamic_slice_in_dim(text_rows, phase_index * part_rows, part_rows, 0)
    mine = spread(mine).reshape(part_rows, dps, depth).transpose(1, 0, 2)
    carried = exchange(mine, "dp").reshape(dps * part_rows, depth)
    own = lax.dynamic_slice_in_dim(carried, lax.axis_index("mp") * piece, piece, 1)

    place = jnp.full((1,), phase_index, jnp.int32)

    later = range(1, phases)
    wq_later, wo_later = arrange(place, wq, later), arrange(place, wo, later)
    packed_width = head_width + LANES
    states = []
    for section in range(phases):
        if section == 0:
            packed = project(query_kernel, place, [carried], wq, 0, packed_width)
        else:
            carried = spread(own)
            weights = [wq_later[section - 1]]
            packed = project(query_kernel, place, [carried], weights, None, packed_width)
        packed = exchange(packed.reshape(dps, part_rows, packed_width), "dp")
        context = attend(
            place, sample_image, tile_counts, text_lengths, packed, keyval, section, width
        )
        context = spread(exchange(context, "dp").reshape(dps * part_rows, head_width))
        if section == 0:
            own = project(output_kernel, place, [context, own], wo, 0, piece)
        else:
            weights = [wo_later[section - 1]]
            own = project(output_kernel, place, [context, own], weights, None, piece)
        states.append(own)
    result = jnp.stack(states).reshape(phases * dps, part_rows, piece)
    result = exchange(result, ("phase", "dp")).reshape(phases, mps, slots, part_rows, piece)
    return assemble(exchange(result.transpose(1, 0, 2, 3, 4), "mp"))


def solution(mesh):
    placed = (
        P("dp", "mp"),
        P("dp", ("phase", "mp"), None),
        P("dp"),
        P("dp"),
        P("dp"),
        P("phase", None),
        P("phase", "dp", "mp"),
        P("phase", None, "mp", None),
        P("phase", "dp", "mp"),
        P("phase"),
    )
    return jax.shard_map(
        on_device, mesh=mesh, in_specs=placed, out_specs=P("phase", "dp", "mp"), check_vma=False
    )
```

```python
import functools

import jax
import jax.numpy as jnp
from jax import lax
from jax.experimental import pallas as pl
from jax.experimental.pallas import tpu as pltpu
from jax.sharding import PartitionSpec as P

HD = 128
HQ_DEV = 4
TROWS = 32
SAMP = 2
TXT = 64
LANES = 128

epsilon = 1e-05
IN_VMEM = pl.BlockSpec(memory_space=pltpu.VMEM)
IN_PLACE = pl.BlockSpec(memory_space=pl.ANY)
IN_SMEM = pl.BlockSpec(memory_space=pltpu.SMEM)
LIMIT = pltpu.CompilerParams(vmem_limit_bytes=24 * 2**20)


def cost(flops, bytes_accessed, transcendentals=0):
    return pl.CostEstimate(
        flops=flops, bytes_accessed=bytes_accessed, transcendentals=transcendentals
    )


def keyval_kernel(samples, choice_ref, gate_ref, images_ref, weight_ref, result_ref, held):
    phases, count = images_ref.shape[:2]
    factor = jnp.tanh(jnp.full((1, HD), gate_ref[0], jnp.float32))
    for image in range(count):
        rows = jnp.concatenate([images_ref[phase, image] for phase in range(phases)], axis=0)
        both = jnp.dot(rows, weight_ref[...], preferred_element_type=jnp.float32)
        held[image, :, :HD] = both[:, :HD].astype(jnp.bfloat16)
        held[image, :, HD:] = (both[:, HD:] * factor).astype(jnp.bfloat16)
    for slot, sample in enumerate(samples):
        result_ref[slot] = held[choice_ref[sample]]


def project_keyval(samples, choice, gate, images, weight):
    phases, count, rows, depth = images.shape
    keys = phases * rows
    return pl.pallas_call(
        functools.partial(keyval_kernel, samples),
        out_shape=jax.ShapeDtypeStruct((len(samples), keys, 2 * HD), jnp.bfloat16),
        in_specs=[IN_SMEM, IN_SMEM, IN_VMEM, IN_VMEM],
        out_specs=IN_VMEM,
        scratch_shapes=[pltpu.VMEM((count, keys, 2 * HD), jnp.bfloat16)],
        compiler_params=LIMIT,
        cost_estimate=cost(4 * count * keys * depth * HD, 2 * images.size + 2 * weight.size),
    )(choice, gate, images, weight)


def start_copy(distance, blocks, target, sems):
    half = target.shape[0] // 2
    for step in range(len(blocks) // 2):

        @pl.when(distance == step)
        def _():
            pltpu.make_async_copy(blocks[2 * step], target.at[:half], sems.at[0]).start()
            pltpu.make_async_copy(blocks[2 * step + 1], target.at[half:], sems.at[1]).start()


def wait_copy(blocks, target, sems):
    half = target.shape[0] // 2
    pltpu.make_async_copy(blocks[0], target.at[:half], sems.at[0]).wait()
    pltpu.make_async_copy(blocks[1], target.at[half:], sems.at[1]).wait()


def arrange_kernel(sections, place_ref, *refs):
    blocks, targets, sems = refs[: -len(sections) - 1], refs[-len(sections) - 1 : -1], refs[-1]
    for step, section in enumerate(sections):
        start_copy(place_ref[0] ^ section, blocks, targets[step], sems.at[step])
    for step in range(len(sections)):
        wait_copy(blocks, targets[step], sems.at[step])


def arrange(place, blocks, sections):
    half, columns = blocks[0].shape
    whole = jax.ShapeDtypeStruct((2 * half, columns), jnp.bfloat16)
    return pl.pallas_call(
        functools.partial(arrange_kernel, sections),
        out_shape=[whole] * len(sections),
        in_specs=[IN_SMEM] + [IN_PLACE] * len(blocks),
        out_specs=[IN_PLACE] * len(sections),
        scratch_shapes=[pltpu.SemaphoreType.DMA((len(sections), 2))],
        compiler_params=LIMIT,
        cost_estimate=cost(0, 8 * half * columns * len(sections)),
    )(place, *blocks)


def query_kernel(section, place_ref, x_ref, *refs):
    if section is None:
        weight_ref, packed_ref = refs
    else:
        *blocks, packed_ref, weight_ref, sems = refs
        start_copy(place_ref[0] ^ section, blocks, weight_ref, sems)
    width = weight_ref.shape[1]
    wide = x_ref[...].astype(jnp.float32)
    squares = jnp.sum(wide * wide, axis=-1, keepdims=True)
    high = squares.astype(jnp.bfloat16).astype(jnp.float32)
    lane = lax.broadcasted_iota(jnp.int32, (x_ref.shape[0], LANES), 1)
    extra = jnp.where(lane == 0, high, jnp.where(lane == 1, squares - high, 0.0))
    packed_ref[:, width:] = extra.astype(jnp.bfloat16)
    if section is not None:
        wait_copy(blocks, weight_ref, sems)
    total = jnp.dot(x_ref[...], weight_ref[...], preferred_element_type=jnp.float32)
    packed_ref[:, :width] = total.astype(jnp.bfloat16)


def output_kernel(section, place_ref, context_ref, own_ref, *refs):
    if section is None:
        weight_ref, result_ref = refs
    else:
        *blocks, result_ref, weight_ref, sems = refs
        start_copy(place_ref[0] ^ section, blocks, weight_ref, sems)
        wait_copy(blocks, weight_ref, sems)
    total = own_ref[...].astype(jnp.float32)
    total += jnp.dot(context_ref[...], weight_ref[...], preferred_element_type=jnp.float32)
    result_ref[...] = total.astype(jnp.bfloat16)


def project(kernel, place, operands, weights, section, columns):
    rows = operands[0].shape[0]
    fetch = section is not None
    depth = weights[0].shape[0] * (2 if fetch else 1)
    width = weights[0].shape[1]
    scratch = [pltpu.VMEM((depth, width), jnp.bfloat16), pltpu.SemaphoreType.DMA((2,))]
    return pl.pallas_call(
        functools.partial(kernel, section),
        out_shape=jax.ShapeDtypeStruct((rows, columns), jnp.bfloat16),
        in_specs=[IN_SMEM]
        + [IN_VMEM] * len(operands)
        + [IN_PLACE if fetch else IN_VMEM] * len(weights),
        out_specs=IN_VMEM,
        scratch_shapes=scratch if fetch else [],
        compiler_params=LIMIT,
        cost_estimate=cost(2 * rows * depth * width, 2 * depth * width),
    )(place, *operands, *weights)


def attend_kernel(
    width, section, place_ref, choice_ref, tiles_ref, length_ref, packed_ref, keyval_ref, result_ref
):
    sources, rows, columns = packed_ref.shape
    heads = (columns - LANES) // HD
    keys = keyval_ref.shape[1]
    first = place_ref[0] * rows
    sample = first // TXT
    key = lax.broadcasted_iota(jnp.int32, (1, keys), 1)
    valid = jnp.where(key < tiles_ref[choice_ref[sample]] * TROWS, 1.0, 0.0)
    position = first - sample * TXT + lax.broadcasted_iota(jnp.int32, (rows, 1), 0)
    live = jnp.where(position < length_ref[sample], 1.0, 0.0)
    summed = packed_ref[0].astype(jnp.float32)
    for source in range(1, sources):
        summed += packed_ref[source].astype(jnp.float32)
    squares = summed[:, heads * HD : heads * HD + 1] + summed[:, heads * HD + 1 : heads * HD + 2]
    inverse = lax.rsqrt(squares / width + epsilon) * (float(HD) ** (-0.5))
    queries = jnp.concatenate(
        [summed[:, head * HD : (head + 1) * HD] * inverse for head in range(heads)], axis=0
    ).astype(jnp.bfloat16)
    scores = lax.dot_general(
        queries,
        keyval_ref[section, :, :HD],
        (((1,), (1,)), ((), ())),
        preferred_element_type=jnp.float32,
    )
    weighted = jnp.exp(scores) * valid
    weights = (weighted / jnp.sum(weighted, axis=-1, keepdims=True)).astype(jnp.bfloat16)
    context = jnp.dot(weights, keyval_ref[section, :, HD:], preferred_element_type=jnp.float32)
    for head in range(heads):
        part = (context[head * rows : (head + 1) * rows] * live).astype(jnp.bfloat16)
        for target in range(result_ref.shape[0]):
            result_ref[target, :, head * HD : (head + 1) * HD] = part


def attend(place, choice, tiles, lengths, packed, keyval, section, width):
    sources, rows, columns = packed.shape
    keys = keyval.shape[1]
    heads = (columns - LANES) // HD
    return pl.pallas_call(
        functools.partial(attend_kernel, width, section),
        out_shape=jax.ShapeDtypeStruct((sources, rows, heads * HD), jnp.bfloat16),
        in_specs=[IN_SMEM, IN_SMEM, IN_SMEM, IN_SMEM, IN_VMEM, IN_VMEM],
        out_specs=IN_VMEM,
        compiler_params=LIMIT,
        cost_estimate=cost(4 * heads * rows * keys * HD, packed.size * 2, heads * rows * keys),
    )(place, choice, tiles, lengths, packed, keyval)


def assemble_kernel(received_ref, result_ref):
    cores, phases, slots, rows, piece = received_ref.shape
    for phase in range(phases):
        for slot in range(slots):
            for core in range(cores):
                column = (slot * cores + core) * piece
                result_ref[0, phase * rows : (phase + 1) * rows, column : column + piece] = (
                    received_ref[core, phase, slot]
                )


def assemble(received):
    cores, phases, slots, rows, piece = received.shape
    return pl.pallas_call(
        assemble_kernel,
        out_shape=jax.ShapeDtypeStruct((1, phases * rows, slots * cores * piece), received.dtype),
        in_specs=[IN_VMEM],
        out_specs=IN_VMEM,
        compiler_params=LIMIT,
        cost_estimate=cost(0, 4 * received.size),
    )(received)


def bring(first, second):
    phases = lax.axis_size("phase")

    def shift(part, distance):
        return lax.ppermute(part, "phase", [(i, i ^ distance) for i in range(phases)])

    near_first, far_first = shift(first, 1), shift(first, 2)
    near_second, far_second = shift(second, 1), shift(second, 2)
    across = shift(far_first, 1), shift(near_second, 2)
    return first, second, near_first, near_second, far_first, far_second, *across


def exchange(block, axes):
    return lax.all_to_all(block, axes, 0, 0, tiled=True)


def on_device(
    text_rows,
    image_rows,
    tile_counts,
    text_lengths,
    sample_image,
    norm_gain,
    query_weight,
    keyval_weight,
    output_weight,
    cross_gate,
):
    phases, dps, mps = (lax.axis_size(name) for name in ("phase", "dp", "mp"))
    phase_index = lax.axis_index("phase")
    width = norm_gain.shape[1]
    own_rows = text_rows.shape[0]
    part_rows = own_rows // phases
    depth, head_width = query_weight.shape[1:]
    slots = dps // mps
    piece = depth // mps
    context_part = output_weight.shape[1]

    def spread(own_part):
        return lax.all_gather(own_part, "mp", axis=1, tiled=True)

    images = jnp.broadcast_to(image_rows[None], (phases,) + image_rows.shape)
    images = exchange(images, "phase")
    gain = lax.dynamic_slice_in_dim(norm_gain[0], lax.axis_index("dp") * depth, depth, 0)
    middle = depth // 2
    wq = [
        (query_weight[0, rows].astype(jnp.float32) * gain[rows, None]).astype(jnp.bfloat16)
        for rows in (slice(0, middle), slice(middle, depth))
    ]
    wo = output_weight.reshape(context_part, slots, mps, piece).transpose(2, 1, 0, 3)
    wo = wo.reshape(mps, slots * context_part, piece)
    images, wq, wo, text_rows = lax.optimization_barrier((images, wq, wo, text_rows))
    wq = bring(*wq)
    wo = exchange(exchange(wo, "mp").reshape(dps, context_part, piece), "dp")

    samples = [(phase * part_rows) // TXT for phase in range(phases)]
    images = lax.all_gather(images, "mp", axis=2, tiled=True)
    keyval = project_keyval(samples, sample_image, cross_gate, images, keyval_weight[0, :, 0, :])
    keyval = exchange(keyval, "phase")

    mine = lax.dynamic_slice_in_dim(text_rows, phase_index * part_rows, part_rows, 0)
    mine = spread(mine).reshape(part_rows, dps, depth).transpose(1, 0, 2)
    carried = exchange(mine, "dp")

    keyval, carried, wo = lax.optimization_barrier((keyval, carried, wo))
    middle = dps // 2
    wo = bring(wo[:middle].reshape(-1, piece), wo[middle:].reshape(-1, piece))
    carried = carried.reshape(dps * part_rows, depth)
    own = lax.dynamic_slice_in_dim(carried, lax.axis_index("mp") * piece, piece, 1)

    place = jnp.full((1,), phase_index, jnp.int32)

    later = range(1, phases)
    wq_later, wo_later = arrange(place, wq, later), arrange(place, wo, later)
    packed_width = head_width + LANES
    states = []
    for section in range(phases):
        if section == 0:
            packed = project(query_kernel, place, [carried], wq, 0, packed_width)
        else:
            carried = spread(own)
            weights = [wq_later[section - 1]]
            packed = project(query_kernel, place, [carried], weights, None, packed_width)
        packed = exchange(packed.reshape(dps, part_rows, packed_width), "dp")
        context = attend(
            place, sample_image, tile_counts, text_lengths, packed, keyval, section, width
        )
        context = spread(exchange(context, "dp").reshape(dps * part_rows, head_width))
        if section == 0:
            own = project(output_kernel, place, [context, own], wo, 0, piece)
        else:
            weights = [wo_later[section - 1]]
            own = project(output_kernel, place, [context, own], weights, None, piece)
        states.append(own)
    result = jnp.stack(states).reshape(phases * dps, part_rows, piece)
    result = exchange(result, ("phase", "dp")).reshape(phases, mps, slots, part_rows, piece)
    return assemble(exchange(result.transpose(1, 0, 2, 3, 4), "mp"))


def solution(mesh):
    placed = (
        P("dp", "mp"),
        P("dp", ("phase", "mp"), None),
        P("dp"),
        P("dp"),
        P("dp"),
        P("phase", None),
        P("phase", "dp", "mp"),
        P("phase", None, "mp", None),
        P("phase", "dp", "mp"),
        P("phase"),
    )
    return jax.shard_map(
        on_device, mesh=mesh, in_specs=placed, out_specs=P("phase", "dp", "mp"), check_vma=False
    )
```

```python
import functools

import jax
import jax.numpy as jnp
from jax import lax
from jax.experimental import pallas as pl
from jax.experimental.pallas import tpu as pltpu
from jax.sharding import PartitionSpec as P

HD = 128
HQ_DEV = 4
TROWS = 32
SAMP = 2
TXT = 64
LANES = 128

epsilon = 1e-05
IN_VMEM = pl.BlockSpec(memory_space=pltpu.VMEM)
IN_PLACE = pl.BlockSpec(memory_space=pl.ANY)
IN_SMEM = pl.BlockSpec(memory_space=pltpu.SMEM)
LIMIT = pltpu.CompilerParams(vmem_limit_bytes=24 * 2**20)


def cost(flops, bytes_accessed, transcendentals=0):
    return pl.CostEstimate(
        flops=flops, bytes_accessed=bytes_accessed, transcendentals=transcendentals
    )


def keyval_kernel(samples, choice_ref, gate_ref, images_ref, weight_ref, result_ref, held):
    phases, count = images_ref.shape[:2]
    factor = jnp.tanh(jnp.full((1, HD), gate_ref[0], jnp.float32))
    for image in range(count):
        rows = jnp.concatenate([images_ref[phase, image] for phase in range(phases)], axis=0)
        both = jnp.dot(rows, weight_ref[...], preferred_element_type=jnp.float32)
        held[image, :, :HD] = both[:, :HD].astype(jnp.bfloat16)
        held[image, :, HD:] = (both[:, HD:] * factor).astype(jnp.bfloat16)
    for slot, sample in enumerate(samples):
        result_ref[slot] = held[choice_ref[sample]]


def project_keyval(samples, choice, gate, images, weight):
    phases, count, rows, depth = images.shape
    keys = phases * rows
    return pl.pallas_call(
        functools.partial(keyval_kernel, samples),
        out_shape=jax.ShapeDtypeStruct((len(samples), keys, 2 * HD), jnp.bfloat16),
        in_specs=[IN_SMEM, IN_SMEM, IN_VMEM, IN_VMEM],
        out_specs=IN_VMEM,
        scratch_shapes=[pltpu.VMEM((count, keys, 2 * HD), jnp.bfloat16)],
        compiler_params=LIMIT,
        cost_estimate=cost(4 * count * keys * depth * HD, 2 * images.size + 2 * weight.size),
    )(choice, gate, images, weight)


def start_copy(distance, blocks, target, sems):
    half = target.shape[0] // 2
    for step in range(len(blocks) // 2):

        @pl.when(distance == step)
        def _():
            pltpu.make_async_copy(blocks[2 * step], target.at[:half], sems.at[0]).start()
            pltpu.make_async_copy(blocks[2 * step + 1], target.at[half:], sems.at[1]).start()


def wait_copy(blocks, target, sems):
    half = target.shape[0] // 2
    pltpu.make_async_copy(blocks[0], target.at[:half], sems.at[0]).wait()
    pltpu.make_async_copy(blocks[1], target.at[half:], sems.at[1]).wait()


def arrange_kernel(sections, place_ref, *refs):
    blocks, targets, sems = refs[: -len(sections) - 1], refs[-len(sections) - 1 : -1], refs[-1]
    for step, section in enumerate(sections):
        start_copy(place_ref[0] ^ section, blocks, targets[step], sems.at[step])
    for step in range(len(sections)):
        wait_copy(blocks, targets[step], sems.at[step])


def arrange(place, blocks, sections):
    half, columns = blocks[0].shape
    whole = jax.ShapeDtypeStruct((2 * half, columns), jnp.bfloat16)
    return pl.pallas_call(
        functools.partial(arrange_kernel, sections),
        out_shape=[whole] * len(sections),
        in_specs=[IN_SMEM] + [IN_PLACE] * len(blocks),
        out_specs=[IN_PLACE] * len(sections),
        scratch_shapes=[pltpu.SemaphoreType.DMA((len(sections), 2))],
        compiler_params=LIMIT,
        cost_estimate=cost(0, 8 * half * columns * len(sections)),
    )(place, *blocks)


def query_kernel(section, place_ref, x_ref, *refs):
    if section is None:
        weight_ref, packed_ref = refs
    else:
        *blocks, packed_ref, weight_ref, sems = refs
        start_copy(place_ref[0] ^ section, blocks, weight_ref, sems)
    width = weight_ref.shape[1]
    wide = x_ref[...].astype(jnp.float32)
    squares = jnp.sum(wide * wide, axis=-1, keepdims=True)
    high = squares.astype(jnp.bfloat16).astype(jnp.float32)
    lane = lax.broadcasted_iota(jnp.int32, (x_ref.shape[0], LANES), 1)
    extra = jnp.where(lane == 0, high, jnp.where(lane == 1, squares - high, 0.0))
    packed_ref[:, width:] = extra.astype(jnp.bfloat16)
    if section is not None:
        wait_copy(blocks, weight_ref, sems)
    total = jnp.dot(x_ref[...], weight_ref[...], preferred_element_type=jnp.float32)
    packed_ref[:, :width] = total.astype(jnp.bfloat16)


def output_kernel(section, place_ref, context_ref, own_ref, *refs):
    if section is None:
        weight_ref, result_ref = refs
    else:
        *blocks, result_ref, weight_ref, sems = refs
        start_copy(place_ref[0] ^ section, blocks, weight_ref, sems)
        wait_copy(blocks, weight_ref, sems)
    total = own_ref[...].astype(jnp.float32)
    total += jnp.dot(context_ref[...], weight_ref[...], preferred_element_type=jnp.float32)
    result_ref[...] = total.astype(jnp.bfloat16)


def project(kernel, place, operands, weights, section, columns):
    rows = operands[0].shape[0]
    fetch = section is not None
    depth = weights[0].shape[0] * (2 if fetch else 1)
    width = weights[0].shape[1]
    scratch = [pltpu.VMEM((depth, width), jnp.bfloat16), pltpu.SemaphoreType.DMA((2,))]
    return pl.pallas_call(
        functools.partial(kernel, section),
        out_shape=jax.ShapeDtypeStruct((rows, columns), jnp.bfloat16),
        in_specs=[IN_SMEM]
        + [IN_VMEM] * len(operands)
        + [IN_PLACE if fetch else IN_VMEM] * len(weights),
        out_specs=IN_VMEM,
        scratch_shapes=scratch if fetch else [],
        compiler_params=LIMIT,
        cost_estimate=cost(2 * rows * depth * width, 2 * depth * width),
    )(place, *operands, *weights)


def attend_kernel(
    width, section, place_ref, choice_ref, tiles_ref, length_ref, packed_ref, keyval_ref, result_ref
):
    sources, rows, columns = packed_ref.shape
    heads = (columns - LANES) // HD
    keys = keyval_ref.shape[1]
    first = place_ref[0] * rows
    sample = first // TXT
    key = lax.broadcasted_iota(jnp.int32, (1, keys), 1)
    valid = jnp.where(key < tiles_ref[choice_ref[sample]] * TROWS, 1.0, 0.0)
    position = first - sample * TXT + lax.broadcasted_iota(jnp.int32, (rows, 1), 0)
    live = jnp.where(position < length_ref[sample], 1.0, 0.0)
    summed = packed_ref[0].astype(jnp.float32)
    for source in range(1, sources):
        summed += packed_ref[source].astype(jnp.float32)
    squares = summed[:, heads * HD : heads * HD + 1] + summed[:, heads * HD + 1 : heads * HD + 2]
    inverse = lax.rsqrt(squares / width + epsilon) * (float(HD) ** (-0.5))
    queries = jnp.concatenate(
        [summed[:, head * HD : (head + 1) * HD] * inverse for head in range(heads)], axis=0
    ).astype(jnp.bfloat16)
    scores = lax.dot_general(
        queries,
        keyval_ref[section, :, :HD],
        (((1,), (1,)), ((), ())),
        preferred_element_type=jnp.float32,
    )
    weighted = jnp.exp(scores) * valid
    weights = (weighted / jnp.sum(weighted, axis=-1, keepdims=True)).astype(jnp.bfloat16)
    context = jnp.dot(weights, keyval_ref[section, :, HD:], preferred_element_type=jnp.float32)
    for head in range(heads):
        part = (context[head * rows : (head + 1) * rows] * live).astype(jnp.bfloat16)
        for target in range(result_ref.shape[0]):
            result_ref[target, :, head * HD : (head + 1) * HD] = part


def attend(place, choice, tiles, lengths, packed, keyval, section, width):
    sources, rows, columns = packed.shape
    keys = keyval.shape[1]
    heads = (columns - LANES) // HD
    return pl.pallas_call(
        functools.partial(attend_kernel, width, section),
        out_shape=jax.ShapeDtypeStruct((sources, rows, heads * HD), jnp.bfloat16),
        in_specs=[IN_SMEM, IN_SMEM, IN_SMEM, IN_SMEM, IN_VMEM, IN_VMEM],
        out_specs=IN_VMEM,
        compiler_params=LIMIT,
        cost_estimate=cost(4 * heads * rows * keys * HD, packed.size * 2, heads * rows * keys),
    )(place, choice, tiles, lengths, packed, keyval)


def assemble_kernel(received_ref, result_ref):
    cores, phases, slots, rows, piece = received_ref.shape
    for phase in range(phases):
        for slot in range(slots):
            for core in range(cores):
                column = (slot * cores + core) * piece
                result_ref[0, phase * rows : (phase + 1) * rows, column : column + piece] = (
                    received_ref[core, phase, slot]
                )


def assemble(received):
    cores, phases, slots, rows, piece = received.shape
    return pl.pallas_call(
        assemble_kernel,
        out_shape=jax.ShapeDtypeStruct((1, phases * rows, slots * cores * piece), received.dtype),
        in_specs=[IN_VMEM],
        out_specs=IN_VMEM,
        compiler_params=LIMIT,
        cost_estimate=cost(0, 4 * received.size),
    )(received)


def bring(first, second):
    phases = lax.axis_size("phase")

    def shift(part, distance):
        return lax.ppermute(part, "phase", [(i, i ^ distance) for i in range(phases)])

    near_first, far_first = shift(first, 1), shift(first, 2)
    near_second, far_second = shift(second, 1), shift(second, 2)
    across = shift(far_first, 1), shift(near_second, 2)
    return first, second, near_first, near_second, far_first, far_second, *across


def exchange(block, axes):
    return lax.all_to_all(block, axes, 0, 0, tiled=True)


def on_device(
    text_rows,
    image_rows,
    tile_counts,
    text_lengths,
    sample_image,
    norm_gain,
    query_weight,
    keyval_weight,
    output_weight,
    cross_gate,
):
    phases, dps, mps = (lax.axis_size(name) for name in ("phase", "dp", "mp"))
    phase_index = lax.axis_index("phase")
    width = norm_gain.shape[1]
    own_rows = text_rows.shape[0]
    part_rows = own_rows // phases
    depth, head_width = query_weight.shape[1:]
    slots = dps // mps
    piece = depth // mps
    context_part = output_weight.shape[1]

    def spread(own_part):
        return lax.all_gather(own_part, "mp", axis=1, tiled=True)

    images = jnp.broadcast_to(image_rows[None], (phases,) + image_rows.shape)
    images = exchange(images, "phase")
    gain = lax.dynamic_slice_in_dim(norm_gain[0], lax.axis_index("dp") * depth, depth, 0)
    middle = depth // 2
    wq = [
        (query_weight[0, rows].astype(jnp.float32) * gain[rows, None]).astype(jnp.bfloat16)
        for rows in (slice(0, middle), slice(middle, depth))
    ]
    wo = output_weight.reshape(context_part, slots, mps, piece).transpose(2, 1, 0, 3)
    wo = wo.reshape(mps, slots * context_part, piece)
    images, wq, wo, text_rows = lax.optimization_barrier((images, wq, wo, text_rows))
    wq = bring(*wq)
    wo = exchange(exchange(wo, "mp").reshape(dps, context_part, piece), "dp")

    samples = [(phase * part_rows) // TXT for phase in range(phases)]
    images = lax.all_gather(images, "mp", axis=2, tiled=True)
    keyval = project_keyval(samples, sample_image, cross_gate, images, keyval_weight[0, :, 0, :])
    keyval = exchange(keyval, "phase")
    middle = dps // 2
    wo = bring(wo[:middle].reshape(-1, piece), wo[middle:].reshape(-1, piece))

    mine = lax.dynamic_slice_in_dim(text_rows, phase_index * part_rows, part_rows, 0)
    mine = spread(mine).reshape(part_rows, dps, depth).transpose(1, 0, 2)
    carried = exchange(mine, "dp").reshape(dps * part_rows, depth)
    own = lax.dynamic_slice_in_dim(carried, lax.axis_index("mp") * piece, piece, 1)

    place = jnp.full((1,), phase_index, jnp.int32)

    later = range(1, phases)
    wq_later, wo_later = arrange(place, wq, later), arrange(place, wo, later)
    packed_width = head_width + LANES
    states = []
    for section in range(phases):
        if section == 0:
            packed = project(query_kernel, place, [carried], wq, 0, packed_width)
        else:
            carried = spread(own)
            weights = [wq_later[section - 1]]
            packed = project(query_kernel, place, [carried], weights, None, packed_width)
        packed = exchange(packed.reshape(dps, part_rows, packed_width), "dp")
        context = attend(
            place, sample_image, tile_counts, text_lengths, packed, keyval, section, width
        )
        context = spread(exchange(context, "dp").reshape(dps * part_rows, head_width))
        if section == 0:
            own = project(output_kernel, place, [context, own], wo, 0, piece)
        else:
            weights = [wo_later[section - 1]]
            own = project(output_kernel, place, [context, own], weights, None, piece)
        states.append(own)
    result = jnp.stack(states).reshape(phases * dps, part_rows, piece)
    result = exchange(result, ("phase", "dp")).reshape(phases, mps, slots, part_rows, piece)
    return assemble(exchange(result.transpose(1, 0, 2, 3, 4), "mp"))


def solution(mesh):
    placed = (
        P("dp", "mp"),
        P("dp", ("phase", "mp"), None),
        P("dp"),
        P("dp"),
        P("dp"),
        P("phase", None),
        P("phase", "dp", "mp"),
        P("phase", None, "mp", None),
        P("phase", "dp", "mp"),
        P("phase"),
    )
    return jax.shard_map(
        on_device, mesh=mesh, in_specs=placed, out_specs=P("phase", "dp", "mp"), check_vma=False
    )
```

```python
import functools

import jax
import jax.numpy as jnp
from jax import lax
from jax.experimental import pallas as pl
from jax.experimental.pallas import tpu as pltpu
from jax.sharding import PartitionSpec as P

HD = 128
HQ_DEV = 4
TROWS = 32
SAMP = 2
TXT = 64
LANES = 128

epsilon = 1e-05
IN_VMEM = pl.BlockSpec(memory_space=pltpu.VMEM)
IN_PLACE = pl.BlockSpec(memory_space=pl.ANY)
IN_SMEM = pl.BlockSpec(memory_space=pltpu.SMEM)
LIMIT = pltpu.CompilerParams(vmem_limit_bytes=24 * 2**20)


def cost(flops, bytes_accessed, transcendentals=0):
    return pl.CostEstimate(
        flops=flops, bytes_accessed=bytes_accessed, transcendentals=transcendentals
    )


def keyval_kernel(part_rows, place_ref, choice_ref, gate_ref, images_ref, weight_ref, *refs):
    *result_refs, held = refs
    phases, count = images_ref.shape[:2]
    factor = jnp.tanh(jnp.full((1, HD), gate_ref[0], jnp.float32))
    for image in range(count):
        rows = jnp.concatenate([images_ref[phase, image] for phase in range(phases)], axis=0)
        both = jnp.dot(rows, weight_ref[...], preferred_element_type=jnp.float32)
        held[image, :, :HD] = both[:, :HD].astype(jnp.bfloat16)
        held[image, :, HD:] = (both[:, HD:] * factor).astype(jnp.bfloat16)
    for distance, result_ref in enumerate(result_refs):
        sample = (place_ref[0] ^ distance) * part_rows // TXT
        result_ref[...] = held[choice_ref[sample]]


def project_keyval(part_rows, place, choice, gate, images, weight):
    phases, count, rows, depth = images.shape
    keys = phases * rows
    block = jax.ShapeDtypeStruct((keys, 2 * HD), jnp.bfloat16)
    return pl.pallas_call(
        functools.partial(keyval_kernel, part_rows),
        out_shape=[block] * phases,
        in_specs=[IN_SMEM, IN_SMEM, IN_SMEM, IN_VMEM, IN_VMEM],
        out_specs=[IN_VMEM] * phases,
        scratch_shapes=[pltpu.VMEM((count, keys, 2 * HD), jnp.bfloat16)],
        compiler_params=LIMIT,
        cost_estimate=cost(4 * count * keys * depth * HD, 2 * images.size + 2 * weight.size),
    )(place, choice, gate, images, weight)


def start_copy(distance, blocks, target, sems):
    half = target.shape[0] // 2
    for step in range(len(blocks) // 2):

        @pl.when(distance == step)
        def _():
            pltpu.make_async_copy(blocks[2 * step], target.at[:half], sems.at[0]).start()
            pltpu.make_async_copy(blocks[2 * step + 1], target.at[half:], sems.at[1]).start()


def wait_copy(blocks, target, sems):
    half = target.shape[0] // 2
    pltpu.make_async_copy(blocks[0], target.at[:half], sems.at[0]).wait()
    pltpu.make_async_copy(blocks[1], target.at[half:], sems.at[1]).wait()


def arrange_kernel(sections, place_ref, *refs):
    blocks, targets, sems = refs[: -len(sections) - 1], refs[-len(sections) - 1 : -1], refs[-1]
    for step, section in enumerate(sections):
        start_copy(place_ref[0] ^ section, blocks, targets[step], sems.at[step])
    for step in range(len(sections)):
        wait_copy(blocks, targets[step], sems.at[step])


def arrange(place, blocks, sections):
    half, columns = blocks[0].shape
    whole = jax.ShapeDtypeStruct((2 * half, columns), jnp.bfloat16)
    return pl.pallas_call(
        functools.partial(arrange_kernel, sections),
        out_shape=[whole] * len(sections),
        in_specs=[IN_SMEM] + [IN_PLACE] * len(blocks),
        out_specs=[IN_PLACE] * len(sections),
        scratch_shapes=[pltpu.SemaphoreType.DMA((len(sections), 2))],
        compiler_params=LIMIT,
        cost_estimate=cost(0, 8 * half * columns * len(sections)),
    )(place, *blocks)


def query_kernel(section, place_ref, x_ref, *refs):
    if section is None:
        weight_ref, packed_ref = refs
    else:
        *blocks, packed_ref, weight_ref, sems = refs
        start_copy(place_ref[0] ^ section, blocks, weight_ref, sems)
    width = weight_ref.shape[1]
    wide = x_ref[...].astype(jnp.float32)
    squares = jnp.sum(wide * wide, axis=-1, keepdims=True)
    high = squares.astype(jnp.bfloat16).astype(jnp.float32)
    lane = lax.broadcasted_iota(jnp.int32, (x_ref.shape[0], LANES), 1)
    extra = jnp.where(lane == 0, high, jnp.where(lane == 1, squares - high, 0.0))
    packed_ref[:, width:] = extra.astype(jnp.bfloat16)
    if section is not None:
        wait_copy(blocks, weight_ref, sems)
    total = jnp.dot(x_ref[...], weight_ref[...], preferred_element_type=jnp.float32)
    packed_ref[:, :width] = total.astype(jnp.bfloat16)


def output_kernel(section, place_ref, context_ref, own_ref, *refs):
    if section is None:
        weight_ref, result_ref = refs
    else:
        *blocks, result_ref, weight_ref, sems = refs
        start_copy(place_ref[0] ^ section, blocks, weight_ref, sems)
        wait_copy(blocks, weight_ref, sems)
    total = own_ref[...].astype(jnp.float32)
    total += jnp.dot(context_ref[...], weight_ref[...], preferred_element_type=jnp.float32)
    result_ref[...] = total.astype(jnp.bfloat16)


def project(kernel, place, operands, weights, section, columns):
    rows = operands[0].shape[0]
    fetch = section is not None
    depth = weights[0].shape[0] * (2 if fetch else 1)
    width = weights[0].shape[1]
    scratch = [pltpu.VMEM((depth, width), jnp.bfloat16), pltpu.SemaphoreType.DMA((2,))]
    return pl.pallas_call(
        functools.partial(kernel, section),
        out_shape=jax.ShapeDtypeStruct((rows, columns), jnp.bfloat16),
        in_specs=[IN_SMEM]
        + [IN_VMEM] * len(operands)
        + [IN_PLACE if fetch else IN_VMEM] * len(weights),
        out_specs=IN_VMEM,
        scratch_shapes=scratch if fetch else [],
        compiler_params=LIMIT,
        cost_estimate=cost(2 * rows * depth * width, 2 * depth * width),
    )(place, *operands, *weights)


def attend_kernel(width, section, place_ref, choice_ref, tiles_ref, length_ref, packed_ref, *refs):
    *blocks, result_ref, held = refs
    for distance, block_ref in enumerate(blocks):

        @pl.when(place_ref[0] ^ section == distance)
        def _():
            held[...] = block_ref[...]

    sources, rows, columns = packed_ref.shape
    heads = (columns - LANES) // HD
    keys = held.shape[0]
    first = place_ref[0] * rows
    sample = first // TXT
    key = lax.broadcasted_iota(jnp.int32, (1, keys), 1)
    valid = jnp.where(key < tiles_ref[choice_ref[sample]] * TROWS, 1.0, 0.0)
    position = first - sample * TXT + lax.broadcasted_iota(jnp.int32, (rows, 1), 0)
    live = jnp.where(position < length_ref[sample], 1.0, 0.0)
    summed = packed_ref[0].astype(jnp.float32)
    for source in range(1, sources):
        summed += packed_ref[source].astype(jnp.float32)
    squares = summed[:, heads * HD : heads * HD + 1] + summed[:, heads * HD + 1 : heads * HD + 2]
    inverse = lax.rsqrt(squares / width + epsilon) * (float(HD) ** (-0.5))
    queries = jnp.concatenate(
        [summed[:, head * HD : (head + 1) * HD] * inverse for head in range(heads)], axis=0
    ).astype(jnp.bfloat16)
    scores = lax.dot_general(
        queries,
        held[:, :HD],
        (((1,), (1,)), ((), ())),
        preferred_element_type=jnp.float32,
    )
    weighted = jnp.exp(scores) * valid
    weights = (weighted / jnp.sum(weighted, axis=-1, keepdims=True)).astype(jnp.bfloat16)
    context = jnp.dot(weights, held[:, HD:], preferred_element_type=jnp.float32)
    for head in range(heads):
        part = (context[head * rows : (head + 1) * rows] * live).astype(jnp.bfloat16)
        for target in range(result_ref.shape[0]):
            result_ref[target, :, head * HD : (head + 1) * HD] = part


def attend(place, choice, tiles, lengths, packed, keyval, section, width):
    sources, rows, columns = packed.shape
    keys = keyval[0].shape[0]
    heads = (columns - LANES) // HD
    return pl.pallas_call(
        functools.partial(attend_kernel, width, section),
        out_shape=jax.ShapeDtypeStruct((sources, rows, heads * HD), jnp.bfloat16),
        in_specs=[IN_SMEM] * 4 + [IN_VMEM] * (1 + len(keyval)),
        out_specs=IN_VMEM,
        scratch_shapes=[pltpu.VMEM(keyval[0].shape, jnp.bfloat16)],
        compiler_params=LIMIT,
        cost_estimate=cost(4 * heads * rows * keys * HD, packed.size * 2, heads * rows * keys),
    )(place, choice, tiles, lengths, packed, *keyval)


def assemble_kernel(received_ref, result_ref):
    cores, phases, slots, rows, piece = received_ref.shape
    for phase in range(phases):
        for slot in range(slots):
            for core in range(cores):
                column = (slot * cores + core) * piece
                result_ref[0, phase * rows : (phase + 1) * rows, column : column + piece] = (
                    received_ref[core, phase, slot]
                )


def assemble(received):
    cores, phases, slots, rows, piece = received.shape
    return pl.pallas_call(
        assemble_kernel,
        out_shape=jax.ShapeDtypeStruct((1, phases * rows, slots * cores * piece), received.dtype),
        in_specs=[IN_VMEM],
        out_specs=IN_VMEM,
        compiler_params=LIMIT,
        cost_estimate=cost(0, 4 * received.size),
    )(received)


def shift(part, distance):
    phases = lax.axis_size("phase")
    return lax.ppermute(part, "phase", [(i, i ^ distance) for i in range(phases)])


def bring(first, second):
    near_first, far_first = shift(first, 1), shift(first, 2)
    near_second, far_second = shift(second, 1), shift(second, 2)
    across = shift(far_first, 1), shift(near_second, 2)
    return first, second, near_first, near_second, far_first, far_second, *across


def exchange(block, axes):
    return lax.all_to_all(block, axes, 0, 0, tiled=True)


def on_device(
    text_rows,
    image_rows,
    tile_counts,
    text_lengths,
    sample_image,
    norm_gain,
    query_weight,
    keyval_weight,
    output_weight,
    cross_gate,
):
    phases, dps, mps = (lax.axis_size(name) for name in ("phase", "dp", "mp"))
    phase_index = lax.axis_index("phase")
    width = norm_gain.shape[1]
    own_rows = text_rows.shape[0]
    part_rows = own_rows // phases
    depth, head_width = query_weight.shape[1:]
    slots = dps // mps
    piece = depth // mps
    context_part = output_weight.shape[1]

    def spread(own_part):
        return lax.all_gather(own_part, "mp", axis=1, tiled=True)

    images = jnp.broadcast_to(image_rows[None], (phases,) + image_rows.shape)
    images = exchange(images, "phase")
    gain = lax.dynamic_slice_in_dim(norm_gain[0], lax.axis_index("dp") * depth, depth, 0)
    middle = depth // 2
    wq = [
        (query_weight[0, rows].astype(jnp.float32) * gain[rows, None]).astype(jnp.bfloat16)
        for rows in (slice(0, middle), slice(middle, depth))
    ]
    wo = output_weight.reshape(context_part, slots, mps, piece).transpose(2, 1, 0, 3)
    wo = wo.reshape(mps, slots * context_part, piece)
    images, wq, wo, text_rows = lax.optimization_barrier((images, wq, wo, text_rows))
    wq = bring(*wq)
    wo = exchange(exchange(wo, "mp").reshape(dps, context_part, piece), "dp")

    place = jnp.full((1,), phase_index, jnp.int32)
    images = lax.all_gather(images, "mp", axis=2, tiled=True)
    keyval = project_keyval(
        part_rows, place, sample_image, cross_gate, images, keyval_weight[0, :, 0, :]
    )
    wo, _ = lax.optimization_barrier((wo, keyval))
    keyval = [shift(keyval[k], k) if k else keyval[k] for k in range(phases)]
    middle = dps // 2
    wo = bring(wo[:middle].reshape(-1, piece), wo[middle:].reshape(-1, piece))

    mine = lax.dynamic_slice_in_dim(text_rows, phase_index * part_rows, part_rows, 0)
    mine = spread(mine).reshape(part_rows, dps, depth).transpose(1, 0, 2)
    carried = exchange(mine, "dp").reshape(dps * part_rows, depth)
    own = lax.dynamic_slice_in_dim(carried, lax.axis_index("mp") * piece, piece, 1)

    later = range(1, phases)
    wq_later, wo_later = arrange(place, wq, later), arrange(place, wo, later)
    packed_width = head_width + LANES
    states = []
    for section in range(phases):
        if section == 0:
            packed = project(query_kernel, place, [carried], wq, 0, packed_width)
        else:
            carried = spread(own)
            weights = [wq_later[section - 1]]
            packed = project(query_kernel, place, [carried], weights, None, packed_width)
        packed = exchange(packed.reshape(dps, part_rows, packed_width), "dp")
        context = attend(
            place, sample_image, tile_counts, text_lengths, packed, keyval, section, width
        )
        context = spread(exchange(context, "dp").reshape(dps * part_rows, head_width))
        if section == 0:
            own = project(output_kernel, place, [context, own], wo, 0, piece)
        else:
            weights = [wo_later[section - 1]]
            own = project(output_kernel, place, [context, own], weights, None, piece)
        states.append(own)
    result = jnp.stack(states).reshape(phases * dps, part_rows, piece)
    result = exchange(result, ("phase", "dp")).reshape(phases, mps, slots, part_rows, piece)
    return assemble(exchange(result.transpose(1, 0, 2, 3, 4), "mp"))


def solution(mesh):
    placed = (
        P("dp", "mp"),
        P("dp", ("phase", "mp"), None),
        P("dp"),
        P("dp"),
        P("dp"),
        P("phase", None),
        P("phase", "dp", "mp"),
        P("phase", None, "mp", None),
        P("phase", "dp", "mp"),
        P("phase"),
    )
    return jax.shard_map(
        on_device, mesh=mesh, in_specs=placed, out_specs=P("phase", "dp", "mp"), check_vma=False
    )
```

```python
import functools

import jax
import jax.numpy as jnp
from jax import lax
from jax.experimental import pallas as pl
from jax.experimental.pallas import tpu as pltpu
from jax.sharding import PartitionSpec as P

HD = 128
HQ_DEV = 4
TROWS = 32
SAMP = 2
TXT = 64
LANES = 128

epsilon = 1e-05
IN_VMEM = pl.BlockSpec(memory_space=pltpu.VMEM)
IN_PLACE = pl.BlockSpec(memory_space=pl.ANY)
IN_SMEM = pl.BlockSpec(memory_space=pltpu.SMEM)
LIMIT = pltpu.CompilerParams(vmem_limit_bytes=24 * 2**20)


def cost(flops, bytes_accessed, transcendentals=0):
    return pl.CostEstimate(
        flops=flops, bytes_accessed=bytes_accessed, transcendentals=transcendentals
    )


def keyval_kernel(part_rows, place_ref, choice_ref, gate_ref, images_ref, weight_ref, *refs):
    *result_refs, held = refs
    phases, count = images_ref.shape[:2]
    factor = jnp.tanh(jnp.full((1, HD), gate_ref[0], jnp.float32))
    for image in range(count):
        rows = jnp.concatenate([images_ref[phase, image] for phase in range(phases)], axis=0)
        both = jnp.dot(rows, weight_ref[...], preferred_element_type=jnp.float32)
        held[image, :, :HD] = both[:, :HD].astype(jnp.bfloat16)
        held[image, :, HD:] = (both[:, HD:] * factor).astype(jnp.bfloat16)
    for distance, result_ref in enumerate(result_refs):
        sample = (place_ref[0] ^ distance) * part_rows // TXT
        result_ref[...] = held[choice_ref[sample]]


def project_keyval(part_rows, place, choice, gate, images, weight):
    phases, count, rows, depth = images.shape
    keys = phases * rows
    block = jax.ShapeDtypeStruct((keys, 2 * HD), jnp.bfloat16)
    return pl.pallas_call(
        functools.partial(keyval_kernel, part_rows),
        out_shape=[block] * phases,
        in_specs=[IN_SMEM, IN_SMEM, IN_SMEM, IN_VMEM, IN_VMEM],
        out_specs=[IN_VMEM] * phases,
        scratch_shapes=[pltpu.VMEM((count, keys, 2 * HD), jnp.bfloat16)],
        compiler_params=LIMIT,
        cost_estimate=cost(4 * count * keys * depth * HD, 2 * images.size + 2 * weight.size),
    )(place, choice, gate, images, weight)


def start_copy(distance, blocks, target, sems):
    half = target.shape[0] // 2
    for step in range(len(blocks) // 2):

        @pl.when(distance == step)
        def _():
            pltpu.make_async_copy(blocks[2 * step], target.at[:half], sems.at[0]).start()
            pltpu.make_async_copy(blocks[2 * step + 1], target.at[half:], sems.at[1]).start()


def wait_copy(blocks, target, sems):
    half = target.shape[0] // 2
    pltpu.make_async_copy(blocks[0], target.at[:half], sems.at[0]).wait()
    pltpu.make_async_copy(blocks[1], target.at[half:], sems.at[1]).wait()


def arrange_kernel(sections, place_ref, *refs):
    blocks, targets, sems = refs[: -len(sections) - 1], refs[-len(sections) - 1 : -1], refs[-1]
    for step, section in enumerate(sections):
        start_copy(place_ref[0] ^ section, blocks, targets[step], sems.at[step])
    for step in range(len(sections)):
        wait_copy(blocks, targets[step], sems.at[step])


def arrange(place, blocks, sections):
    half, columns = blocks[0].shape
    whole = jax.ShapeDtypeStruct((2 * half, columns), jnp.bfloat16)
    return pl.pallas_call(
        functools.partial(arrange_kernel, sections),
        out_shape=[whole] * len(sections),
        in_specs=[IN_SMEM] + [IN_PLACE] * len(blocks),
        out_specs=[IN_PLACE] * len(sections),
        scratch_shapes=[pltpu.SemaphoreType.DMA((len(sections), 2))],
        compiler_params=LIMIT,
        cost_estimate=cost(0, 8 * half * columns * len(sections)),
    )(place, *blocks)


def query_kernel(section, place_ref, x_ref, *refs):
    if section is None:
        weight_ref, packed_ref = refs
    else:
        *blocks, packed_ref, weight_ref, sems = refs
        start_copy(place_ref[0] ^ section, blocks, weight_ref, sems)
    width = weight_ref.shape[1]
    wide = x_ref[...].astype(jnp.float32)
    squares = jnp.sum(wide * wide, axis=-1, keepdims=True)
    high = squares.astype(jnp.bfloat16).astype(jnp.float32)
    lane = lax.broadcasted_iota(jnp.int32, (x_ref.shape[0], LANES), 1)
    extra = jnp.where(lane == 0, high, jnp.where(lane == 1, squares - high, 0.0))
    packed_ref[:, width:] = extra.astype(jnp.bfloat16)
    if section is not None:
        wait_copy(blocks, weight_ref, sems)
    total = jnp.dot(x_ref[...], weight_ref[...], preferred_element_type=jnp.float32)
    packed_ref[:, :width] = total.astype(jnp.bfloat16)


def output_kernel(section, place_ref, context_ref, own_ref, *refs):
    if section is None:
        weight_ref, result_ref = refs
    else:
        *blocks, result_ref, weight_ref, sems = refs
        start_copy(place_ref[0] ^ section, blocks, weight_ref, sems)
        wait_copy(blocks, weight_ref, sems)
    total = own_ref[...].astype(jnp.float32)
    total += jnp.dot(context_ref[...], weight_ref[...], preferred_element_type=jnp.float32)
    result_ref[...] = total.astype(jnp.bfloat16)


def project(kernel, place, operands, weights, section, columns):
    rows = operands[0].shape[0]
    fetch = section is not None
    depth = weights[0].shape[0] * (2 if fetch else 1)
    width = weights[0].shape[1]
    scratch = [pltpu.VMEM((depth, width), jnp.bfloat16), pltpu.SemaphoreType.DMA((2,))]
    return pl.pallas_call(
        functools.partial(kernel, section),
        out_shape=jax.ShapeDtypeStruct((rows, columns), jnp.bfloat16),
        in_specs=[IN_SMEM]
        + [IN_VMEM] * len(operands)
        + [IN_PLACE if fetch else IN_VMEM] * len(weights),
        out_specs=IN_VMEM,
        scratch_shapes=scratch if fetch else [],
        compiler_params=LIMIT,
        cost_estimate=cost(2 * rows * depth * width, 2 * depth * width),
    )(place, *operands, *weights)


def attend_kernel(width, section, place_ref, choice_ref, tiles_ref, length_ref, packed_ref, *refs):
    *blocks, result_ref, held = refs
    for distance, block_ref in enumerate(blocks):

        @pl.when(place_ref[0] ^ section == distance)
        def _():
            held[...] = block_ref[...]

    sources, rows, columns = packed_ref.shape
    heads = (columns - LANES) // HD
    keys = held.shape[0]
    first = place_ref[0] * rows
    sample = first // TXT
    key = lax.broadcasted_iota(jnp.int32, (1, keys), 1)
    valid = jnp.where(key < tiles_ref[choice_ref[sample]] * TROWS, 1.0, 0.0)
    position = first - sample * TXT + lax.broadcasted_iota(jnp.int32, (rows, 1), 0)
    live = jnp.where(position < length_ref[sample], 1.0, 0.0)
    summed = packed_ref[0].astype(jnp.float32)
    for source in range(1, sources):
        summed += packed_ref[source].astype(jnp.float32)
    squares = summed[:, heads * HD : heads * HD + 1] + summed[:, heads * HD + 1 : heads * HD + 2]
    inverse = lax.rsqrt(squares / width + epsilon) * (float(HD) ** (-0.5))
    queries = jnp.concatenate(
        [summed[:, head * HD : (head + 1) * HD] * inverse for head in range(heads)], axis=0
    ).astype(jnp.bfloat16)
    scores = lax.dot_general(
        queries,
        held[:, :HD],
        (((1,), (1,)), ((), ())),
        preferred_element_type=jnp.float32,
    )
    weighted = jnp.exp(scores) * valid
    weights = (weighted / jnp.sum(weighted, axis=-1, keepdims=True)).astype(jnp.bfloat16)
    context = jnp.dot(weights, held[:, HD:], preferred_element_type=jnp.float32)
    for head in range(heads):
        part = (context[head * rows : (head + 1) * rows] * live).astype(jnp.bfloat16)
        for target in range(result_ref.shape[0]):
            result_ref[target, :, head * HD : (head + 1) * HD] = part


def attend(place, choice, tiles, lengths, packed, keyval, section, width):
    sources, rows, columns = packed.shape
    keys = keyval[0].shape[0]
    heads = (columns - LANES) // HD
    return pl.pallas_call(
        functools.partial(attend_kernel, width, section),
        out_shape=jax.ShapeDtypeStruct((sources, rows, heads * HD), jnp.bfloat16),
        in_specs=[IN_SMEM] * 4 + [IN_VMEM] * (1 + len(keyval)),
        out_specs=IN_VMEM,
        scratch_shapes=[pltpu.VMEM(keyval[0].shape, jnp.bfloat16)],
        compiler_params=LIMIT,
        cost_estimate=cost(4 * heads * rows * keys * HD, packed.size * 2, heads * rows * keys),
    )(place, choice, tiles, lengths, packed, *keyval)


def assemble_kernel(received_ref, result_ref):
    cores, phases, slots, rows, piece = received_ref.shape
    for phase in range(phases):
        for slot in range(slots):
            for core in range(cores):
                column = (slot * cores + core) * piece
                result_ref[0, phase * rows : (phase + 1) * rows, column : column + piece] = (
                    received_ref[core, phase, slot]
                )


def assemble(received):
    cores, phases, slots, rows, piece = received.shape
    return pl.pallas_call(
        assemble_kernel,
        out_shape=jax.ShapeDtypeStruct((1, phases * rows, slots * cores * piece), received.dtype),
        in_specs=[IN_VMEM],
        out_specs=IN_VMEM,
        compiler_params=LIMIT,
        cost_estimate=cost(0, 4 * received.size),
    )(received)


def shift(part, distance):
    phases = lax.axis_size("phase")
    return lax.ppermute(part, "phase", [(i, i ^ distance) for i in range(phases)])


def bring(first, second):
    near_first, far_first = shift(first, 1), shift(first, 2)
    near_second, far_second = shift(second, 1), shift(second, 2)
    across = shift(far_first, 1), shift(near_second, 2)
    return first, second, near_first, near_second, far_first, far_second, *across


def exchange(block, axes):
    return lax.all_to_all(block, axes, 0, 0, tiled=True)


def on_device(
    text_rows,
    image_rows,
    tile_counts,
    text_lengths,
    sample_image,
    norm_gain,
    query_weight,
    keyval_weight,
    output_weight,
    cross_gate,
):
    phases, dps, mps = (lax.axis_size(name) for name in ("phase", "dp", "mp"))
    phase_index = lax.axis_index("phase")
    width = norm_gain.shape[1]
    own_rows = text_rows.shape[0]
    part_rows = own_rows // phases
    depth, head_width = query_weight.shape[1:]
    slots = dps // mps
    piece = depth // mps
    context_part = output_weight.shape[1]

    def spread(own_part):
        return lax.all_gather(own_part, "mp", axis=1, tiled=True)

    images = jnp.broadcast_to(image_rows[None], (phases,) + image_rows.shape)
    images = exchange(images, "phase")
    gain = lax.dynamic_slice_in_dim(norm_gain[0], lax.axis_index("dp") * depth, depth, 0)
    middle = depth // 2
    wq = [
        (query_weight[0, rows].astype(jnp.float32) * gain[rows, None]).astype(jnp.bfloat16)
        for rows in (slice(0, middle), slice(middle, depth))
    ]
    wo = output_weight.reshape(context_part, slots, mps, piece).transpose(2, 1, 0, 3)
    wo = wo.reshape(mps, slots * context_part, piece)
    images, wq, wo, text_rows = lax.optimization_barrier((images, wq, wo, text_rows))
    wq = bring(*wq)
    wo = exchange(exchange(wo, "mp").reshape(dps, context_part, piece), "dp")

    place = jnp.full((1,), phase_index, jnp.int32)
    images = lax.all_gather(images, "mp", axis=2, tiled=True)
    keyval = project_keyval(
        part_rows, place, sample_image, cross_gate, images, keyval_weight[0, :, 0, :]
    )
    keyval = [shift(keyval[k], k) if k else keyval[k] for k in range(phases)]
    wo, keyval = lax.optimization_barrier((wo, keyval))
    middle = dps // 2
    wo = bring(wo[:middle].reshape(-1, piece), wo[middle:].reshape(-1, piece))

    mine = lax.dynamic_slice_in_dim(text_rows, phase_index * part_rows, part_rows, 0)
    mine = spread(mine).reshape(part_rows, dps, depth).transpose(1, 0, 2)
    carried = exchange(mine, "dp").reshape(dps * part_rows, depth)
    own = lax.dynamic_slice_in_dim(carried, lax.axis_index("mp") * piece, piece, 1)

    later = range(1, phases)
    wq_later, wo_later = arrange(place, wq, later), arrange(place, wo, later)
    packed_width = head_width + LANES
    states = []
    for section in range(phases):
        if section == 0:
            packed = project(query_kernel, place, [carried], wq, 0, packed_width)
        else:
            carried = spread(own)
            weights = [wq_later[section - 1]]
            packed = project(query_kernel, place, [carried], weights, None, packed_width)
        packed = exchange(packed.reshape(dps, part_rows, packed_width), "dp")
        context = attend(
            place, sample_image, tile_counts, text_lengths, packed, keyval, section, width
        )
        context = spread(exchange(context, "dp").reshape(dps * part_rows, head_width))
        if section == 0:
            own = project(output_kernel, place, [context, own], wo, 0, piece)
        else:
            weights = [wo_later[section - 1]]
            own = project(output_kernel, place, [context, own], weights, None, piece)
        states.append(own)
    result = jnp.stack(states).reshape(phases * dps, part_rows, piece)
    result = exchange(result, ("phase", "dp")).reshape(phases, mps, slots, part_rows, piece)
    return assemble(exchange(result.transpose(1, 0, 2, 3, 4), "mp"))


def solution(mesh):
    placed = (
        P("dp", "mp"),
        P("dp", ("phase", "mp"), None),
        P("dp"),
        P("dp"),
        P("dp"),
        P("phase", None),
        P("phase", "dp", "mp"),
        P("phase", None, "mp", None),
        P("phase", "dp", "mp"),
        P("phase"),
    )
    return jax.shard_map(
        on_device, mesh=mesh, in_specs=placed, out_specs=P("phase", "dp", "mp"), check_vma=False
    )
```

```python
import functools

import jax
import jax.numpy as jnp
from jax import lax
from jax.experimental import pallas as pl
from jax.experimental.pallas import tpu as pltpu
from jax.sharding import PartitionSpec as P

HD = 128
HQ_DEV = 4
TROWS = 32
SAMP = 2
TXT = 64
LANES = 128

epsilon = 1e-05
IN_VMEM = pl.BlockSpec(memory_space=pltpu.VMEM)
IN_PLACE = pl.BlockSpec(memory_space=pl.ANY)
IN_SMEM = pl.BlockSpec(memory_space=pltpu.SMEM)
LIMIT = pltpu.CompilerParams(vmem_limit_bytes=24 * 2**20)


def cost(flops, bytes_accessed, transcendentals=0):
    return pl.CostEstimate(
        flops=flops, bytes_accessed=bytes_accessed, transcendentals=transcendentals
    )


def keyval_kernel(part_rows, place_ref, choice_ref, gate_ref, images_ref, weight_ref, *refs):
    *result_refs, held = refs
    phases, count = images_ref.shape[:2]
    factor = jnp.tanh(jnp.full((1, HD), gate_ref[0], jnp.float32))
    for image in range(count):
        rows = jnp.concatenate([images_ref[phase, image] for phase in range(phases)], axis=0)
        both = jnp.dot(rows, weight_ref[...], preferred_element_type=jnp.float32)
        held[image, :, :HD] = both[:, :HD].astype(jnp.bfloat16)
        held[image, :, HD:] = (both[:, HD:] * factor).astype(jnp.bfloat16)
    for distance, result_ref in enumerate(result_refs):
        sample = (place_ref[0] ^ distance) * part_rows // TXT
        result_ref[...] = held[choice_ref[sample]]


def project_keyval(part_rows, place, choice, gate, images, weight):
    phases, count, rows, depth = images.shape
    keys = phases * rows
    block = jax.ShapeDtypeStruct((keys, 2 * HD), jnp.bfloat16)
    return pl.pallas_call(
        functools.partial(keyval_kernel, part_rows),
        out_shape=[block] * phases,
        in_specs=[IN_SMEM, IN_SMEM, IN_SMEM, IN_VMEM, IN_VMEM],
        out_specs=[IN_VMEM] * phases,
        scratch_shapes=[pltpu.VMEM((count, keys, 2 * HD), jnp.bfloat16)],
        compiler_params=LIMIT,
        cost_estimate=cost(4 * count * keys * depth * HD, 2 * images.size + 2 * weight.size),
    )(place, choice, gate, images, weight)


def start_copy(distance, blocks, target, sems):
    half = target.shape[0] // 2
    for step in range(len(blocks) // 2):

        @pl.when(distance == step)
        def _():
            pltpu.make_async_copy(blocks[2 * step], target.at[:half], sems.at[0]).start()
            pltpu.make_async_copy(blocks[2 * step + 1], target.at[half:], sems.at[1]).start()


def wait_copy(blocks, target, sems):
    half = target.shape[0] // 2
    pltpu.make_async_copy(blocks[0], target.at[:half], sems.at[0]).wait()
    pltpu.make_async_copy(blocks[1], target.at[half:], sems.at[1]).wait()


def arrange_kernel(sections, place_ref, *refs):
    blocks, targets, sems = refs[: -len(sections) - 1], refs[-len(sections) - 1 : -1], refs[-1]
    for step, section in enumerate(sections):
        start_copy(place_ref[0] ^ section, blocks, targets[step], sems.at[step])
    for step in range(len(sections)):
        wait_copy(blocks, targets[step], sems.at[step])


def arrange(place, blocks, sections):
    half, columns = blocks[0].shape
    whole = jax.ShapeDtypeStruct((2 * half, columns), jnp.bfloat16)
    return pl.pallas_call(
        functools.partial(arrange_kernel, sections),
        out_shape=[whole] * len(sections),
        in_specs=[IN_SMEM] + [IN_PLACE] * len(blocks),
        out_specs=[IN_PLACE] * len(sections),
        scratch_shapes=[pltpu.SemaphoreType.DMA((len(sections), 2))],
        compiler_params=LIMIT,
        cost_estimate=cost(0, 8 * half * columns * len(sections)),
    )(place, *blocks)


def query_kernel(section, place_ref, x_ref, *refs):
    if section is None:
        weight_ref, packed_ref = refs
    else:
        *blocks, packed_ref, weight_ref, sems = refs
        start_copy(place_ref[0] ^ section, blocks, weight_ref, sems)
    width = weight_ref.shape[1]
    wide = x_ref[...].astype(jnp.float32)
    squares = jnp.sum(wide * wide, axis=-1, keepdims=True)
    high = squares.astype(jnp.bfloat16).astype(jnp.float32)
    lane = lax.broadcasted_iota(jnp.int32, (x_ref.shape[0], LANES), 1)
    extra = jnp.where(lane == 0, high, jnp.where(lane == 1, squares - high, 0.0))
    packed_ref[:, width:] = extra.astype(jnp.bfloat16)
    if section is not None:
        wait_copy(blocks, weight_ref, sems)
    total = jnp.dot(x_ref[...], weight_ref[...], preferred_element_type=jnp.float32)
    packed_ref[:, :width] = total.astype(jnp.bfloat16)


def output_kernel(section, place_ref, context_ref, own_ref, *refs):
    if section is None:
        weight_ref, result_ref = refs
    else:
        *blocks, result_ref, weight_ref, sems = refs
        start_copy(place_ref[0] ^ section, blocks, weight_ref, sems)
        wait_copy(blocks, weight_ref, sems)
    total = own_ref[...].astype(jnp.float32)
    total += jnp.dot(context_ref[...], weight_ref[...], preferred_element_type=jnp.float32)
    result_ref[...] = total.astype(jnp.bfloat16)


def project(kernel, place, operands, weights, section, columns):
    rows = operands[0].shape[0]
    fetch = section is not None
    depth = weights[0].shape[0] * (2 if fetch else 1)
    width = weights[0].shape[1]
    scratch = [pltpu.VMEM((depth, width), jnp.bfloat16), pltpu.SemaphoreType.DMA((2,))]
    return pl.pallas_call(
        functools.partial(kernel, section),
        out_shape=jax.ShapeDtypeStruct((rows, columns), jnp.bfloat16),
        in_specs=[IN_SMEM]
        + [IN_VMEM] * len(operands)
        + [IN_PLACE if fetch else IN_VMEM] * len(weights),
        out_specs=IN_VMEM,
        scratch_shapes=scratch if fetch else [],
        compiler_params=LIMIT,
        cost_estimate=cost(2 * rows * depth * width, 2 * depth * width),
    )(place, *operands, *weights)


def attend_kernel(width, section, place_ref, choice_ref, tiles_ref, length_ref, packed_ref, *refs):
    *blocks, result_ref, held = refs
    for distance, block_ref in enumerate(blocks):

        @pl.when(place_ref[0] ^ section == distance)
        def _():
            held[...] = block_ref[...]

    sources, rows, columns = packed_ref.shape
    heads = (columns - LANES) // HD
    keys = held.shape[0]
    first = place_ref[0] * rows
    sample = first // TXT
    key = lax.broadcasted_iota(jnp.int32, (1, keys), 1)
    valid = jnp.where(key < tiles_ref[choice_ref[sample]] * TROWS, 1.0, 0.0)
    position = first - sample * TXT + lax.broadcasted_iota(jnp.int32, (rows, 1), 0)
    live = jnp.where(position < length_ref[sample], 1.0, 0.0)
    summed = packed_ref[0].astype(jnp.float32)
    for source in range(1, sources):
        summed += packed_ref[source].astype(jnp.float32)
    squares = summed[:, heads * HD : heads * HD + 1] + summed[:, heads * HD + 1 : heads * HD + 2]
    inverse = lax.rsqrt(squares / width + epsilon) * (float(HD) ** (-0.5))
    queries = jnp.concatenate(
        [summed[:, head * HD : (head + 1) * HD] * inverse for head in range(heads)], axis=0
    ).astype(jnp.bfloat16)
    scores = lax.dot_general(
        queries,
        held[:, :HD],
        (((1,), (1,)), ((), ())),
        preferred_element_type=jnp.float32,
    )
    weighted = jnp.exp(scores) * valid
    weights = (weighted / jnp.sum(weighted, axis=-1, keepdims=True)).astype(jnp.bfloat16)
    context = jnp.dot(weights, held[:, HD:], preferred_element_type=jnp.float32)
    for head in range(heads):
        part = (context[head * rows : (head + 1) * rows] * live).astype(jnp.bfloat16)
        for target in range(result_ref.shape[0]):
            result_ref[target, :, head * HD : (head + 1) * HD] = part


def attend(place, choice, tiles, lengths, packed, keyval, section, width):
    sources, rows, columns = packed.shape
    keys = keyval[0].shape[0]
    heads = (columns - LANES) // HD
    return pl.pallas_call(
        functools.partial(attend_kernel, width, section),
        out_shape=jax.ShapeDtypeStruct((sources, rows, heads * HD), jnp.bfloat16),
        in_specs=[IN_SMEM] * 4 + [IN_VMEM] * (1 + len(keyval)),
        out_specs=IN_VMEM,
        scratch_shapes=[pltpu.VMEM(keyval[0].shape, jnp.bfloat16)],
        compiler_params=LIMIT,
        cost_estimate=cost(4 * heads * rows * keys * HD, packed.size * 2, heads * rows * keys),
    )(place, choice, tiles, lengths, packed, *keyval)


def assemble_kernel(received_ref, result_ref):
    cores, phases, slots, rows, piece = received_ref.shape
    for phase in range(phases):
        for slot in range(slots):
            for core in range(cores):
                column = (slot * cores + core) * piece
                result_ref[0, phase * rows : (phase + 1) * rows, column : column + piece] = (
                    received_ref[core, phase, slot]
                )


def assemble(received):
    cores, phases, slots, rows, piece = received.shape
    return pl.pallas_call(
        assemble_kernel,
        out_shape=jax.ShapeDtypeStruct((1, phases * rows, slots * cores * piece), received.dtype),
        in_specs=[IN_VMEM],
        out_specs=IN_VMEM,
        compiler_params=LIMIT,
        cost_estimate=cost(0, 4 * received.size),
    )(received)


def shift(part, distance):
    phases = lax.axis_size("phase")
    return lax.ppermute(part, "phase", [(i, i ^ distance) for i in range(phases)])


def bring_near(first, second):
    near_first, far_first = shift(first, 1), shift(first, 2)
    near_second, far_second = shift(second, 1), shift(second, 2)
    return first, second, near_first, near_second, far_first, far_second


def bring_across(parts):
    return *parts, shift(parts[4], 1), shift(parts[3], 2)


def bring(first, second):
    return bring_across(bring_near(first, second))


def exchange(block, axes):
    return lax.all_to_all(block, axes, 0, 0, tiled=True)


def on_device(
    text_rows,
    image_rows,
    tile_counts,
    text_lengths,
    sample_image,
    norm_gain,
    query_weight,
    keyval_weight,
    output_weight,
    cross_gate,
):
    phases, dps, mps = (lax.axis_size(name) for name in ("phase", "dp", "mp"))
    phase_index = lax.axis_index("phase")
    width = norm_gain.shape[1]
    own_rows = text_rows.shape[0]
    part_rows = own_rows // phases
    depth, head_width = query_weight.shape[1:]
    slots = dps // mps
    piece = depth // mps
    context_part = output_weight.shape[1]

    def spread(own_part):
        return lax.all_gather(own_part, "mp", axis=1, tiled=True)

    images = jnp.broadcast_to(image_rows[None], (phases,) + image_rows.shape)
    images = exchange(images, "phase")
    gain = lax.dynamic_slice_in_dim(norm_gain[0], lax.axis_index("dp") * depth, depth, 0)
    middle = depth // 2
    wq = [
        (query_weight[0, rows].astype(jnp.float32) * gain[rows, None]).astype(jnp.bfloat16)
        for rows in (slice(0, middle), slice(middle, depth))
    ]
    wo = output_weight.reshape(context_part, slots, mps, piece).transpose(2, 1, 0, 3)
    wo = wo.reshape(mps, slots * context_part, piece)
    images, wo, text_rows = lax.optimization_barrier((images, wo, text_rows))
    wo = exchange(exchange(wo, "mp").reshape(dps, context_part, piece), "dp")

    place = jnp.full((1,), phase_index, jnp.int32)
    images = lax.all_gather(images, "mp", axis=2, tiled=True)
    keyval = project_keyval(
        part_rows, place, sample_image, cross_gate, images, keyval_weight[0, :, 0, :]
    )
    keyval = [shift(keyval[k], k) if k else keyval[k] for k in range(phases)]
    wq, keyval = lax.optimization_barrier((wq, keyval))
    wq = bring(*wq)
    middle = dps // 2
    wo_parts = bring_near(wo[:middle].reshape(-1, piece), wo[middle:].reshape(-1, piece))

    mine = lax.dynamic_slice_in_dim(text_rows, phase_index * part_rows, part_rows, 0)
    mine = spread(mine).reshape(part_rows, dps, depth).transpose(1, 0, 2)
    carried = exchange(mine, "dp").reshape(dps * part_rows, depth)
    own = lax.dynamic_slice_in_dim(carried, lax.axis_index("mp") * piece, piece, 1)

    packed_width = head_width + LANES
    packed = project(query_kernel, place, [carried], wq, 0, packed_width)
    wo_parts, _ = lax.optimization_barrier((wo_parts, packed))
    wo = bring_across(wo_parts)
    later = range(1, phases)
    wq_later, wo_later = arrange(place, wq, later), arrange(place, wo, later)
    states = []
    for section in range(phases):
        if section:
            carried = spread(own)
            weights = [wq_later[section - 1]]
            packed = project(query_kernel, place, [carried], weights, None, packed_width)
        packed = exchange(packed.reshape(dps, part_rows, packed_width), "dp")
        context = attend(
            place, sample_image, tile_counts, text_lengths, packed, keyval, section, width
        )
        context = spread(exchange(context, "dp").reshape(dps * part_rows, head_width))
        if section == 0:
            own = project(output_kernel, place, [context, own], wo, 0, piece)
        else:
            weights = [wo_later[section - 1]]
            own = project(output_kernel, place, [context, own], weights, None, piece)
        states.append(own)
    result = jnp.stack(states).reshape(phases * dps, part_rows, piece)
    result = exchange(result, ("phase", "dp")).reshape(phases, mps, slots, part_rows, piece)
    return assemble(exchange(result.transpose(1, 0, 2, 3, 4), "mp"))


def solution(mesh):
    placed = (
        P("dp", "mp"),
        P("dp", ("phase", "mp"), None),
        P("dp"),
        P("dp"),
        P("dp"),
        P("phase", None),
        P("phase", "dp", "mp"),
        P("phase", None, "mp", None),
        P("phase", "dp", "mp"),
        P("phase"),
    )
    return jax.shard_map(
        on_device, mesh=mesh, in_specs=placed, out_specs=P("phase", "dp", "mp"), check_vma=False
    )
```

```python
import functools

import jax
import jax.numpy as jnp
from jax import lax
from jax.experimental import pallas as pl
from jax.experimental.pallas import tpu as pltpu
from jax.sharding import PartitionSpec as P

HD = 128
HQ_DEV = 4
TROWS = 32
SAMP = 2
TXT = 64
LANES = 128

epsilon = 1e-05
IN_VMEM = pl.BlockSpec(memory_space=pltpu.VMEM)
IN_PLACE = pl.BlockSpec(memory_space=pl.ANY)
IN_SMEM = pl.BlockSpec(memory_space=pltpu.SMEM)
LIMIT = pltpu.CompilerParams(vmem_limit_bytes=24 * 2**20)


def cost(flops, bytes_accessed, transcendentals=0):
    return pl.CostEstimate(
        flops=flops, bytes_accessed=bytes_accessed, transcendentals=transcendentals
    )


def keyval_kernel(part_rows, place_ref, choice_ref, gate_ref, images_ref, weight_ref, *refs):
    *result_refs, held = refs
    phases, count = images_ref.shape[:2]
    factor = jnp.tanh(jnp.full((1, HD), gate_ref[0], jnp.float32))
    for image in range(count):
        rows = jnp.concatenate([images_ref[phase, image] for phase in range(phases)], axis=0)
        both = jnp.dot(rows, weight_ref[...], preferred_element_type=jnp.float32)
        held[image, :, :HD] = both[:, :HD].astype(jnp.bfloat16)
        held[image, :, HD:] = (both[:, HD:] * factor).astype(jnp.bfloat16)
    for distance, result_ref in enumerate(result_refs):
        sample = (place_ref[0] ^ distance) * part_rows // TXT
        result_ref[...] = held[choice_ref[sample]]


def project_keyval(part_rows, place, choice, gate, images, weight):
    phases, count, rows, depth = images.shape
    keys = phases * rows
    block = jax.ShapeDtypeStruct((keys, 2 * HD), jnp.bfloat16)
    return pl.pallas_call(
        functools.partial(keyval_kernel, part_rows),
        out_shape=[block] * phases,
        in_specs=[IN_SMEM, IN_SMEM, IN_SMEM, IN_VMEM, IN_VMEM],
        out_specs=[IN_VMEM] * phases,
        scratch_shapes=[pltpu.VMEM((count, keys, 2 * HD), jnp.bfloat16)],
        compiler_params=LIMIT,
        cost_estimate=cost(4 * count * keys * depth * HD, 2 * images.size + 2 * weight.size),
    )(place, choice, gate, images, weight)


def start_copy(distance, blocks, target, sems):
    half = target.shape[0] // 2
    for step in range(len(blocks) // 2):

        @pl.when(distance == step)
        def _():
            pltpu.make_async_copy(blocks[2 * step], target.at[:half], sems.at[0]).start()
            pltpu.make_async_copy(blocks[2 * step + 1], target.at[half:], sems.at[1]).start()


def wait_copy(blocks, target, sems):
    half = target.shape[0] // 2
    pltpu.make_async_copy(blocks[0], target.at[:half], sems.at[0]).wait()
    pltpu.make_async_copy(blocks[1], target.at[half:], sems.at[1]).wait()


def arrange_kernel(sections, place_ref, *refs):
    blocks, targets, sems = refs[: -len(sections) - 1], refs[-len(sections) - 1 : -1], refs[-1]
    for step, section in enumerate(sections):
        start_copy(place_ref[0] ^ section, blocks, targets[step], sems.at[step])
    for step in range(len(sections)):
        wait_copy(blocks, targets[step], sems.at[step])


def arrange(place, blocks, sections):
    half, columns = blocks[0].shape
    whole = jax.ShapeDtypeStruct((2 * half, columns), jnp.bfloat16)
    return pl.pallas_call(
        functools.partial(arrange_kernel, sections),
        out_shape=[whole] * len(sections),
        in_specs=[IN_SMEM] + [IN_PLACE] * len(blocks),
        out_specs=[IN_PLACE] * len(sections),
        scratch_shapes=[pltpu.SemaphoreType.DMA((len(sections), 2))],
        compiler_params=LIMIT,
        cost_estimate=cost(0, 8 * half * columns * len(sections)),
    )(place, *blocks)


def query_kernel(section, place_ref, x_ref, *refs):
    if section is None:
        weight_ref, packed_ref = refs
    else:
        *blocks, packed_ref, weight_ref, sems = refs
        start_copy(place_ref[0] ^ section, blocks, weight_ref, sems)
    width = weight_ref.shape[1]
    wide = x_ref[...].astype(jnp.float32)
    squares = jnp.sum(wide * wide, axis=-1, keepdims=True)
    high = squares.astype(jnp.bfloat16).astype(jnp.float32)
    lane = lax.broadcasted_iota(jnp.int32, (x_ref.shape[0], LANES), 1)
    extra = jnp.where(lane == 0, high, jnp.where(lane == 1, squares - high, 0.0))
    packed_ref[:, width:] = extra.astype(jnp.bfloat16)
    if section is not None:
        wait_copy(blocks, weight_ref, sems)
    total = jnp.dot(x_ref[...], weight_ref[...], preferred_element_type=jnp.float32)
    packed_ref[:, :width] = total.astype(jnp.bfloat16)


def output_kernel(section, place_ref, context_ref, own_ref, *refs):
    if section is None:
        weight_ref, result_ref = refs
    else:
        *blocks, result_ref, weight_ref, sems = refs
        start_copy(place_ref[0] ^ section, blocks, weight_ref, sems)
        wait_copy(blocks, weight_ref, sems)
    total = own_ref[...].astype(jnp.float32)
    total += jnp.dot(context_ref[...], weight_ref[...], preferred_element_type=jnp.float32)
    result_ref[...] = total.astype(jnp.bfloat16)


def project(kernel, place, operands, weights, section, columns):
    rows = operands[0].shape[0]
    fetch = section is not None
    depth = weights[0].shape[0] * (2 if fetch else 1)
    width = weights[0].shape[1]
    scratch = [pltpu.VMEM((depth, width), jnp.bfloat16), pltpu.SemaphoreType.DMA((2,))]
    return pl.pallas_call(
        functools.partial(kernel, section),
        out_shape=jax.ShapeDtypeStruct((rows, columns), jnp.bfloat16),
        in_specs=[IN_SMEM]
        + [IN_VMEM] * len(operands)
        + [IN_PLACE if fetch else IN_VMEM] * len(weights),
        out_specs=IN_VMEM,
        scratch_shapes=scratch if fetch else [],
        compiler_params=LIMIT,
        cost_estimate=cost(2 * rows * depth * width, 2 * depth * width),
    )(place, *operands, *weights)


def attend_kernel(width, section, place_ref, choice_ref, tiles_ref, length_ref, packed_ref, *refs):
    *blocks, result_ref, held = refs
    for distance, block_ref in enumerate(blocks):

        @pl.when(place_ref[0] ^ section == distance)
        def _():
            held[...] = block_ref[...]

    sources, rows, columns = packed_ref.shape
    heads = (columns - LANES) // HD
    keys = held.shape[0]
    first = place_ref[0] * rows
    sample = first // TXT
    key = lax.broadcasted_iota(jnp.int32, (1, keys), 1)
    valid = jnp.where(key < tiles_ref[choice_ref[sample]] * TROWS, 1.0, 0.0)
    position = first - sample * TXT + lax.broadcasted_iota(jnp.int32, (rows, 1), 0)
    live = jnp.where(position < length_ref[sample], 1.0, 0.0)
    summed = packed_ref[0].astype(jnp.float32)
    for source in range(1, sources):
        summed += packed_ref[source].astype(jnp.float32)
    squares = summed[:, heads * HD : heads * HD + 1] + summed[:, heads * HD + 1 : heads * HD + 2]
    inverse = lax.rsqrt(squares / width + epsilon) * (float(HD) ** (-0.5))
    queries = jnp.concatenate(
        [summed[:, head * HD : (head + 1) * HD] * inverse for head in range(heads)], axis=0
    ).astype(jnp.bfloat16)
    scores = lax.dot_general(
        queries,
        held[:, :HD],
        (((1,), (1,)), ((), ())),
        preferred_element_type=jnp.float32,
    )
    weighted = jnp.exp(scores) * valid
    weights = (weighted / jnp.sum(weighted, axis=-1, keepdims=True)).astype(jnp.bfloat16)
    context = jnp.dot(weights, held[:, HD:], preferred_element_type=jnp.float32)
    for head in range(heads):
        part = (context[head * rows : (head + 1) * rows] * live).astype(jnp.bfloat16)
        for target in range(result_ref.shape[0]):
            result_ref[target, :, head * HD : (head + 1) * HD] = part


def attend(place, choice, tiles, lengths, packed, keyval, section, width):
    sources, rows, columns = packed.shape
    keys = keyval[0].shape[0]
    heads = (columns - LANES) // HD
    return pl.pallas_call(
        functools.partial(attend_kernel, width, section),
        out_shape=jax.ShapeDtypeStruct((sources, rows, heads * HD), jnp.bfloat16),
        in_specs=[IN_SMEM] * 4 + [IN_VMEM] * (1 + len(keyval)),
        out_specs=IN_VMEM,
        scratch_shapes=[pltpu.VMEM(keyval[0].shape, jnp.bfloat16)],
        compiler_params=LIMIT,
        cost_estimate=cost(4 * heads * rows * keys * HD, packed.size * 2, heads * rows * keys),
    )(place, choice, tiles, lengths, packed, *keyval)


def assemble_kernel(received_ref, result_ref):
    cores, phases, slots, rows, piece = received_ref.shape
    for phase in range(phases):
        for slot in range(slots):
            for core in range(cores):
                column = (slot * cores + core) * piece
                result_ref[0, phase * rows : (phase + 1) * rows, column : column + piece] = (
                    received_ref[core, phase, slot]
                )


def assemble(received):
    cores, phases, slots, rows, piece = received.shape
    return pl.pallas_call(
        assemble_kernel,
        out_shape=jax.ShapeDtypeStruct((1, phases * rows, slots * cores * piece), received.dtype),
        in_specs=[IN_VMEM],
        out_specs=IN_VMEM,
        compiler_params=LIMIT,
        cost_estimate=cost(0, 4 * received.size),
    )(received)


def shift(part, distance):
    phases = lax.axis_size("phase")
    return lax.ppermute(part, "phase", [(i, i ^ distance) for i in range(phases)])


def bring_near(first, second):
    near_first, far_first = shift(first, 1), shift(first, 2)
    near_second, far_second = shift(second, 1), shift(second, 2)
    return first, second, near_first, near_second, far_first, far_second


def bring_across(parts, near_second, far_first):
    return *parts, shift(far_first, 1), shift(near_second, 2)


def exchange(block, axes):
    return lax.all_to_all(block, axes, 0, 0, tiled=True)


def on_device(
    text_rows,
    image_rows,
    tile_counts,
    text_lengths,
    sample_image,
    norm_gain,
    query_weight,
    keyval_weight,
    output_weight,
    cross_gate,
):
    phases, dps, mps = (lax.axis_size(name) for name in ("phase", "dp", "mp"))
    phase_index = lax.axis_index("phase")
    width = norm_gain.shape[1]
    own_rows = text_rows.shape[0]
    part_rows = own_rows // phases
    depth, head_width = query_weight.shape[1:]
    slots = dps // mps
    piece = depth // mps
    context_part = output_weight.shape[1]

    def spread(own_part):
        return lax.all_gather(own_part, "mp", axis=1, tiled=True)

    images = jnp.broadcast_to(image_rows[None], (phases,) + image_rows.shape)
    images = exchange(images, "phase")
    gain = lax.dynamic_slice_in_dim(norm_gain[0], lax.axis_index("dp") * depth, depth, 0)
    middle = depth // 2
    wq = [
        (query_weight[0, rows].astype(jnp.float32) * gain[rows, None]).astype(jnp.bfloat16)
        for rows in (slice(0, middle), slice(middle, depth))
    ]
    wo = output_weight.reshape(context_part, slots, mps, piece).transpose(2, 1, 0, 3)
    wo = wo.reshape(mps, slots * context_part, piece)
    images, wq, wo, text_rows = lax.optimization_barrier((images, wq, wo, text_rows))
    wq_parts = bring_near(*wq)
    wo = exchange(exchange(wo, "mp").reshape(dps, context_part, piece), "dp")

    place = jnp.full((1,), phase_index, jnp.int32)
    images = lax.all_gather(images, "mp", axis=2, tiled=True)
    keyval = project_keyval(
        part_rows, place, sample_image, cross_gate, images, keyval_weight[0, :, 0, :]
    )
    forward, keyval = lax.optimization_barrier((wq_parts[3:5], keyval))
    wq = bring_across(wq_parts, *forward)
    keyval = [shift(keyval[k], k) if k else keyval[k] for k in range(phases)]
    wo, keyval = lax.optimization_barrier((wo, keyval))
    middle = dps // 2
    wo_parts = bring_near(wo[:middle].reshape(-1, piece), wo[middle:].reshape(-1, piece))

    mine = lax.dynamic_slice_in_dim(text_rows, phase_index * part_rows, part_rows, 0)
    mine = spread(mine).reshape(part_rows, dps, depth).transpose(1, 0, 2)
    carried = exchange(mine, "dp").reshape(dps * part_rows, depth)
    own = lax.dynamic_slice_in_dim(carried, lax.axis_index("mp") * piece, piece, 1)

    packed_width = head_width + LANES
    packed = project(query_kernel, place, [carried], wq, 0, packed_width)
    forward, _ = lax.optimization_barrier((wo_parts[3:5], packed))
    wo = bring_across(wo_parts, *forward)
    later = range(1, phases)
    wq_later, wo_later = arrange(place, wq, later), arrange(place, wo, later)
    states = []
    for section in range(phases):
        if section:
            carried = spread(own)
            weights = [wq_later[section - 1]]
            packed = project(query_kernel, place, [carried], weights, None, packed_width)
        packed = exchange(packed.reshape(dps, part_rows, packed_width), "dp")
        context = attend(
            place, sample_image, tile_counts, text_lengths, packed, keyval, section, width
        )
        context = spread(exchange(context, "dp").reshape(dps * part_rows, head_width))
        if section == 0:
            own = project(output_kernel, place, [context, own], wo, 0, piece)
        else:
            weights = [wo_later[section - 1]]
            own = project(output_kernel, place, [context, own], weights, None, piece)
        states.append(own)
    result = jnp.stack(states).reshape(phases * dps, part_rows, piece)
    result = exchange(result, ("phase", "dp")).reshape(phases, mps, slots, part_rows, piece)
    return assemble(exchange(result.transpose(1, 0, 2, 3, 4), "mp"))


def solution(mesh):
    placed = (
        P("dp", "mp"),
        P("dp", ("phase", "mp"), None),
        P("dp"),
        P("dp"),
        P("dp"),
        P("phase", None),
        P("phase", "dp", "mp"),
        P("phase", None, "mp", None),
        P("phase", "dp", "mp"),
        P("phase"),
    )
    return jax.shard_map(
        on_device, mesh=mesh, in_specs=placed, out_specs=P("phase", "dp", "mp"), check_vma=False
    )
```

```python
import functools

import jax
import jax.numpy as jnp
from jax import lax
from jax.experimental import pallas as pl
from jax.experimental.pallas import tpu as pltpu
from jax.sharding import PartitionSpec as P

HD = 128
HQ_DEV = 4
TROWS = 32
SAMP = 2
TXT = 64
LANES = 128

epsilon = 1e-05
IN_VMEM = pl.BlockSpec(memory_space=pltpu.VMEM)
IN_PLACE = pl.BlockSpec(memory_space=pl.ANY)
IN_SMEM = pl.BlockSpec(memory_space=pltpu.SMEM)
LIMIT = pltpu.CompilerParams(vmem_limit_bytes=24 * 2**20)


def cost(flops, bytes_accessed, transcendentals=0):
    return pl.CostEstimate(
        flops=flops, bytes_accessed=bytes_accessed, transcendentals=transcendentals
    )


def keyval_kernel(part_rows, place_ref, choice_ref, gate_ref, images_ref, weight_ref, *refs):
    *result_refs, held = refs
    phases, count = images_ref.shape[:2]
    factor = jnp.tanh(jnp.full((1, HD), gate_ref[0], jnp.float32))
    for image in range(count):
        rows = jnp.concatenate([images_ref[phase, image] for phase in range(phases)], axis=0)
        both = jnp.dot(rows, weight_ref[...], preferred_element_type=jnp.float32)
        held[image, :, :HD] = both[:, :HD].astype(jnp.bfloat16)
        held[image, :, HD:] = (both[:, HD:] * factor).astype(jnp.bfloat16)
    for distance, result_ref in enumerate(result_refs):
        sample = (place_ref[0] ^ distance) * part_rows // TXT
        result_ref[...] = held[choice_ref[sample]]


def project_keyval(part_rows, place, choice, gate, images, weight):
    phases, count, rows, depth = images.shape
    keys = phases * rows
    block = jax.ShapeDtypeStruct((keys, 2 * HD), jnp.bfloat16)
    return pl.pallas_call(
        functools.partial(keyval_kernel, part_rows),
        out_shape=[block] * phases,
        in_specs=[IN_SMEM, IN_SMEM, IN_SMEM, IN_VMEM, IN_VMEM],
        out_specs=[IN_VMEM] * phases,
        scratch_shapes=[pltpu.VMEM((count, keys, 2 * HD), jnp.bfloat16)],
        compiler_params=LIMIT,
        cost_estimate=cost(4 * count * keys * depth * HD, 2 * images.size + 2 * weight.size),
    )(place, choice, gate, images, weight)


def start_copy(distance, blocks, target, sems):
    half = target.shape[0] // 2
    for step in range(len(blocks) // 2):

        @pl.when(distance == step)
        def _():
            pltpu.make_async_copy(blocks[2 * step], target.at[:half], sems.at[0]).start()
            pltpu.make_async_copy(blocks[2 * step + 1], target.at[half:], sems.at[1]).start()


def wait_copy(blocks, target, sems):
    half = target.shape[0] // 2
    pltpu.make_async_copy(blocks[0], target.at[:half], sems.at[0]).wait()
    pltpu.make_async_copy(blocks[1], target.at[half:], sems.at[1]).wait()


def arrange_kernel(sections, place_ref, *refs):
    blocks, targets, sems = refs[: -len(sections) - 1], refs[-len(sections) - 1 : -1], refs[-1]
    for step, section in enumerate(sections):
        start_copy(place_ref[0] ^ section, blocks, targets[step], sems.at[step])
    for step in range(len(sections)):
        wait_copy(blocks, targets[step], sems.at[step])


def arrange(place, blocks, sections):
    half, columns = blocks[0].shape
    whole = jax.ShapeDtypeStruct((2 * half, columns), jnp.bfloat16)
    return pl.pallas_call(
        functools.partial(arrange_kernel, sections),
        out_shape=[whole] * len(sections),
        in_specs=[IN_SMEM] + [IN_PLACE] * len(blocks),
        out_specs=[IN_PLACE] * len(sections),
        scratch_shapes=[pltpu.SemaphoreType.DMA((len(sections), 2))],
        compiler_params=LIMIT,
        cost_estimate=cost(0, 8 * half * columns * len(sections)),
    )(place, *blocks)


def query_kernel(section, place_ref, x_ref, *refs):
    if section is None:
        weight_ref, packed_ref = refs
    else:
        *blocks, packed_ref, weight_ref, sems = refs
        start_copy(place_ref[0] ^ section, blocks, weight_ref, sems)
    width = weight_ref.shape[1]
    wide = x_ref[...].astype(jnp.float32)
    squares = jnp.sum(wide * wide, axis=-1, keepdims=True)
    high = squares.astype(jnp.bfloat16).astype(jnp.float32)
    lane = lax.broadcasted_iota(jnp.int32, (x_ref.shape[0], LANES), 1)
    extra = jnp.where(lane == 0, high, jnp.where(lane == 1, squares - high, 0.0))
    packed_ref[:, width:] = extra.astype(jnp.bfloat16)
    if section is not None:
        wait_copy(blocks, weight_ref, sems)
    total = jnp.dot(x_ref[...], weight_ref[...], preferred_element_type=jnp.float32)
    packed_ref[:, :width] = total.astype(jnp.bfloat16)


def output_kernel(section, place_ref, context_ref, own_ref, *refs):
    if section is None:
        weight_ref, result_ref = refs
    else:
        *blocks, result_ref, weight_ref, sems = refs
        start_copy(place_ref[0] ^ section, blocks, weight_ref, sems)
        wait_copy(blocks, weight_ref, sems)
    total = own_ref[...].astype(jnp.float32)
    total += jnp.dot(context_ref[...], weight_ref[...], preferred_element_type=jnp.float32)
    result_ref[...] = total.astype(jnp.bfloat16)


def project(kernel, place, operands, weights, section, columns):
    rows = operands[0].shape[0]
    fetch = section is not None
    depth = weights[0].shape[0] * (2 if fetch else 1)
    width = weights[0].shape[1]
    scratch = [pltpu.VMEM((depth, width), jnp.bfloat16), pltpu.SemaphoreType.DMA((2,))]
    return pl.pallas_call(
        functools.partial(kernel, section),
        out_shape=jax.ShapeDtypeStruct((rows, columns), jnp.bfloat16),
        in_specs=[IN_SMEM]
        + [IN_VMEM] * len(operands)
        + [IN_PLACE if fetch else IN_VMEM] * len(weights),
        out_specs=IN_VMEM,
        scratch_shapes=scratch if fetch else [],
        compiler_params=LIMIT,
        cost_estimate=cost(2 * rows * depth * width, 2 * depth * width),
    )(place, *operands, *weights)


def attend_kernel(width, section, place_ref, choice_ref, tiles_ref, length_ref, packed_ref, *refs):
    *blocks, result_ref, held = refs
    for distance, block_ref in enumerate(blocks):

        @pl.when(place_ref[0] ^ section == distance)
        def _():
            held[...] = block_ref[...]

    sources, rows, columns = packed_ref.shape
    heads = (columns - LANES) // HD
    keys = held.shape[0]
    first = place_ref[0] * rows
    sample = first // TXT
    key = lax.broadcasted_iota(jnp.int32, (1, keys), 1)
    valid = jnp.where(key < tiles_ref[choice_ref[sample]] * TROWS, 1.0, 0.0)
    position = first - sample * TXT + lax.broadcasted_iota(jnp.int32, (rows, 1), 0)
    live = jnp.where(position < length_ref[sample], 1.0, 0.0)
    summed = packed_ref[0].astype(jnp.float32)
    for source in range(1, sources):
        summed += packed_ref[source].astype(jnp.float32)
    squares = summed[:, heads * HD : heads * HD + 1] + summed[:, heads * HD + 1 : heads * HD + 2]
    inverse = lax.rsqrt(squares / width + epsilon) * (float(HD) ** (-0.5))
    queries = jnp.concatenate(
        [summed[:, head * HD : (head + 1) * HD] * inverse for head in range(heads)], axis=0
    ).astype(jnp.bfloat16)
    scores = lax.dot_general(
        queries,
        held[:, :HD],
        (((1,), (1,)), ((), ())),
        preferred_element_type=jnp.float32,
    )
    weighted = jnp.exp(scores) * valid
    weights = (weighted / jnp.sum(weighted, axis=-1, keepdims=True)).astype(jnp.bfloat16)
    context = jnp.dot(weights, held[:, HD:], preferred_element_type=jnp.float32)
    for head in range(heads):
        part = (context[head * rows : (head + 1) * rows] * live).astype(jnp.bfloat16)
        for target in range(result_ref.shape[0]):
            result_ref[target, :, head * HD : (head + 1) * HD] = part


def attend(place, choice, tiles, lengths, packed, keyval, section, width):
    sources, rows, columns = packed.shape
    keys = keyval[0].shape[0]
    heads = (columns - LANES) // HD
    return pl.pallas_call(
        functools.partial(attend_kernel, width, section),
        out_shape=jax.ShapeDtypeStruct((sources, rows, heads * HD), jnp.bfloat16),
        in_specs=[IN_SMEM] * 4 + [IN_VMEM] * (1 + len(keyval)),
        out_specs=IN_VMEM,
        scratch_shapes=[pltpu.VMEM(keyval[0].shape, jnp.bfloat16)],
        compiler_params=LIMIT,
        cost_estimate=cost(4 * heads * rows * keys * HD, packed.size * 2, heads * rows * keys),
    )(place, choice, tiles, lengths, packed, *keyval)


def assemble_kernel(received_ref, result_ref):
    cores, phases, slots, rows, piece = received_ref.shape
    for phase in range(phases):
        for slot in range(slots):
            for core in range(cores):
                column = (slot * cores + core) * piece
                result_ref[0, phase * rows : (phase + 1) * rows, column : column + piece] = (
                    received_ref[core, phase, slot]
                )


def assemble(received):
    cores, phases, slots, rows, piece = received.shape
    return pl.pallas_call(
        assemble_kernel,
        out_shape=jax.ShapeDtypeStruct((1, phases * rows, slots * cores * piece), received.dtype),
        in_specs=[IN_VMEM],
        out_specs=IN_VMEM,
        compiler_params=LIMIT,
        cost_estimate=cost(0, 4 * received.size),
    )(received)


def shift(part, distance):
    phases = lax.axis_size("phase")
    return lax.ppermute(part, "phase", [(i, i ^ distance) for i in range(phases)])


def bring_near(first, second):
    near_first, far_first = shift(first, 1), shift(first, 2)
    near_second, far_second = shift(second, 1), shift(second, 2)
    return first, second, near_first, near_second, far_first, far_second


def bring_across(parts, near_second, far_first):
    return *parts, shift(far_first, 1), shift(near_second, 2)


def exchange(block, axes):
    return lax.all_to_all(block, axes, 0, 0, tiled=True)


def on_device(
    text_rows,
    image_rows,
    tile_counts,
    text_lengths,
    sample_image,
    norm_gain,
    query_weight,
    keyval_weight,
    output_weight,
    cross_gate,
):
    phases, dps, mps = (lax.axis_size(name) for name in ("phase", "dp", "mp"))
    phase_index = lax.axis_index("phase")
    width = norm_gain.shape[1]
    own_rows = text_rows.shape[0]
    part_rows = own_rows // phases
    depth, head_width = query_weight.shape[1:]
    slots = dps // mps
    piece = depth // mps
    context_part = output_weight.shape[1]

    def spread(own_part):
        return lax.all_gather(own_part, "mp", axis=1, tiled=True)

    images = jnp.broadcast_to(image_rows[None], (phases,) + image_rows.shape)
    images = exchange(images, "phase")
    gain = lax.dynamic_slice_in_dim(norm_gain[0], lax.axis_index("dp") * depth, depth, 0)
    middle = depth // 2
    wq = [
        (query_weight[0, rows].astype(jnp.float32) * gain[rows, None]).astype(jnp.bfloat16)
        for rows in (slice(0, middle), slice(middle, depth))
    ]
    wo = output_weight.reshape(context_part, slots, mps, piece).transpose(2, 1, 0, 3)
    wo = wo.reshape(mps, slots * context_part, piece)
    mine = lax.dynamic_slice_in_dim(text_rows, phase_index * part_rows, part_rows, 0)
    mine = spread(mine).reshape(part_rows, dps, depth).transpose(1, 0, 2)
    carried = exchange(mine, "dp")
    images, wq, wo, carried = lax.optimization_barrier((images, wq, wo, carried))
    wq_parts = bring_near(*wq)
    wo = exchange(exchange(wo, "mp").reshape(dps, context_part, piece), "dp")

    place = jnp.full((1,), phase_index, jnp.int32)
    images = lax.all_gather(images, "mp", axis=2, tiled=True)
    keyval = project_keyval(
        part_rows, place, sample_image, cross_gate, images, keyval_weight[0, :, 0, :]
    )
    forward, keyval = lax.optimization_barrier((wq_parts[3:5], keyval))
    wq = bring_across(wq_parts, *forward)
    keyval = [shift(keyval[k], k) if k else keyval[k] for k in range(phases)]
    wo, keyval, wq = lax.optimization_barrier((wo, keyval, wq))
    middle = dps // 2
    wo_parts = bring_near(wo[:middle].reshape(-1, piece), wo[middle:].reshape(-1, piece))

    carried = carried.reshape(dps * part_rows, depth)
    own = lax.dynamic_slice_in_dim(carried, lax.axis_index("mp") * piece, piece, 1)

    packed_width = head_width + LANES
    packed = project(query_kernel, place, [carried], wq, 0, packed_width)
    forward, _ = lax.optimization_barrier((wo_parts[3:5], packed))
    wo = bring_across(wo_parts, *forward)
    later = range(1, phases)
    wq_later, wo_later = arrange(place, wq, later), arrange(place, wo, later)
    states = []
    for section in range(phases):
        if section:
            carried = spread(own)
            weights = [wq_later[section - 1]]
            packed = project(query_kernel, place, [carried], weights, None, packed_width)
        packed = exchange(packed.reshape(dps, part_rows, packed_width), "dp")
        context = attend(
            place, sample_image, tile_counts, text_lengths, packed, keyval, section, width
        )
        context = spread(exchange(context, "dp").reshape(dps * part_rows, head_width))
        if section == 0:
            own = project(output_kernel, place, [context, own], wo, 0, piece)
        else:
            weights = [wo_later[section - 1]]
            own = project(output_kernel, place, [context, own], weights, None, piece)
        states.append(own)
    result = jnp.stack(states).reshape(phases * dps, part_rows, piece)
    result = exchange(result, ("phase", "dp")).reshape(phases, mps, slots, part_rows, piece)
    return assemble(exchange(result.transpose(1, 0, 2, 3, 4), "mp"))


def solution(mesh):
    placed = (
        P("dp", "mp"),
        P("dp", ("phase", "mp"), None),
        P("dp"),
        P("dp"),
        P("dp"),
        P("phase", None),
        P("phase", "dp", "mp"),
        P("phase", None, "mp", None),
        P("phase", "dp", "mp"),
        P("phase"),
    )
    return jax.shard_map(
        on_device, mesh=mesh, in_specs=placed, out_specs=P("phase", "dp", "mp"), check_vma=False
    )
```

```python
import functools

import jax
import jax.numpy as jnp
from jax import lax
from jax.experimental import pallas as pl
from jax.experimental.pallas import tpu as pltpu
from jax.sharding import PartitionSpec as P

HD = 128
HQ_DEV = 4
TROWS = 32
SAMP = 2
TXT = 64
LANES = 128

epsilon = 1e-05
IN_VMEM = pl.BlockSpec(memory_space=pltpu.VMEM)
IN_PLACE = pl.BlockSpec(memory_space=pl.ANY)
IN_SMEM = pl.BlockSpec(memory_space=pltpu.SMEM)
LIMIT = pltpu.CompilerParams(vmem_limit_bytes=24 * 2**20)


def cost(flops, bytes_accessed, transcendentals=0):
    return pl.CostEstimate(
        flops=flops, bytes_accessed=bytes_accessed, transcendentals=transcendentals
    )


def keyval_kernel(part_rows, place_ref, choice_ref, gate_ref, images_ref, weight_ref, *refs):
    *result_refs, held = refs
    phases, count = images_ref.shape[:2]
    factor = jnp.tanh(jnp.full((1, HD), gate_ref[0], jnp.float32))
    for image in range(count):
        rows = jnp.concatenate([images_ref[phase, image] for phase in range(phases)], axis=0)
        both = jnp.dot(rows, weight_ref[...], preferred_element_type=jnp.float32)
        held[image, :, :HD] = both[:, :HD].astype(jnp.bfloat16)
        held[image, :, HD:] = (both[:, HD:] * factor).astype(jnp.bfloat16)
    for distance, result_ref in enumerate(result_refs):
        sample = (place_ref[0] ^ distance) * part_rows // TXT
        result_ref[...] = held[choice_ref[sample]]


def project_keyval(part_rows, place, choice, gate, images, weight):
    phases, count, rows, depth = images.shape
    keys = phases * rows
    block = jax.ShapeDtypeStruct((keys, 2 * HD), jnp.bfloat16)
    return pl.pallas_call(
        functools.partial(keyval_kernel, part_rows),
        out_shape=[block] * phases,
        in_specs=[IN_SMEM, IN_SMEM, IN_SMEM, IN_VMEM, IN_VMEM],
        out_specs=[IN_VMEM] * phases,
        scratch_shapes=[pltpu.VMEM((count, keys, 2 * HD), jnp.bfloat16)],
        compiler_params=LIMIT,
        cost_estimate=cost(4 * count * keys * depth * HD, 2 * images.size + 2 * weight.size),
    )(place, choice, gate, images, weight)


def start_copy(distance, blocks, target, sems):
    half = target.shape[0] // 2
    for step in range(len(blocks) // 2):

        @pl.when(distance == step)
        def _():
            pltpu.make_async_copy(blocks[2 * step], target.at[:half], sems.at[0]).start()
            pltpu.make_async_copy(blocks[2 * step + 1], target.at[half:], sems.at[1]).start()


def wait_copy(blocks, target, sems):
    half = target.shape[0] // 2
    pltpu.make_async_copy(blocks[0], target.at[:half], sems.at[0]).wait()
    pltpu.make_async_copy(blocks[1], target.at[half:], sems.at[1]).wait()


def arrange_kernel(sections, place_ref, *refs):
    blocks, targets, sems = refs[: -len(sections) - 1], refs[-len(sections) - 1 : -1], refs[-1]
    for step, section in enumerate(sections):
        start_copy(place_ref[0] ^ section, blocks, targets[step], sems.at[step])
    for step in range(len(sections)):
        wait_copy(blocks, targets[step], sems.at[step])


def arrange(place, blocks, sections):
    half, columns = blocks[0].shape
    whole = jax.ShapeDtypeStruct((2 * half, columns), jnp.bfloat16)
    return pl.pallas_call(
        functools.partial(arrange_kernel, sections),
        out_shape=[whole] * len(sections),
        in_specs=[IN_SMEM] + [IN_PLACE] * len(blocks),
        out_specs=[IN_PLACE] * len(sections),
        scratch_shapes=[pltpu.SemaphoreType.DMA((len(sections), 2))],
        compiler_params=LIMIT,
        cost_estimate=cost(0, 8 * half * columns * len(sections)),
    )(place, *blocks)


def query_kernel(section, place_ref, x_ref, *refs):
    if section is None:
        weight_ref, packed_ref = refs
    else:
        *blocks, packed_ref, weight_ref, sems = refs
        start_copy(place_ref[0] ^ section, blocks, weight_ref, sems)
    width = weight_ref.shape[1]
    wide = x_ref[...].astype(jnp.float32)
    squares = jnp.sum(wide * wide, axis=-1, keepdims=True)
    high = squares.astype(jnp.bfloat16).astype(jnp.float32)
    lane = lax.broadcasted_iota(jnp.int32, (x_ref.shape[0], LANES), 1)
    extra = jnp.where(lane == 0, high, jnp.where(lane == 1, squares - high, 0.0))
    packed_ref[:, width:] = extra.astype(jnp.bfloat16)
    if section is not None:
        wait_copy(blocks, weight_ref, sems)
    total = jnp.dot(x_ref[...], weight_ref[...], preferred_element_type=jnp.float32)
    packed_ref[:, :width] = total.astype(jnp.bfloat16)


def output_kernel(section, place_ref, context_ref, own_ref, *refs):
    if section is None:
        weight_ref, result_ref = refs
    else:
        *blocks, result_ref, weight_ref, sems = refs
        start_copy(place_ref[0] ^ section, blocks, weight_ref, sems)
        wait_copy(blocks, weight_ref, sems)
    total = own_ref[...].astype(jnp.float32)
    total += jnp.dot(context_ref[...], weight_ref[...], preferred_element_type=jnp.float32)
    result_ref[...] = total.astype(jnp.bfloat16)


def project(kernel, place, operands, weights, section, columns):
    rows = operands[0].shape[0]
    fetch = section is not None
    depth = weights[0].shape[0] * (2 if fetch else 1)
    width = weights[0].shape[1]
    scratch = [pltpu.VMEM((depth, width), jnp.bfloat16), pltpu.SemaphoreType.DMA((2,))]
    return pl.pallas_call(
        functools.partial(kernel, section),
        out_shape=jax.ShapeDtypeStruct((rows, columns), jnp.bfloat16),
        in_specs=[IN_SMEM]
        + [IN_VMEM] * len(operands)
        + [IN_PLACE if fetch else IN_VMEM] * len(weights),
        out_specs=IN_VMEM,
        scratch_shapes=scratch if fetch else [],
        compiler_params=LIMIT,
        cost_estimate=cost(2 * rows * depth * width, 2 * depth * width),
    )(place, *operands, *weights)


def attend_kernel(width, section, place_ref, choice_ref, tiles_ref, length_ref, packed_ref, *refs):
    *blocks, result_ref, held = refs
    for distance, block_ref in enumerate(blocks):

        @pl.when(place_ref[0] ^ section == distance)
        def _():
            held[...] = block_ref[...]

    sources, rows, columns = packed_ref.shape
    heads = (columns - LANES) // HD
    keys = held.shape[0]
    first = place_ref[0] * rows
    sample = first // TXT
    key = lax.broadcasted_iota(jnp.int32, (1, keys), 1)
    valid = jnp.where(key < tiles_ref[choice_ref[sample]] * TROWS, 1.0, 0.0)
    position = first - sample * TXT + lax.broadcasted_iota(jnp.int32, (rows, 1), 0)
    live = jnp.where(position < length_ref[sample], 1.0, 0.0)
    summed = packed_ref[0].astype(jnp.float32)
    for source in range(1, sources):
        summed += packed_ref[source].astype(jnp.float32)
    squares = summed[:, heads * HD : heads * HD + 1] + summed[:, heads * HD + 1 : heads * HD + 2]
    inverse = lax.rsqrt(squares / width + epsilon) * (float(HD) ** (-0.5))
    queries = jnp.concatenate(
        [summed[:, head * HD : (head + 1) * HD] * inverse for head in range(heads)], axis=0
    ).astype(jnp.bfloat16)
    scores = lax.dot_general(
        queries,
        held[:, :HD],
        (((1,), (1,)), ((), ())),
        preferred_element_type=jnp.float32,
    )
    weighted = jnp.exp(scores) * valid
    weights = (weighted / jnp.sum(weighted, axis=-1, keepdims=True)).astype(jnp.bfloat16)
    context = jnp.dot(weights, held[:, HD:], preferred_element_type=jnp.float32)
    for head in range(heads):
        part = (context[head * rows : (head + 1) * rows] * live).astype(jnp.bfloat16)
        for target in range(result_ref.shape[0]):
            result_ref[target, :, head * HD : (head + 1) * HD] = part


def attend(place, choice, tiles, lengths, packed, keyval, section, width):
    sources, rows, columns = packed.shape
    keys = keyval[0].shape[0]
    heads = (columns - LANES) // HD
    return pl.pallas_call(
        functools.partial(attend_kernel, width, section),
        out_shape=jax.ShapeDtypeStruct((sources, rows, heads * HD), jnp.bfloat16),
        in_specs=[IN_SMEM] * 4 + [IN_VMEM] * (1 + len(keyval)),
        out_specs=IN_VMEM,
        scratch_shapes=[pltpu.VMEM(keyval[0].shape, jnp.bfloat16)],
        compiler_params=LIMIT,
        cost_estimate=cost(4 * heads * rows * keys * HD, packed.size * 2, heads * rows * keys),
    )(place, choice, tiles, lengths, packed, *keyval)


def assemble_kernel(received_ref, result_ref):
    cores, phases, slots, rows, piece = received_ref.shape
    for phase in range(phases):
        for slot in range(slots):
            for core in range(cores):
                column = (slot * cores + core) * piece
                result_ref[0, phase * rows : (phase + 1) * rows, column : column + piece] = (
                    received_ref[core, phase, slot]
                )


def assemble(received):
    cores, phases, slots, rows, piece = received.shape
    return pl.pallas_call(
        assemble_kernel,
        out_shape=jax.ShapeDtypeStruct((1, phases * rows, slots * cores * piece), received.dtype),
        in_specs=[IN_VMEM],
        out_specs=IN_VMEM,
        compiler_params=LIMIT,
        cost_estimate=cost(0, 4 * received.size),
    )(received)


def shift(part, distance):
    phases = lax.axis_size("phase")
    return lax.ppermute(part, "phase", [(i, i ^ distance) for i in range(phases)])


def bring_near(first, second):
    near_first, far_first = shift(first, 1), shift(first, 2)
    near_second, far_second = shift(second, 1), shift(second, 2)
    return first, second, near_first, near_second, far_first, far_second


def bring_across(parts, near_second, far_first):
    return *parts, shift(far_first, 1), shift(near_second, 2)


def exchange(block, axes):
    return lax.all_to_all(block, axes, 0, 0, tiled=True)


def on_device(
    text_rows,
    image_rows,
    tile_counts,
    text_lengths,
    sample_image,
    norm_gain,
    query_weight,
    keyval_weight,
    output_weight,
    cross_gate,
):
    phases, dps, mps = (lax.axis_size(name) for name in ("phase", "dp", "mp"))
    phase_index = lax.axis_index("phase")
    width = norm_gain.shape[1]
    own_rows = text_rows.shape[0]
    part_rows = own_rows // phases
    depth, head_width = query_weight.shape[1:]
    slots = dps // mps
    piece = depth // mps
    context_part = output_weight.shape[1]

    def spread(own_part):
        return lax.all_gather(own_part, "mp", axis=1, tiled=True)

    images = jnp.broadcast_to(image_rows[None], (phases,) + image_rows.shape)
    images = exchange(images, "phase")
    gain = lax.dynamic_slice_in_dim(norm_gain[0], lax.axis_index("dp") * depth, depth, 0)
    middle = depth // 2
    wq = [
        (query_weight[0, rows].astype(jnp.float32) * gain[rows, None]).astype(jnp.bfloat16)
        for rows in (slice(0, middle), slice(middle, depth))
    ]
    mine = lax.dynamic_slice_in_dim(text_rows, phase_index * part_rows, part_rows, 0)
    wo = jnp.concatenate([output_weight[0], mine], axis=0)
    wo = wo.reshape(-1, slots, mps, piece).transpose(2, 1, 0, 3).reshape(mps, -1, piece)
    images, wq, wo = lax.optimization_barrier((images, wq, wo))
    wq_parts = bring_near(*wq)
    wo = exchange(exchange(wo, "mp").reshape(dps, context_part + part_rows, piece), "dp")

    place = jnp.full((1,), phase_index, jnp.int32)
    images = lax.all_gather(images, "mp", axis=2, tiled=True)
    keyval = project_keyval(
        part_rows, place, sample_image, cross_gate, images, keyval_weight[0, :, 0, :]
    )
    wq = bring_across(wq_parts, *wq_parts[3:5])
    keyval, _ = lax.optimization_barrier((keyval, wq_parts[2:6]))
    keyval = [shift(keyval[k], k) if k else keyval[k] for k in range(phases)]
    wo, keyval = lax.optimization_barrier((wo, keyval))
    middle = dps // 2
    own = wo[:, context_part:].reshape(dps * part_rows, piece)
    wo = wo[:, :context_part]
    wo_parts = bring_near(wo[:middle].reshape(-1, piece), wo[middle:].reshape(-1, piece))
    carried = spread(own)


    packed_width = head_width + LANES
    packed = project(query_kernel, place, [carried], wq, 0, packed_width)
    forward, _ = lax.optimization_barrier((wo_parts[3:5], packed))
    wo = bring_across(wo_parts, *forward)
    later = range(1, phases)
    wq_later, wo_later = arrange(place, wq, later), arrange(place, wo, later)
    states = []
    for section in range(phases):
        if section:
            carried = spread(own)
            weights = [wq_later[section - 1]]
            packed = project(query_kernel, place, [carried], weights, None, packed_width)
        packed = exchange(packed.reshape(dps, part_rows, packed_width), "dp")
        context = attend(
            place, sample_image, tile_counts, text_lengths, packed, keyval, section, width
        )
        context = spread(exchange(context, "dp").reshape(dps * part_rows, head_width))
        if section == 0:
            own = project(output_kernel, place, [context, own], wo, 0, piece)
        else:
            weights = [wo_later[section - 1]]
            own = project(output_kernel, place, [context, own], weights, None, piece)
        states.append(own)
    result = jnp.stack(states).reshape(phases * dps, part_rows, piece)
    result = exchange(result, ("phase", "dp")).reshape(phases, mps, slots, part_rows, piece)
    return assemble(exchange(result.transpose(1, 0, 2, 3, 4), "mp"))


def solution(mesh):
    placed = (
        P("dp", "mp"),
        P("dp", ("phase", "mp"), None),
        P("dp"),
        P("dp"),
        P("dp"),
        P("phase", None),
        P("phase", "dp", "mp"),
        P("phase", None, "mp", None),
        P("phase", "dp", "mp"),
        P("phase"),
    )
    return jax.shard_map(
        on_device, mesh=mesh, in_specs=placed, out_specs=P("phase", "dp", "mp"), check_vma=False
    )
```

```python
import functools

import jax
import jax.numpy as jnp
from jax import lax
from jax.experimental import pallas as pl
from jax.experimental.pallas import tpu as pltpu
from jax.sharding import PartitionSpec as P

HD = 128
HQ_DEV = 4
TROWS = 32
SAMP = 2
TXT = 64
LANES = 128

epsilon = 1e-05
IN_VMEM = pl.BlockSpec(memory_space=pltpu.VMEM)
IN_PLACE = pl.BlockSpec(memory_space=pl.ANY)
IN_SMEM = pl.BlockSpec(memory_space=pltpu.SMEM)
LIMIT = pltpu.CompilerParams(vmem_limit_bytes=24 * 2**20)


def cost(flops, bytes_accessed, transcendentals=0):
    return pl.CostEstimate(
        flops=flops, bytes_accessed=bytes_accessed, transcendentals=transcendentals
    )


def keyval_kernel(part_rows, place_ref, choice_ref, gate_ref, images_ref, weight_ref, *refs):
    *result_refs, held = refs
    phases, count = images_ref.shape[:2]
    factor = jnp.tanh(jnp.full((1, HD), gate_ref[0], jnp.float32))
    for image in range(count):
        rows = jnp.concatenate([images_ref[phase, image] for phase in range(phases)], axis=0)
        both = jnp.dot(rows, weight_ref[...], preferred_element_type=jnp.float32)
        held[image, :, :HD] = both[:, :HD].astype(jnp.bfloat16)
        held[image, :, HD:] = (both[:, HD:] * factor).astype(jnp.bfloat16)
    for distance, result_ref in enumerate(result_refs):
        sample = (place_ref[0] ^ distance) * part_rows // TXT
        result_ref[...] = held[choice_ref[sample]]


def project_keyval(part_rows, place, choice, gate, images, weight):
    phases, count, rows, depth = images.shape
    keys = phases * rows
    block = jax.ShapeDtypeStruct((keys, 2 * HD), jnp.bfloat16)
    return pl.pallas_call(
        functools.partial(keyval_kernel, part_rows),
        out_shape=[block] * phases,
        in_specs=[IN_SMEM, IN_SMEM, IN_SMEM, IN_VMEM, IN_VMEM],
        out_specs=[IN_VMEM] * phases,
        scratch_shapes=[pltpu.VMEM((count, keys, 2 * HD), jnp.bfloat16)],
        compiler_params=LIMIT,
        cost_estimate=cost(4 * count * keys * depth * HD, 2 * images.size + 2 * weight.size),
    )(place, choice, gate, images, weight)


def start_copy(distance, blocks, target, sems):
    half = target.shape[0] // 2
    for step in range(len(blocks) // 2):

        @pl.when(distance == step)
        def _():
            pltpu.make_async_copy(blocks[2 * step], target.at[:half], sems.at[0]).start()
            pltpu.make_async_copy(blocks[2 * step + 1], target.at[half:], sems.at[1]).start()


def wait_copy(blocks, target, sems):
    half = target.shape[0] // 2
    pltpu.make_async_copy(blocks[0], target.at[:half], sems.at[0]).wait()
    pltpu.make_async_copy(blocks[1], target.at[half:], sems.at[1]).wait()


def arrange_kernel(sections, place_ref, *refs):
    blocks, targets, sems = refs[: -len(sections) - 1], refs[-len(sections) - 1 : -1], refs[-1]
    for step, section in enumerate(sections):
        start_copy(place_ref[0] ^ section, blocks, targets[step], sems.at[step])
    for step in range(len(sections)):
        wait_copy(blocks, targets[step], sems.at[step])


def arrange(place, blocks, sections):
    half, columns = blocks[0].shape
    whole = jax.ShapeDtypeStruct((2 * half, columns), jnp.bfloat16)
    return pl.pallas_call(
        functools.partial(arrange_kernel, sections),
        out_shape=[whole] * len(sections),
        in_specs=[IN_SMEM] + [IN_PLACE] * len(blocks),
        out_specs=[IN_PLACE] * len(sections),
        scratch_shapes=[pltpu.SemaphoreType.DMA((len(sections), 2))],
        compiler_params=LIMIT,
        cost_estimate=cost(0, 8 * half * columns * len(sections)),
    )(place, *blocks)


def query_kernel(section, place_ref, x_ref, *refs):
    if section is None:
        weight_ref, packed_ref = refs
    else:
        *blocks, packed_ref, weight_ref, sems = refs
        start_copy(place_ref[0] ^ section, blocks, weight_ref, sems)
    width = weight_ref.shape[1]
    wide = x_ref[...].astype(jnp.float32)
    squares = jnp.sum(wide * wide, axis=-1, keepdims=True)
    high = squares.astype(jnp.bfloat16).astype(jnp.float32)
    lane = lax.broadcasted_iota(jnp.int32, (x_ref.shape[0], LANES), 1)
    extra = jnp.where(lane == 0, high, jnp.where(lane == 1, squares - high, 0.0))
    packed_ref[:, width:] = extra.astype(jnp.bfloat16)
    if section is not None:
        wait_copy(blocks, weight_ref, sems)
    total = jnp.dot(x_ref[...], weight_ref[...], preferred_element_type=jnp.float32)
    packed_ref[:, :width] = total.astype(jnp.bfloat16)


def output_kernel(section, place_ref, context_ref, own_ref, *refs):
    if section is None:
        weight_ref, result_ref = refs
    else:
        *blocks, result_ref, weight_ref, sems = refs
        start_copy(place_ref[0] ^ section, blocks, weight_ref, sems)
        wait_copy(blocks, weight_ref, sems)
    total = own_ref[...].astype(jnp.float32)
    total += jnp.dot(context_ref[...], weight_ref[...], preferred_element_type=jnp.float32)
    result_ref[...] = total.astype(jnp.bfloat16)


def project(kernel, place, operands, weights, section, columns):
    rows = operands[0].shape[0]
    fetch = section is not None
    depth = weights[0].shape[0] * (2 if fetch else 1)
    width = weights[0].shape[1]
    scratch = [pltpu.VMEM((depth, width), jnp.bfloat16), pltpu.SemaphoreType.DMA((2,))]
    return pl.pallas_call(
        functools.partial(kernel, section),
        out_shape=jax.ShapeDtypeStruct((rows, columns), jnp.bfloat16),
        in_specs=[IN_SMEM]
        + [IN_VMEM] * len(operands)
        + [IN_PLACE if fetch else IN_VMEM] * len(weights),
        out_specs=IN_VMEM,
        scratch_shapes=scratch if fetch else [],
        compiler_params=LIMIT,
        cost_estimate=cost(2 * rows * depth * width, 2 * depth * width),
    )(place, *operands, *weights)


def attend_kernel(width, section, place_ref, choice_ref, tiles_ref, length_ref, packed_ref, *refs):
    *blocks, result_ref, held = refs
    for distance, block_ref in enumerate(blocks):

        @pl.when(place_ref[0] ^ section == distance)
        def _():
            held[...] = block_ref[...]

    sources, rows, columns = packed_ref.shape
    heads = (columns - LANES) // HD
    keys = held.shape[0]
    first = place_ref[0] * rows
    sample = first // TXT
    key = lax.broadcasted_iota(jnp.int32, (1, keys), 1)
    valid = jnp.where(key < tiles_ref[choice_ref[sample]] * TROWS, 1.0, 0.0)
    position = first - sample * TXT + lax.broadcasted_iota(jnp.int32, (rows, 1), 0)
    live = jnp.where(position < length_ref[sample], 1.0, 0.0)
    summed = packed_ref[0].astype(jnp.float32)
    for source in range(1, sources):
        summed += packed_ref[source].astype(jnp.float32)
    squares = summed[:, heads * HD : heads * HD + 1] + summed[:, heads * HD + 1 : heads * HD + 2]
    inverse = lax.rsqrt(squares / width + epsilon) * (float(HD) ** (-0.5))
    queries = jnp.concatenate(
        [summed[:, head * HD : (head + 1) * HD] * inverse for head in range(heads)], axis=0
    ).astype(jnp.bfloat16)
    scores = lax.dot_general(
        queries,
        held[:, :HD],
        (((1,), (1,)), ((), ())),
        preferred_element_type=jnp.float32,
    )
    weighted = jnp.exp(scores) * valid
    weights = (weighted / jnp.sum(weighted, axis=-1, keepdims=True)).astype(jnp.bfloat16)
    context = jnp.dot(weights, held[:, HD:], preferred_element_type=jnp.float32)
    for head in range(heads):
        part = (context[head * rows : (head + 1) * rows] * live).astype(jnp.bfloat16)
        for target in range(result_ref.shape[0]):
            result_ref[target, :, head * HD : (head + 1) * HD] = part


def attend(place, choice, tiles, lengths, packed, keyval, section, width):
    sources, rows, columns = packed.shape
    keys = keyval[0].shape[0]
    heads = (columns - LANES) // HD
    return pl.pallas_call(
        functools.partial(attend_kernel, width, section),
        out_shape=jax.ShapeDtypeStruct((sources, rows, heads * HD), jnp.bfloat16),
        in_specs=[IN_SMEM] * 4 + [IN_VMEM] * (1 + len(keyval)),
        out_specs=IN_VMEM,
        scratch_shapes=[pltpu.VMEM(keyval[0].shape, jnp.bfloat16)],
        compiler_params=LIMIT,
        cost_estimate=cost(4 * heads * rows * keys * HD, packed.size * 2, heads * rows * keys),
    )(place, choice, tiles, lengths, packed, *keyval)


def assemble_kernel(received_ref, result_ref):
    cores, phases, slots, rows, piece = received_ref.shape
    for phase in range(phases):
        for slot in range(slots):
            for core in range(cores):
                column = (slot * cores + core) * piece
                result_ref[0, phase * rows : (phase + 1) * rows, column : column + piece] = (
                    received_ref[core, phase, slot]
                )


def assemble(received):
    cores, phases, slots, rows, piece = received.shape
    return pl.pallas_call(
        assemble_kernel,
        out_shape=jax.ShapeDtypeStruct((1, phases * rows, slots * cores * piece), received.dtype),
        in_specs=[IN_VMEM],
        out_specs=IN_VMEM,
        compiler_params=LIMIT,
        cost_estimate=cost(0, 4 * received.size),
    )(received)


def shift(part, distance):
    phases = lax.axis_size("phase")
    return lax.ppermute(part, "phase", [(i, i ^ distance) for i in range(phases)])


def bring_near(first, second):
    near_first, far_first = shift(first, 1), shift(first, 2)
    near_second, far_second = shift(second, 1), shift(second, 2)
    return first, second, near_first, near_second, far_first, far_second


def bring_across(parts, near_second, far_first):
    return *parts, shift(far_first, 1), shift(near_second, 2)


def exchange(block, axes):
    return lax.all_to_all(block, axes, 0, 0, tiled=True)


def on_device(
    text_rows,
    image_rows,
    tile_counts,
    text_lengths,
    sample_image,
    norm_gain,
    query_weight,
    keyval_weight,
    output_weight,
    cross_gate,
):
    phases, dps, mps = (lax.axis_size(name) for name in ("phase", "dp", "mp"))
    phase_index = lax.axis_index("phase")
    width = norm_gain.shape[1]
    own_rows = text_rows.shape[0]
    part_rows = own_rows // phases
    depth, head_width = query_weight.shape[1:]
    slots = dps // mps
    piece = depth // mps
    context_part = output_weight.shape[1]

    def spread(own_part):
        return lax.all_gather(own_part, "mp", axis=1, tiled=True)

    images = jnp.broadcast_to(image_rows[None], (phases,) + image_rows.shape)
    images = exchange(images, "phase")
    gain = lax.dynamic_slice_in_dim(norm_gain[0], lax.axis_index("dp") * depth, depth, 0)
    middle = depth // 2
    wq = [
        (query_weight[0, rows].astype(jnp.float32) * gain[rows, None]).astype(jnp.bfloat16)
        for rows in (slice(0, middle), slice(middle, depth))
    ]
    mine = lax.dynamic_slice_in_dim(text_rows, phase_index * part_rows, part_rows, 0)
    wo = jnp.concatenate([output_weight[0], mine], axis=0)
    wo = wo.reshape(-1, slots, mps, piece).transpose(2, 1, 0, 3).reshape(mps, -1, piece)
    images, wq, wo = lax.optimization_barrier((images, wq, wo))
    wq_parts = bring_near(*wq)
    wo = exchange(exchange(wo, "mp").reshape(dps, context_part + part_rows, piece), "dp")

    place = jnp.full((1,), phase_index, jnp.int32)
    images = lax.all_gather(images, "mp", axis=2, tiled=True)
    keyval = project_keyval(
        part_rows, place, sample_image, cross_gate, images, keyval_weight[0, :, 0, :]
    )
    wq = bring_across(wq_parts, *wq_parts[3:5])
    keyval, _ = lax.optimization_barrier((keyval, wq[6:]))
    keyval = [shift(keyval[k], k) if k else keyval[k] for k in range(phases)]
    wo, keyval = lax.optimization_barrier((wo, keyval))
    middle = dps // 2
    own = wo[:, context_part:].reshape(dps * part_rows, piece)
    wo = wo[:, :context_part]
    wo_parts = bring_near(wo[:middle].reshape(-1, piece), wo[middle:].reshape(-1, piece))
    carried = spread(own)


    packed_width = head_width + LANES
    packed = project(query_kernel, place, [carried], wq, 0, packed_width)
    packed = exchange(packed.reshape(dps, part_rows, packed_width), "dp")
    forward, _ = lax.optimization_barrier((wo_parts[3:5], packed))
    wo = bring_across(wo_parts, *forward)
    later = range(1, phases)
    wq_later, wo_later = arrange(place, wq, later), arrange(place, wo, later)
    states = []
    for section in range(phases):
        if section:
            carried = spread(own)
            weights = [wq_later[section - 1]]
            packed = project(query_kernel, place, [carried], weights, None, packed_width)
            packed = exchange(packed.reshape(dps, part_rows, packed_width), "dp")
        context = attend(
            place, sample_image, tile_counts, text_lengths, packed, keyval, section, width
        )
        context = spread(exchange(context, "dp").reshape(dps * part_rows, head_width))
        if section == 0:
            own = project(output_kernel, place, [context, own], wo, 0, piece)
        else:
            weights = [wo_later[section - 1]]
            own = project(output_kernel, place, [context, own], weights, None, piece)
        states.append(own)
    result = jnp.stack(states).reshape(phases * dps, part_rows, piece)
    result = exchange(result, ("phase", "dp")).reshape(phases, mps, slots, part_rows, piece)
    return assemble(exchange(result.transpose(1, 0, 2, 3, 4), "mp"))


def solution(mesh):
    placed = (
        P("dp", "mp"),
        P("dp", ("phase", "mp"), None),
        P("dp"),
        P("dp"),
        P("dp"),
        P("phase", None),
        P("phase", "dp", "mp"),
        P("phase", None, "mp", None),
        P("phase", "dp", "mp"),
        P("phase"),
    )
    return jax.shard_map(
        on_device, mesh=mesh, in_specs=placed, out_specs=P("phase", "dp", "mp"), check_vma=False
    )
```

```python
import functools

import jax
import jax.numpy as jnp
from jax import lax
from jax.experimental import pallas as pl
from jax.experimental.pallas import tpu as pltpu
from jax.sharding import PartitionSpec as P

HD = 128
HQ_DEV = 4
TROWS = 32
SAMP = 2
TXT = 64
LANES = 128

epsilon = 1e-05
IN_VMEM = pl.BlockSpec(memory_space=pltpu.VMEM)
IN_PLACE = pl.BlockSpec(memory_space=pl.ANY)
IN_SMEM = pl.BlockSpec(memory_space=pltpu.SMEM)
LIMIT = pltpu.CompilerParams(vmem_limit_bytes=24 * 2**20)


def cost(flops, bytes_accessed, transcendentals=0):
    return pl.CostEstimate(
        flops=flops, bytes_accessed=bytes_accessed, transcendentals=transcendentals
    )


def keyval_kernel(part_rows, place_ref, choice_ref, gate_ref, images_ref, weight_ref, *refs):
    *result_refs, held = refs
    phases, count = images_ref.shape[:2]
    factor = jnp.tanh(jnp.full((1, HD), gate_ref[0], jnp.float32))
    for image in range(count):
        rows = jnp.concatenate([images_ref[phase, image] for phase in range(phases)], axis=0)
        both = jnp.dot(rows, weight_ref[...], preferred_element_type=jnp.float32)
        held[image, :, :HD] = both[:, :HD].astype(jnp.bfloat16)
        held[image, :, HD:] = (both[:, HD:] * factor).astype(jnp.bfloat16)
    for distance, result_ref in enumerate(result_refs):
        sample = (place_ref[0] ^ distance) * part_rows // TXT
        result_ref[...] = held[choice_ref[sample]]


def project_keyval(part_rows, place, choice, gate, images, weight):
    phases, count, rows, depth = images.shape
    keys = phases * rows
    block = jax.ShapeDtypeStruct((keys, 2 * HD), jnp.bfloat16)
    return pl.pallas_call(
        functools.partial(keyval_kernel, part_rows),
        out_shape=[block] * phases,
        in_specs=[IN_SMEM, IN_SMEM, IN_SMEM, IN_VMEM, IN_VMEM],
        out_specs=[IN_VMEM] * phases,
        scratch_shapes=[pltpu.VMEM((count, keys, 2 * HD), jnp.bfloat16)],
        compiler_params=LIMIT,
        cost_estimate=cost(4 * count * keys * depth * HD, 2 * images.size + 2 * weight.size),
    )(place, choice, gate, images, weight)


def start_copy(distance, blocks, target, sems):
    half = target.shape[0] // 2
    for step in range(len(blocks) // 2):

        @pl.when(distance == step)
        def _():
            pltpu.make_async_copy(blocks[2 * step], target.at[:half], sems.at[0]).start()
            pltpu.make_async_copy(blocks[2 * step + 1], target.at[half:], sems.at[1]).start()


def wait_copy(blocks, target, sems):
    half = target.shape[0] // 2
    pltpu.make_async_copy(blocks[0], target.at[:half], sems.at[0]).wait()
    pltpu.make_async_copy(blocks[1], target.at[half:], sems.at[1]).wait()


def arrange_kernel(sections, place_ref, *refs):
    blocks, targets, sems = refs[: -len(sections) - 1], refs[-len(sections) - 1 : -1], refs[-1]
    for step, section in enumerate(sections):
        start_copy(place_ref[0] ^ section, blocks, targets[step], sems.at[step])
    for step in range(len(sections)):
        wait_copy(blocks, targets[step], sems.at[step])


def arrange(place, blocks, sections):
    half, columns = blocks[0].shape
    whole = jax.ShapeDtypeStruct((2 * half, columns), jnp.bfloat16)
    return pl.pallas_call(
        functools.partial(arrange_kernel, sections),
        out_shape=[whole] * len(sections),
        in_specs=[IN_SMEM] + [IN_PLACE] * len(blocks),
        out_specs=[IN_PLACE] * len(sections),
        scratch_shapes=[pltpu.SemaphoreType.DMA((len(sections), 2))],
        compiler_params=LIMIT,
        cost_estimate=cost(0, 8 * half * columns * len(sections)),
    )(place, *blocks)


def query_kernel(section, place_ref, x_ref, *refs):
    if section is None:
        weight_ref, packed_ref = refs
    else:
        *blocks, packed_ref, weight_ref, sems = refs
        start_copy(place_ref[0] ^ section, blocks, weight_ref, sems)
    width = weight_ref.shape[1]
    wide = x_ref[...].astype(jnp.float32)
    squares = jnp.sum(wide * wide, axis=-1, keepdims=True)
    high = squares.astype(jnp.bfloat16).astype(jnp.float32)
    lane = lax.broadcasted_iota(jnp.int32, (x_ref.shape[0], LANES), 1)
    extra = jnp.where(lane == 0, high, jnp.where(lane == 1, squares - high, 0.0))
    packed_ref[:, width:] = extra.astype(jnp.bfloat16)
    if section is not None:
        wait_copy(blocks, weight_ref, sems)
    total = jnp.dot(x_ref[...], weight_ref[...], preferred_element_type=jnp.float32)
    packed_ref[:, :width] = total.astype(jnp.bfloat16)


def output_kernel(section, place_ref, context_ref, own_ref, *refs):
    if section is None:
        weight_ref, result_ref = refs
    else:
        *blocks, result_ref, weight_ref, sems = refs
        start_copy(place_ref[0] ^ section, blocks, weight_ref, sems)
        wait_copy(blocks, weight_ref, sems)
    total = own_ref[...].astype(jnp.float32)
    total += jnp.dot(context_ref[...], weight_ref[...], preferred_element_type=jnp.float32)
    result_ref[...] = total.astype(jnp.bfloat16)


def project(kernel, place, operands, weights, section, columns):
    rows = operands[0].shape[0]
    fetch = section is not None
    depth = weights[0].shape[0] * (2 if fetch else 1)
    width = weights[0].shape[1]
    scratch = [pltpu.VMEM((depth, width), jnp.bfloat16), pltpu.SemaphoreType.DMA((2,))]
    return pl.pallas_call(
        functools.partial(kernel, section),
        out_shape=jax.ShapeDtypeStruct((rows, columns), jnp.bfloat16),
        in_specs=[IN_SMEM]
        + [IN_VMEM] * len(operands)
        + [IN_PLACE if fetch else IN_VMEM] * len(weights),
        out_specs=IN_VMEM,
        scratch_shapes=scratch if fetch else [],
        compiler_params=LIMIT,
        cost_estimate=cost(2 * rows * depth * width, 2 * depth * width),
    )(place, *operands, *weights)


def attend_kernel(width, section, place_ref, choice_ref, tiles_ref, length_ref, packed_ref, *refs):
    *blocks, result_ref, held = refs
    for distance, block_ref in enumerate(blocks):

        @pl.when(place_ref[0] ^ section == distance)
        def _():
            held[...] = block_ref[...]

    sources, rows, columns = packed_ref.shape
    heads = (columns - LANES) // HD
    keys = held.shape[0]
    first = place_ref[0] * rows
    sample = first // TXT
    key = lax.broadcasted_iota(jnp.int32, (1, keys), 1)
    valid = jnp.where(key < tiles_ref[choice_ref[sample]] * TROWS, 1.0, 0.0)
    position = first - sample * TXT + lax.broadcasted_iota(jnp.int32, (rows, 1), 0)
    live = jnp.where(position < length_ref[sample], 1.0, 0.0)
    summed = packed_ref[0].astype(jnp.float32)
    for source in range(1, sources):
        summed += packed_ref[source].astype(jnp.float32)
    squares = summed[:, heads * HD : heads * HD + 1] + summed[:, heads * HD + 1 : heads * HD + 2]
    inverse = lax.rsqrt(squares / width + epsilon) * (float(HD) ** (-0.5))
    queries = jnp.concatenate(
        [summed[:, head * HD : (head + 1) * HD] * inverse for head in range(heads)], axis=0
    ).astype(jnp.bfloat16)
    scores = lax.dot_general(
        queries,
        held[:, :HD],
        (((1,), (1,)), ((), ())),
        preferred_element_type=jnp.float32,
    )
    weighted = jnp.exp(scores) * valid
    weights = (weighted / jnp.sum(weighted, axis=-1, keepdims=True)).astype(jnp.bfloat16)
    context = jnp.dot(weights, held[:, HD:], preferred_element_type=jnp.float32)
    for head in range(heads):
        part = (context[head * rows : (head + 1) * rows] * live).astype(jnp.bfloat16)
        for target in range(result_ref.shape[0]):
            result_ref[target, :, head * HD : (head + 1) * HD] = part


def attend(place, choice, tiles, lengths, packed, keyval, section, width):
    sources, rows, columns = packed.shape
    keys = keyval[0].shape[0]
    heads = (columns - LANES) // HD
    return pl.pallas_call(
        functools.partial(attend_kernel, width, section),
        out_shape=jax.ShapeDtypeStruct((sources, rows, heads * HD), jnp.bfloat16),
        in_specs=[IN_SMEM] * 4 + [IN_VMEM] * (1 + len(keyval)),
        out_specs=IN_VMEM,
        scratch_shapes=[pltpu.VMEM(keyval[0].shape, jnp.bfloat16)],
        compiler_params=LIMIT,
        cost_estimate=cost(4 * heads * rows * keys * HD, packed.size * 2, heads * rows * keys),
    )(place, choice, tiles, lengths, packed, *keyval)


def assemble_kernel(received_ref, result_ref):
    cores, phases, slots, rows, piece = received_ref.shape
    for phase in range(phases):
        for slot in range(slots):
            for core in range(cores):
                column = (slot * cores + core) * piece
                result_ref[0, phase * rows : (phase + 1) * rows, column : column + piece] = (
                    received_ref[core, phase, slot]
                )


def assemble(received):
    cores, phases, slots, rows, piece = received.shape
    return pl.pallas_call(
        assemble_kernel,
        out_shape=jax.ShapeDtypeStruct((1, phases * rows, slots * cores * piece), received.dtype),
        in_specs=[IN_VMEM],
        out_specs=IN_VMEM,
        compiler_params=LIMIT,
        cost_estimate=cost(0, 4 * received.size),
    )(received)


def shift(part, distance):
    phases = lax.axis_size("phase")
    return lax.ppermute(part, "phase", [(i, i ^ distance) for i in range(phases)])


def bring_near(first, second):
    near_first, far_first = shift(first, 1), shift(first, 2)
    near_second, far_second = shift(second, 1), shift(second, 2)
    return first, second, near_first, near_second, far_first, far_second


def bring_across(parts, near_second, far_first):
    return *parts, shift(far_first, 1), shift(near_second, 2)


def exchange(block, axes):
    return lax.all_to_all(block, axes, 0, 0, tiled=True)


def on_device(
    text_rows,
    image_rows,
    tile_counts,
    text_lengths,
    sample_image,
    norm_gain,
    query_weight,
    keyval_weight,
    output_weight,
    cross_gate,
):
    phases, dps, mps = (lax.axis_size(name) for name in ("phase", "dp", "mp"))
    phase_index = lax.axis_index("phase")
    width = norm_gain.shape[1]
    own_rows = text_rows.shape[0]
    part_rows = own_rows // phases
    depth, head_width = query_weight.shape[1:]
    slots = dps // mps
    piece = depth // mps
    context_part = output_weight.shape[1]

    def spread(own_part):
        return lax.all_gather(own_part, "mp", axis=1, tiled=True)

    images = jnp.broadcast_to(image_rows[None], (phases,) + image_rows.shape)
    images = exchange(images, "phase")
    gain = lax.dynamic_slice_in_dim(norm_gain[0], lax.axis_index("dp") * depth, depth, 0)
    middle = depth // 2
    wq = [
        (query_weight[0, rows].astype(jnp.float32) * gain[rows, None]).astype(jnp.bfloat16)
        for rows in (slice(0, middle), slice(middle, depth))
    ]
    mine = lax.dynamic_slice_in_dim(text_rows, phase_index * part_rows, part_rows, 0)
    wo = jnp.concatenate([output_weight[0], mine], axis=0)
    wo = wo.reshape(-1, slots, mps, piece).transpose(2, 1, 0, 3).reshape(mps, -1, piece)
    images, wq, wo = lax.optimization_barrier((images, wq, wo))
    wq_parts = bring_near(*wq)
    wo = exchange(exchange(wo, "mp").reshape(dps, context_part + part_rows, piece), "dp")

    place = jnp.full((1,), phase_index, jnp.int32)
    images = lax.all_gather(images, "mp", axis=2, tiled=True)
    keyval = project_keyval(
        part_rows, place, sample_image, cross_gate, images, keyval_weight[0, :, 0, :]
    )
    wq = bring_across(wq_parts, *wq_parts[3:5])
    keyval, wo = lax.optimization_barrier((keyval, wo))
    keyval = [shift(keyval[k], k) if k else keyval[k] for k in range(phases)]
    wo, keyval = lax.optimization_barrier((wo, keyval))
    middle = dps // 2
    own = wo[:, context_part:].reshape(dps * part_rows, piece)
    wo = wo[:, :context_part]
    wo_parts = bring_near(wo[:middle].reshape(-1, piece), wo[middle:].reshape(-1, piece))
    carried = spread(own)


    packed_width = head_width + LANES
    packed = project(query_kernel, place, [carried], wq, 0, packed_width)
    packed = exchange(packed.reshape(dps, part_rows, packed_width), "dp")
    forward, _ = lax.optimization_barrier((wo_parts[3:5], packed))
    wo = bring_across(wo_parts, *forward)
    later = range(1, phases)
    wq_later, wo_later = arrange(place, wq, later), arrange(place, wo, later)
    states = []
    for section in range(phases):
        if section:
            carried = spread(own)
            weights = [wq_later[section - 1]]
            packed = project(query_kernel, place, [carried], weights, None, packed_width)
            packed = exchange(packed.reshape(dps, part_rows, packed_width), "dp")
        context = attend(
            place, sample_image, tile_counts, text_lengths, packed, keyval, section, width
        )
        context = spread(exchange(context, "dp").reshape(dps * part_rows, head_width))
        if section == 0:
            own = project(output_kernel, place, [context, own], wo, 0, piece)
        else:
            weights = [wo_later[section - 1]]
            own = project(output_kernel, place, [context, own], weights, None, piece)
        states.append(own)
    result = jnp.stack(states).reshape(phases * dps, part_rows, piece)
    result = exchange(result, ("phase", "dp")).reshape(phases, mps, slots, part_rows, piece)
    return assemble(exchange(result.transpose(1, 0, 2, 3, 4), "mp"))


def solution(mesh):
    placed = (
        P("dp", "mp"),
        P("dp", ("phase", "mp"), None),
        P("dp"),
        P("dp"),
        P("dp"),
        P("phase", None),
        P("phase", "dp", "mp"),
        P("phase", None, "mp", None),
        P("phase", "dp", "mp"),
        P("phase"),
    )
    return jax.shard_map(
        on_device, mesh=mesh, in_specs=placed, out_specs=P("phase", "dp", "mp"), check_vma=False
    )
```

```python
import functools

import jax
import jax.numpy as jnp
from jax import lax
from jax.experimental import pallas as pl
from jax.experimental.pallas import tpu as pltpu
from jax.sharding import PartitionSpec as P

HD = 128
HQ_DEV = 4
TROWS = 32
SAMP = 2
TXT = 64
LANES = 128

epsilon = 1e-05
IN_VMEM = pl.BlockSpec(memory_space=pltpu.VMEM)
IN_PLACE = pl.BlockSpec(memory_space=pl.ANY)
IN_SMEM = pl.BlockSpec(memory_space=pltpu.SMEM)
LIMIT = pltpu.CompilerParams(vmem_limit_bytes=24 * 2**20)


def cost(flops, bytes_accessed, transcendentals=0):
    return pl.CostEstimate(
        flops=flops, bytes_accessed=bytes_accessed, transcendentals=transcendentals
    )


def keyval_kernel(part_rows, place_ref, choice_ref, gate_ref, images_ref, weight_ref, *refs):
    *result_refs, held = refs
    phases, count = images_ref.shape[:2]
    factor = jnp.tanh(jnp.full((1, HD), gate_ref[0], jnp.float32))
    for image in range(count):
        rows = jnp.concatenate([images_ref[phase, image] for phase in range(phases)], axis=0)
        both = jnp.dot(rows, weight_ref[...], preferred_element_type=jnp.float32)
        held[image, :, :HD] = both[:, :HD].astype(jnp.bfloat16)
        held[image, :, HD:] = (both[:, HD:] * factor).astype(jnp.bfloat16)
    for distance, result_ref in enumerate(result_refs):
        sample = (place_ref[0] ^ distance) * part_rows // TXT
        result_ref[...] = held[choice_ref[sample]]


def project_keyval(part_rows, place, choice, gate, images, weight):
    phases, count, rows, depth = images.shape
    keys = phases * rows
    block = jax.ShapeDtypeStruct((keys, 2 * HD), jnp.bfloat16)
    return pl.pallas_call(
        functools.partial(keyval_kernel, part_rows),
        out_shape=[block] * phases,
        in_specs=[IN_SMEM, IN_SMEM, IN_SMEM, IN_VMEM, IN_VMEM],
        out_specs=[IN_VMEM] * phases,
        scratch_shapes=[pltpu.VMEM((count, keys, 2 * HD), jnp.bfloat16)],
        compiler_params=LIMIT,
        cost_estimate=cost(4 * count * keys * depth * HD, 2 * images.size + 2 * weight.size),
    )(place, choice, gate, images, weight)


def start_copy(distance, blocks, target, sems):
    half = target.shape[0] // 2
    for step in range(len(blocks) // 2):

        @pl.when(distance == step)
        def _():
            pltpu.make_async_copy(blocks[2 * step], target.at[:half], sems.at[0]).start()
            pltpu.make_async_copy(blocks[2 * step + 1], target.at[half:], sems.at[1]).start()


def wait_copy(blocks, target, sems):
    half = target.shape[0] // 2
    pltpu.make_async_copy(blocks[0], target.at[:half], sems.at[0]).wait()
    pltpu.make_async_copy(blocks[1], target.at[half:], sems.at[1]).wait()


def arrange_kernel(sections, place_ref, *refs):
    blocks, targets, sems = refs[: -len(sections) - 1], refs[-len(sections) - 1 : -1], refs[-1]
    for step, section in enumerate(sections):
        start_copy(place_ref[0] ^ section, blocks, targets[step], sems.at[step])
    for step in range(len(sections)):
        wait_copy(blocks, targets[step], sems.at[step])


def arrange(place, blocks, sections):
    half, columns = blocks[0].shape
    whole = jax.ShapeDtypeStruct((2 * half, columns), jnp.bfloat16)
    return pl.pallas_call(
        functools.partial(arrange_kernel, sections),
        out_shape=[whole] * len(sections),
        in_specs=[IN_SMEM] + [IN_PLACE] * len(blocks),
        out_specs=[IN_PLACE] * len(sections),
        scratch_shapes=[pltpu.SemaphoreType.DMA((len(sections), 2))],
        compiler_params=LIMIT,
        cost_estimate=cost(0, 8 * half * columns * len(sections)),
    )(place, *blocks)


def query_kernel(section, place_ref, x_ref, *refs):
    if section is None:
        weight_ref, packed_ref = refs
    else:
        *blocks, packed_ref, weight_ref, sems = refs
        start_copy(place_ref[0] ^ section, blocks, weight_ref, sems)
    width = weight_ref.shape[1]
    wide = x_ref[...].astype(jnp.float32)
    squares = jnp.sum(wide * wide, axis=-1, keepdims=True)
    high = squares.astype(jnp.bfloat16).astype(jnp.float32)
    lane = lax.broadcasted_iota(jnp.int32, (x_ref.shape[0], LANES), 1)
    extra = jnp.where(lane == 0, high, jnp.where(lane == 1, squares - high, 0.0))
    packed_ref[:, width:] = extra.astype(jnp.bfloat16)
    if section is not None:
        wait_copy(blocks, weight_ref, sems)
    total = jnp.dot(x_ref[...], weight_ref[...], preferred_element_type=jnp.float32)
    packed_ref[:, :width] = total.astype(jnp.bfloat16)


def output_kernel(section, place_ref, context_ref, own_ref, *refs):
    if section is None:
        weight_ref, result_ref = refs
    else:
        *blocks, result_ref, weight_ref, sems = refs
        start_copy(place_ref[0] ^ section, blocks, weight_ref, sems)
        wait_copy(blocks, weight_ref, sems)
    total = own_ref[...].astype(jnp.float32)
    total += jnp.dot(context_ref[...], weight_ref[...], preferred_element_type=jnp.float32)
    result_ref[...] = total.astype(jnp.bfloat16)


def project(kernel, place, operands, weights, section, columns):
    rows = operands[0].shape[0]
    fetch = section is not None
    depth = weights[0].shape[0] * (2 if fetch else 1)
    width = weights[0].shape[1]
    scratch = [pltpu.VMEM((depth, width), jnp.bfloat16), pltpu.SemaphoreType.DMA((2,))]
    return pl.pallas_call(
        functools.partial(kernel, section),
        out_shape=jax.ShapeDtypeStruct((rows, columns), jnp.bfloat16),
        in_specs=[IN_SMEM]
        + [IN_VMEM] * len(operands)
        + [IN_PLACE if fetch else IN_VMEM] * len(weights),
        out_specs=IN_VMEM,
        scratch_shapes=scratch if fetch else [],
        compiler_params=LIMIT,
        cost_estimate=cost(2 * rows * depth * width, 2 * depth * width),
    )(place, *operands, *weights)


def attend_kernel(width, section, place_ref, choice_ref, tiles_ref, length_ref, packed_ref, *refs):
    *blocks, result_ref, held = refs
    for distance, block_ref in enumerate(blocks):

        @pl.when(place_ref[0] ^ section == distance)
        def _():
            held[...] = block_ref[...]

    sources, rows, columns = packed_ref.shape
    heads = (columns - LANES) // HD
    keys = held.shape[0]
    first = place_ref[0] * rows
    sample = first // TXT
    key = lax.broadcasted_iota(jnp.int32, (1, keys), 1)
    valid = jnp.where(key < tiles_ref[choice_ref[sample]] * TROWS, 1.0, 0.0)
    position = first - sample * TXT + lax.broadcasted_iota(jnp.int32, (rows, 1), 0)
    live = jnp.where(position < length_ref[sample], 1.0, 0.0)
    summed = packed_ref[0].astype(jnp.float32)
    for source in range(1, sources):
        summed += packed_ref[source].astype(jnp.float32)
    squares = summed[:, heads * HD : heads * HD + 1] + summed[:, heads * HD + 1 : heads * HD + 2]
    inverse = lax.rsqrt(squares / width + epsilon) * (float(HD) ** (-0.5))
    queries = jnp.concatenate(
        [summed[:, head * HD : (head + 1) * HD] * inverse for head in range(heads)], axis=0
    ).astype(jnp.bfloat16)
    scores = lax.dot_general(
        queries,
        held[:, :HD],
        (((1,), (1,)), ((), ())),
        preferred_element_type=jnp.float32,
    )
    weighted = jnp.exp(scores) * valid
    weights = (weighted / jnp.sum(weighted, axis=-1, keepdims=True)).astype(jnp.bfloat16)
    context = jnp.dot(weights, held[:, HD:], preferred_element_type=jnp.float32)
    for head in range(heads):
        part = (context[head * rows : (head + 1) * rows] * live).astype(jnp.bfloat16)
        for target in range(result_ref.shape[0]):
            result_ref[target, :, head * HD : (head + 1) * HD] = part


def attend(place, choice, tiles, lengths, packed, keyval, section, width):
    sources, rows, columns = packed.shape
    keys = keyval[0].shape[0]
    heads = (columns - LANES) // HD
    return pl.pallas_call(
        functools.partial(attend_kernel, width, section),
        out_shape=jax.ShapeDtypeStruct((sources, rows, heads * HD), jnp.bfloat16),
        in_specs=[IN_SMEM] * 4 + [IN_VMEM] * (1 + len(keyval)),
        out_specs=IN_VMEM,
        scratch_shapes=[pltpu.VMEM(keyval[0].shape, jnp.bfloat16)],
        compiler_params=LIMIT,
        cost_estimate=cost(4 * heads * rows * keys * HD, packed.size * 2, heads * rows * keys),
    )(place, choice, tiles, lengths, packed, *keyval)


def assemble_kernel(received_ref, result_ref):
    cores, phases, slots, rows, piece = received_ref.shape
    for phase in range(phases):
        for slot in range(slots):
            for core in range(cores):
                column = (slot * cores + core) * piece
                result_ref[0, phase * rows : (phase + 1) * rows, column : column + piece] = (
                    received_ref[core, phase, slot]
                )


def assemble(received):
    cores, phases, slots, rows, piece = received.shape
    return pl.pallas_call(
        assemble_kernel,
        out_shape=jax.ShapeDtypeStruct((1, phases * rows, slots * cores * piece), received.dtype),
        in_specs=[IN_VMEM],
        out_specs=IN_VMEM,
        compiler_params=LIMIT,
        cost_estimate=cost(0, 4 * received.size),
    )(received)


def shift(part, distance):
    phases = lax.axis_size("phase")
    return lax.ppermute(part, "phase", [(i, i ^ distance) for i in range(phases)])


def bring_near(first, second):
    near_first, far_first = shift(first, 1), shift(first, 2)
    near_second, far_second = shift(second, 1), shift(second, 2)
    return first, second, near_first, near_second, far_first, far_second


def bring_across(parts, near_second, far_first):
    return *parts, shift(far_first, 1), shift(near_second, 2)


def exchange(block, axes):
    return lax.all_to_all(block, axes, 0, 0, tiled=True)


def on_device(
    text_rows,
    image_rows,
    tile_counts,
    text_lengths,
    sample_image,
    norm_gain,
    query_weight,
    keyval_weight,
    output_weight,
    cross_gate,
):
    phases, dps, mps = (lax.axis_size(name) for name in ("phase", "dp", "mp"))
    phase_index = lax.axis_index("phase")
    width = norm_gain.shape[1]
    own_rows = text_rows.shape[0]
    part_rows = own_rows // phases
    depth, head_width = query_weight.shape[1:]
    slots = dps // mps
    piece = depth // mps
    context_part = output_weight.shape[1]

    def spread(own_part):
        return lax.all_gather(own_part, "mp", axis=1, tiled=True)

    images = jnp.broadcast_to(image_rows[None], (phases,) + image_rows.shape)
    images = exchange(images, "phase")
    gain = lax.dynamic_slice_in_dim(norm_gain[0], lax.axis_index("dp") * depth, depth, 0)
    middle = depth // 2
    wq = [
        (query_weight[0, rows].astype(jnp.float32) * gain[rows, None]).astype(jnp.bfloat16)
        for rows in (slice(0, middle), slice(middle, depth))
    ]
    mine = lax.dynamic_slice_in_dim(text_rows, phase_index * part_rows, part_rows, 0)
    wo = jnp.concatenate([output_weight[0], mine], axis=0)
    wo = wo.reshape(-1, slots, mps, piece).transpose(2, 1, 0, 3).reshape(mps, -1, piece)
    images, wq, wo = lax.optimization_barrier((images, wq, wo))
    wq_parts = bring_near(*wq)
    wo = exchange(exchange(wo, "mp").reshape(dps, context_part + part_rows, piece), "dp")

    place = jnp.full((1,), phase_index, jnp.int32)
    images = lax.all_gather(images, "mp", axis=2, tiled=True)
    keyval = project_keyval(
        part_rows, place, sample_image, cross_gate, images, keyval_weight[0, :, 0, :]
    )
    wq = bring_across(wq_parts, *wq_parts[3:5])
    keyval, _ = lax.optimization_barrier((keyval, wq_parts[2:6]))
    keyval = [shift(keyval[k], k) if k else keyval[k] for k in range(phases)]
    wo, keyval = lax.optimization_barrier((wo, keyval))
    middle = dps // 2
    own = wo[:, context_part:].reshape(dps * part_rows, piece)
    wo = wo[:, :context_part]
    wo_parts = bring_near(wo[:middle].reshape(-1, piece), wo[middle:].reshape(-1, piece))
    carried = spread(own)


    packed_width = head_width + LANES
    packed = project(query_kernel, place, [carried], wq, 0, packed_width)
    packed = exchange(packed.reshape(dps, part_rows, packed_width), "dp")
    forward, _ = lax.optimization_barrier((wo_parts[3:5], packed))
    wo = bring_across(wo_parts, *forward)
    later = range(1, phases)
    wq_later, wo_later = arrange(place, wq, later), arrange(place, wo, later)
    states = []
    for section in range(phases):
        if section:
            carried = spread(own)
            weights = [wq_later[section - 1]]
            packed = project(query_kernel, place, [carried], weights, None, packed_width)
            packed = exchange(packed.reshape(dps, part_rows, packed_width), "dp")
        context = attend(
            place, sample_image, tile_counts, text_lengths, packed, keyval, section, width
        )
        context = spread(exchange(context, "dp").reshape(dps * part_rows, head_width))
        if section == 0:
            own = project(output_kernel, place, [context, own], wo, 0, piece)
        else:
            weights = [wo_later[section - 1]]
            own = project(output_kernel, place, [context, own], weights, None, piece)
        states.append(own)
    result = jnp.stack(states).reshape(phases * dps, part_rows, piece)
    result = exchange(result, ("phase", "dp")).reshape(phases, mps, slots, part_rows, piece)
    return assemble(exchange(result.transpose(1, 0, 2, 3, 4), "mp"))


def solution(mesh):
    placed = (
        P("dp", "mp"),
        P("dp", ("phase", "mp"), None),
        P("dp"),
        P("dp"),
        P("dp"),
        P("phase", None),
        P("phase", "dp", "mp"),
        P("phase", None, "mp", None),
        P("phase", "dp", "mp"),
        P("phase"),
    )
    return jax.shard_map(
        on_device, mesh=mesh, in_specs=placed, out_specs=P("phase", "dp", "mp"), check_vma=False
    )
```

```python
import functools

import jax
import jax.numpy as jnp
from jax import lax
from jax.experimental import pallas as pl
from jax.experimental.pallas import tpu as pltpu
from jax.sharding import PartitionSpec as P

HD = 128
HQ_DEV = 4
TROWS = 32
SAMP = 2
TXT = 64
LANES = 128

epsilon = 1e-05
IN_VMEM = pl.BlockSpec(memory_space=pltpu.VMEM)
IN_PLACE = pl.BlockSpec(memory_space=pl.ANY)
IN_SMEM = pl.BlockSpec(memory_space=pltpu.SMEM)
LIMIT = pltpu.CompilerParams(vmem_limit_bytes=24 * 2**20)


def cost(flops, bytes_accessed, transcendentals=0):
    return pl.CostEstimate(
        flops=flops, bytes_accessed=bytes_accessed, transcendentals=transcendentals
    )


def keyval_kernel(part_rows, place_ref, choice_ref, gate_ref, images_ref, weight_ref, *refs):
    *result_refs, held = refs
    phases, count = images_ref.shape[:2]
    factor = jnp.tanh(jnp.full((1, HD), gate_ref[0], jnp.float32))
    for image in range(count):
        rows = jnp.concatenate([images_ref[phase, image] for phase in range(phases)], axis=0)
        both = jnp.dot(rows, weight_ref[...], preferred_element_type=jnp.float32)
        held[image, :, :HD] = both[:, :HD].astype(jnp.bfloat16)
        held[image, :, HD:] = (both[:, HD:] * factor).astype(jnp.bfloat16)
    for distance, result_ref in enumerate(result_refs):
        sample = (place_ref[0] ^ distance) * part_rows // TXT
        result_ref[...] = held[choice_ref[sample]]


def project_keyval(part_rows, place, choice, gate, images, weight):
    phases, count, rows, depth = images.shape
    keys = phases * rows
    block = jax.ShapeDtypeStruct((keys, 2 * HD), jnp.bfloat16)
    return pl.pallas_call(
        functools.partial(keyval_kernel, part_rows),
        out_shape=[block] * phases,
        in_specs=[IN_SMEM, IN_SMEM, IN_SMEM, IN_VMEM, IN_VMEM],
        out_specs=[IN_VMEM] * phases,
        scratch_shapes=[pltpu.VMEM((count, keys, 2 * HD), jnp.bfloat16)],
        compiler_params=LIMIT,
        cost_estimate=cost(4 * count * keys * depth * HD, 2 * images.size + 2 * weight.size),
    )(place, choice, gate, images, weight)


def start_copy(distance, blocks, target, sems):
    half = target.shape[0] // 2
    for step in range(len(blocks) // 2):

        @pl.when(distance == step)
        def _():
            pltpu.make_async_copy(blocks[2 * step], target.at[:half], sems.at[0]).start()
            pltpu.make_async_copy(blocks[2 * step + 1], target.at[half:], sems.at[1]).start()


def wait_copy(blocks, target, sems):
    half = target.shape[0] // 2
    pltpu.make_async_copy(blocks[0], target.at[:half], sems.at[0]).wait()
    pltpu.make_async_copy(blocks[1], target.at[half:], sems.at[1]).wait()


def arrange_kernel(sections, place_ref, *refs):
    blocks, targets, sems = refs[: -len(sections) - 1], refs[-len(sections) - 1 : -1], refs[-1]
    for step, section in enumerate(sections):
        start_copy(place_ref[0] ^ section, blocks, targets[step], sems.at[step])
    for step in range(len(sections)):
        wait_copy(blocks, targets[step], sems.at[step])


def arrange(place, blocks, sections):
    half, columns = blocks[0].shape
    whole = jax.ShapeDtypeStruct((2 * half, columns), jnp.bfloat16)
    return pl.pallas_call(
        functools.partial(arrange_kernel, sections),
        out_shape=[whole] * len(sections),
        in_specs=[IN_SMEM] + [IN_PLACE] * len(blocks),
        out_specs=[IN_PLACE] * len(sections),
        scratch_shapes=[pltpu.SemaphoreType.DMA((len(sections), 2))],
        compiler_params=LIMIT,
        cost_estimate=cost(0, 8 * half * columns * len(sections)),
    )(place, *blocks)


def query_kernel(section, place_ref, x_ref, *refs):
    if section is None:
        weight_ref, packed_ref = refs
    else:
        *blocks, packed_ref, weight_ref, sems = refs
        start_copy(place_ref[0] ^ section, blocks, weight_ref, sems)
    width = weight_ref.shape[1]
    wide = x_ref[...].astype(jnp.float32)
    squares = jnp.sum(wide * wide, axis=-1, keepdims=True)
    high = squares.astype(jnp.bfloat16).astype(jnp.float32)
    lane = lax.broadcasted_iota(jnp.int32, (x_ref.shape[0], LANES), 1)
    extra = jnp.where(lane == 0, high, jnp.where(lane == 1, squares - high, 0.0))
    packed_ref[:, width:] = extra.astype(jnp.bfloat16)
    if section is not None:
        wait_copy(blocks, weight_ref, sems)
    total = jnp.dot(x_ref[...], weight_ref[...], preferred_element_type=jnp.float32)
    packed_ref[:, :width] = total.astype(jnp.bfloat16)


def output_kernel(section, place_ref, context_ref, own_ref, *refs):
    if section is None:
        weight_ref, result_ref = refs
    else:
        *blocks, result_ref, weight_ref, sems = refs
        start_copy(place_ref[0] ^ section, blocks, weight_ref, sems)
        wait_copy(blocks, weight_ref, sems)
    total = own_ref[...].astype(jnp.float32)
    total += jnp.dot(context_ref[...], weight_ref[...], preferred_element_type=jnp.float32)
    result_ref[...] = total.astype(jnp.bfloat16)


def project(kernel, place, operands, weights, section, columns):
    rows = operands[0].shape[0]
    fetch = section is not None
    depth = weights[0].shape[0] * (2 if fetch else 1)
    width = weights[0].shape[1]
    scratch = [pltpu.VMEM((depth, width), jnp.bfloat16), pltpu.SemaphoreType.DMA((2,))]
    return pl.pallas_call(
        functools.partial(kernel, section),
        out_shape=jax.ShapeDtypeStruct((rows, columns), jnp.bfloat16),
        in_specs=[IN_SMEM]
        + [IN_VMEM] * len(operands)
        + [IN_PLACE if fetch else IN_VMEM] * len(weights),
        out_specs=IN_VMEM,
        scratch_shapes=scratch if fetch else [],
        compiler_params=LIMIT,
        cost_estimate=cost(2 * rows * depth * width, 2 * depth * width),
    )(place, *operands, *weights)


def attend_kernel(width, section, place_ref, choice_ref, tiles_ref, length_ref, packed_ref, *refs):
    *blocks, result_ref, held = refs
    for distance, block_ref in enumerate(blocks):

        @pl.when(place_ref[0] ^ section == distance)
        def _():
            held[...] = block_ref[...]

    sources, rows, columns = packed_ref.shape
    heads = (columns - LANES) // HD
    keys = held.shape[0]
    first = place_ref[0] * rows
    sample = first // TXT
    key = lax.broadcasted_iota(jnp.int32, (1, keys), 1)
    valid = jnp.where(key < tiles_ref[choice_ref[sample]] * TROWS, 1.0, 0.0)
    position = first - sample * TXT + lax.broadcasted_iota(jnp.int32, (rows, 1), 0)
    live = jnp.where(position < length_ref[sample], 1.0, 0.0)
    summed = packed_ref[0].astype(jnp.float32)
    for source in range(1, sources):
        summed += packed_ref[source].astype(jnp.float32)
    squares = summed[:, heads * HD : heads * HD + 1] + summed[:, heads * HD + 1 : heads * HD + 2]
    inverse = lax.rsqrt(squares / width + epsilon) * (float(HD) ** (-0.5))
    queries = jnp.concatenate(
        [summed[:, head * HD : (head + 1) * HD] * inverse for head in range(heads)], axis=0
    ).astype(jnp.bfloat16)
    scores = lax.dot_general(
        queries,
        held[:, :HD],
        (((1,), (1,)), ((), ())),
        preferred_element_type=jnp.float32,
    )
    weighted = jnp.exp(scores) * valid
    weights = (weighted / jnp.sum(weighted, axis=-1, keepdims=True)).astype(jnp.bfloat16)
    context = jnp.dot(weights, held[:, HD:], preferred_element_type=jnp.float32)
    for head in range(heads):
        part = (context[head * rows : (head + 1) * rows] * live).astype(jnp.bfloat16)
        for target in range(result_ref.shape[0]):
            result_ref[target, :, head * HD : (head + 1) * HD] = part


def attend(place, choice, tiles, lengths, packed, keyval, section, width):
    sources, rows, columns = packed.shape
    keys = keyval[0].shape[0]
    heads = (columns - LANES) // HD
    return pl.pallas_call(
        functools.partial(attend_kernel, width, section),
        out_shape=jax.ShapeDtypeStruct((sources, rows, heads * HD), jnp.bfloat16),
        in_specs=[IN_SMEM] * 4 + [IN_VMEM] * (1 + len(keyval)),
        out_specs=IN_VMEM,
        scratch_shapes=[pltpu.VMEM(keyval[0].shape, jnp.bfloat16)],
        compiler_params=LIMIT,
        cost_estimate=cost(4 * heads * rows * keys * HD, packed.size * 2, heads * rows * keys),
    )(place, choice, tiles, lengths, packed, *keyval)


def assemble_kernel(received_ref, result_ref):
    cores, phases, slots, rows, piece = received_ref.shape
    for phase in range(phases):
        for slot in range(slots):
            for core in range(cores):
                column = (slot * cores + core) * piece
                result_ref[0, phase * rows : (phase + 1) * rows, column : column + piece] = (
                    received_ref[core, phase, slot]
                )


def assemble(received):
    cores, phases, slots, rows, piece = received.shape
    return pl.pallas_call(
        assemble_kernel,
        out_shape=jax.ShapeDtypeStruct((1, phases * rows, slots * cores * piece), received.dtype),
        in_specs=[IN_VMEM],
        out_specs=IN_VMEM,
        compiler_params=LIMIT,
        cost_estimate=cost(0, 4 * received.size),
    )(received)


def shift(part, distance):
    phases = lax.axis_size("phase")
    return lax.ppermute(part, "phase", [(i, i ^ distance) for i in range(phases)])


def bring_near(first, second):
    near_first, far_first = shift(first, 1), shift(first, 2)
    near_second, far_second = shift(second, 1), shift(second, 2)
    return first, second, near_first, near_second, far_first, far_second


def bring_across(parts, near_second, far_first):
    return *parts, shift(far_first, 1), shift(near_second, 2)


def exchange(block, axes):
    return lax.all_to_all(block, axes, 0, 0, tiled=True)


def on_device(
    text_rows,
    image_rows,
    tile_counts,
    text_lengths,
    sample_image,
    norm_gain,
    query_weight,
    keyval_weight,
    output_weight,
    cross_gate,
):
    phases, dps, mps = (lax.axis_size(name) for name in ("phase", "dp", "mp"))
    phase_index = lax.axis_index("phase")
    width = norm_gain.shape[1]
    own_rows = text_rows.shape[0]
    part_rows = own_rows // phases
    depth, head_width = query_weight.shape[1:]
    slots = dps // mps
    piece = depth // mps
    context_part = output_weight.shape[1]

    def spread(own_part):
        return lax.all_gather(own_part, "mp", axis=1, tiled=True)

    images = jnp.broadcast_to(image_rows[None], (phases,) + image_rows.shape)
    images = exchange(images, "phase")
    gain = lax.dynamic_slice_in_dim(norm_gain[0], lax.axis_index("dp") * depth, depth, 0)
    middle = depth // 2
    wq = [
        (query_weight[0, rows].astype(jnp.float32) * gain[rows, None]).astype(jnp.bfloat16)
        for rows in (slice(0, middle), slice(middle, depth))
    ]
    mine = lax.dynamic_slice_in_dim(text_rows, phase_index * part_rows, part_rows, 0)
    wo = jnp.concatenate([output_weight[0], mine], axis=0)
    wo = wo.reshape(-1, slots, mps, piece).transpose(2, 1, 0, 3).reshape(mps, -1, piece)
    images, wo = lax.optimization_barrier((images, wo))
    wq_parts = bring_near(*wq)
    wo = exchange(exchange(wo, "mp").reshape(dps, context_part + part_rows, piece), "dp")

    place = jnp.full((1,), phase_index, jnp.int32)
    images = lax.all_gather(images, "mp", axis=2, tiled=True)
    keyval = project_keyval(
        part_rows, place, sample_image, cross_gate, images, keyval_weight[0, :, 0, :]
    )
    wq = bring_across(wq_parts, *wq_parts[3:5])
    keyval, _ = lax.optimization_barrier((keyval, wq_parts[2:6]))
    keyval = [shift(keyval[k], k) if k else keyval[k] for k in range(phases)]
    wo, keyval = lax.optimization_barrier((wo, keyval))
    middle = dps // 2
    own = wo[:, context_part:].reshape(dps * part_rows, piece)
    wo = wo[:, :context_part]
    wo_parts = bring_near(wo[:middle].reshape(-1, piece), wo[middle:].reshape(-1, piece))
    carried = spread(own)


    packed_width = head_width + LANES
    packed = project(query_kernel, place, [carried], wq, 0, packed_width)
    packed = exchange(packed.reshape(dps, part_rows, packed_width), "dp")
    forward, _ = lax.optimization_barrier((wo_parts[3:5], packed))
    wo = bring_across(wo_parts, *forward)
    later = range(1, phases)
    wq_later, wo_later = arrange(place, wq, later), arrange(place, wo, later)
    states = []
    for section in range(phases):
        if section:
            carried = spread(own)
            weights = [wq_later[section - 1]]
            packed = project(query_kernel, place, [carried], weights, None, packed_width)
            packed = exchange(packed.reshape(dps, part_rows, packed_width), "dp")
        context = attend(
            place, sample_image, tile_counts, text_lengths, packed, keyval, section, width
        )
        context = spread(exchange(context, "dp").reshape(dps * part_rows, head_width))
        if section == 0:
            own = project(output_kernel, place, [context, own], wo, 0, piece)
        else:
            weights = [wo_later[section - 1]]
            own = project(output_kernel, place, [context, own], weights, None, piece)
        states.append(own)
    result = jnp.stack(states).reshape(phases * dps, part_rows, piece)
    result = exchange(result, ("phase", "dp")).reshape(phases, mps, slots, part_rows, piece)
    return assemble(exchange(result.transpose(1, 0, 2, 3, 4), "mp"))


def solution(mesh):
    placed = (
        P("dp", "mp"),
        P("dp", ("phase", "mp"), None),
        P("dp"),
        P("dp"),
        P("dp"),
        P("phase", None),
        P("phase", "dp", "mp"),
        P("phase", None, "mp", None),
        P("phase", "dp", "mp"),
        P("phase"),
    )
    return jax.shard_map(
        on_device, mesh=mesh, in_specs=placed, out_specs=P("phase", "dp", "mp"), check_vma=False
    )
```

```python
import functools

import jax
import jax.numpy as jnp
from jax import lax
from jax.experimental import pallas as pl
from jax.experimental.pallas import tpu as pltpu
from jax.sharding import PartitionSpec as P

HD = 128
HQ_DEV = 4
TROWS = 32
SAMP = 2
TXT = 64
LANES = 128

epsilon = 1e-05
IN_VMEM = pl.BlockSpec(memory_space=pltpu.VMEM)
IN_PLACE = pl.BlockSpec(memory_space=pl.ANY)
IN_SMEM = pl.BlockSpec(memory_space=pltpu.SMEM)
LIMIT = pltpu.CompilerParams(vmem_limit_bytes=24 * 2**20)


def cost(flops, bytes_accessed, transcendentals=0):
    return pl.CostEstimate(
        flops=flops, bytes_accessed=bytes_accessed, transcendentals=transcendentals
    )


def keyval_kernel(part_rows, place_ref, choice_ref, gate_ref, images_ref, weight_ref, *refs):
    *result_refs, held = refs
    phases, count = images_ref.shape[:2]
    factor = jnp.tanh(jnp.full((1, HD), gate_ref[0], jnp.float32))
    for image in range(count):
        rows = jnp.concatenate([images_ref[phase, image] for phase in range(phases)], axis=0)
        both = jnp.dot(rows, weight_ref[...], preferred_element_type=jnp.float32)
        held[image, :, :HD] = both[:, :HD].astype(jnp.bfloat16)
        held[image, :, HD:] = (both[:, HD:] * factor).astype(jnp.bfloat16)
    for distance, result_ref in enumerate(result_refs):
        sample = (place_ref[0] ^ distance) * part_rows // TXT
        result_ref[...] = held[choice_ref[sample]]


def project_keyval(part_rows, place, choice, gate, images, weight):
    phases, count, rows, depth = images.shape
    keys = phases * rows
    block = jax.ShapeDtypeStruct((keys, 2 * HD), jnp.bfloat16)
    return pl.pallas_call(
        functools.partial(keyval_kernel, part_rows),
        out_shape=[block] * phases,
        in_specs=[IN_SMEM, IN_SMEM, IN_SMEM, IN_VMEM, IN_VMEM],
        out_specs=[IN_VMEM] * phases,
        scratch_shapes=[pltpu.VMEM((count, keys, 2 * HD), jnp.bfloat16)],
        compiler_params=LIMIT,
        cost_estimate=cost(4 * count * keys * depth * HD, 2 * images.size + 2 * weight.size),
    )(place, choice, gate, images, weight)


def start_copy(distance, blocks, target, sems):
    half = target.shape[0] // 2
    for step in range(len(blocks) // 2):

        @pl.when(distance == step)
        def _():
            pltpu.make_async_copy(blocks[2 * step], target.at[:half], sems.at[0]).start()
            pltpu.make_async_copy(blocks[2 * step + 1], target.at[half:], sems.at[1]).start()


def wait_copy(blocks, target, sems):
    half = target.shape[0] // 2
    pltpu.make_async_copy(blocks[0], target.at[:half], sems.at[0]).wait()
    pltpu.make_async_copy(blocks[1], target.at[half:], sems.at[1]).wait()


def arrange_kernel(sections, place_ref, *refs):
    blocks, targets, sems = refs[: -len(sections) - 1], refs[-len(sections) - 1 : -1], refs[-1]
    for step, section in enumerate(sections):
        start_copy(place_ref[0] ^ section, blocks, targets[step], sems.at[step])
    for step in range(len(sections)):
        wait_copy(blocks, targets[step], sems.at[step])


def arrange(place, blocks, sections):
    half, columns = blocks[0].shape
    whole = jax.ShapeDtypeStruct((2 * half, columns), jnp.bfloat16)
    return pl.pallas_call(
        functools.partial(arrange_kernel, sections),
        out_shape=[whole] * len(sections),
        in_specs=[IN_SMEM] + [IN_PLACE] * len(blocks),
        out_specs=[IN_PLACE] * len(sections),
        scratch_shapes=[pltpu.SemaphoreType.DMA((len(sections), 2))],
        compiler_params=LIMIT,
        cost_estimate=cost(0, 8 * half * columns * len(sections)),
    )(place, *blocks)


def query_kernel(section, place_ref, x_ref, *refs):
    if section is None:
        weight_ref, packed_ref = refs
    else:
        *blocks, packed_ref, weight_ref, sems = refs
        start_copy(place_ref[0] ^ section, blocks, weight_ref, sems)
    width = weight_ref.shape[1]
    wide = x_ref[...].astype(jnp.float32)
    squares = jnp.sum(wide * wide, axis=-1, keepdims=True)
    high = squares.astype(jnp.bfloat16).astype(jnp.float32)
    lane = lax.broadcasted_iota(jnp.int32, (x_ref.shape[0], LANES), 1)
    extra = jnp.where(lane == 0, high, jnp.where(lane == 1, squares - high, 0.0))
    packed_ref[:, width:] = extra.astype(jnp.bfloat16)
    if section is not None:
        wait_copy(blocks, weight_ref, sems)
    total = jnp.dot(x_ref[...], weight_ref[...], preferred_element_type=jnp.float32)
    packed_ref[:, :width] = total.astype(jnp.bfloat16)


def output_kernel(section, place_ref, context_ref, own_ref, *refs):
    if section is None:
        weight_ref, result_ref = refs
    else:
        *blocks, result_ref, weight_ref, sems = refs
        start_copy(place_ref[0] ^ section, blocks, weight_ref, sems)
        wait_copy(blocks, weight_ref, sems)
    total = own_ref[...].astype(jnp.float32)
    total += jnp.dot(context_ref[...], weight_ref[...], preferred_element_type=jnp.float32)
    result_ref[...] = total.astype(jnp.bfloat16)


def project(kernel, place, operands, weights, section, columns):
    rows = operands[0].shape[0]
    fetch = section is not None
    depth = weights[0].shape[0] * (2 if fetch else 1)
    width = weights[0].shape[1]
    scratch = [pltpu.VMEM((depth, width), jnp.bfloat16), pltpu.SemaphoreType.DMA((2,))]
    return pl.pallas_call(
        functools.partial(kernel, section),
        out_shape=jax.ShapeDtypeStruct((rows, columns), jnp.bfloat16),
        in_specs=[IN_SMEM]
        + [IN_VMEM] * len(operands)
        + [IN_PLACE if fetch else IN_VMEM] * len(weights),
        out_specs=IN_VMEM,
        scratch_shapes=scratch if fetch else [],
        compiler_params=LIMIT,
        cost_estimate=cost(2 * rows * depth * width, 2 * depth * width),
    )(place, *operands, *weights)


def attend_kernel(width, section, place_ref, choice_ref, tiles_ref, length_ref, packed_ref, *refs):
    *blocks, result_ref, held = refs
    for distance, block_ref in enumerate(blocks):

        @pl.when(place_ref[0] ^ section == distance)
        def _():
            held[...] = block_ref[...]

    sources, rows, columns = packed_ref.shape
    heads = (columns - LANES) // HD
    keys = held.shape[0]
    first = place_ref[0] * rows
    sample = first // TXT
    key = lax.broadcasted_iota(jnp.int32, (1, keys), 1)
    valid = jnp.where(key < tiles_ref[choice_ref[sample]] * TROWS, 1.0, 0.0)
    position = first - sample * TXT + lax.broadcasted_iota(jnp.int32, (rows, 1), 0)
    live = jnp.where(position < length_ref[sample], 1.0, 0.0)
    summed = packed_ref[0].astype(jnp.float32)
    for source in range(1, sources):
        summed += packed_ref[source].astype(jnp.float32)
    squares = summed[:, heads * HD : heads * HD + 1] + summed[:, heads * HD + 1 : heads * HD + 2]
    inverse = lax.rsqrt(squares / width + epsilon) * (float(HD) ** (-0.5))
    queries = jnp.concatenate(
        [summed[:, head * HD : (head + 1) * HD] * inverse for head in range(heads)], axis=0
    ).astype(jnp.bfloat16)
    scores = lax.dot_general(
        queries,
        held[:, :HD],
        (((1,), (1,)), ((), ())),
        preferred_element_type=jnp.float32,
    )
    weighted = jnp.exp(scores) * valid
    weights = (weighted / jnp.sum(weighted, axis=-1, keepdims=True)).astype(jnp.bfloat16)
    context = jnp.dot(weights, held[:, HD:], preferred_element_type=jnp.float32)
    for head in range(heads):
        part = (context[head * rows : (head + 1) * rows] * live).astype(jnp.bfloat16)
        for target in range(result_ref.shape[0]):
            result_ref[target, :, head * HD : (head + 1) * HD] = part


def attend(place, choice, tiles, lengths, packed, keyval, section, width):
    sources, rows, columns = packed.shape
    keys = keyval[0].shape[0]
    heads = (columns - LANES) // HD
    return pl.pallas_call(
        functools.partial(attend_kernel, width, section),
        out_shape=jax.ShapeDtypeStruct((sources, rows, heads * HD), jnp.bfloat16),
        in_specs=[IN_SMEM] * 4 + [IN_VMEM] * (1 + len(keyval)),
        out_specs=IN_VMEM,
        scratch_shapes=[pltpu.VMEM(keyval[0].shape, jnp.bfloat16)],
        compiler_params=LIMIT,
        cost_estimate=cost(4 * heads * rows * keys * HD, packed.size * 2, heads * rows * keys),
    )(place, choice, tiles, lengths, packed, *keyval)


def assemble_kernel(received_ref, result_ref):
    cores, phases, slots, rows, piece = received_ref.shape
    for phase in range(phases):
        for slot in range(slots):
            for core in range(cores):
                column = (slot * cores + core) * piece
                result_ref[0, phase * rows : (phase + 1) * rows, column : column + piece] = (
                    received_ref[core, phase, slot]
                )


def assemble(received):
    cores, phases, slots, rows, piece = received.shape
    return pl.pallas_call(
        assemble_kernel,
        out_shape=jax.ShapeDtypeStruct((1, phases * rows, slots * cores * piece), received.dtype),
        in_specs=[IN_VMEM],
        out_specs=IN_VMEM,
        compiler_params=LIMIT,
        cost_estimate=cost(0, 4 * received.size),
    )(received)


def shift(part, distance):
    phases = lax.axis_size("phase")
    return lax.ppermute(part, "phase", [(i, i ^ distance) for i in range(phases)])


def bring_near(first, second):
    near_first, far_first = shift(first, 1), shift(first, 2)
    near_second, far_second = shift(second, 1), shift(second, 2)
    return first, second, near_first, near_second, far_first, far_second


def bring_across(parts, near_second, far_first):
    return *parts, shift(far_first, 1), shift(near_second, 2)


def exchange(block, axes):
    return lax.all_to_all(block, axes, 0, 0, tiled=True)


def on_device(
    text_rows,
    image_rows,
    tile_counts,
    text_lengths,
    sample_image,
    norm_gain,
    query_weight,
    keyval_weight,
    output_weight,
    cross_gate,
):
    phases, dps, mps = (lax.axis_size(name) for name in ("phase", "dp", "mp"))
    phase_index = lax.axis_index("phase")
    width = norm_gain.shape[1]
    own_rows = text_rows.shape[0]
    part_rows = own_rows // phases
    depth, head_width = query_weight.shape[1:]
    slots = dps // mps
    piece = depth // mps
    context_part = output_weight.shape[1]

    def spread(own_part):
        return lax.all_gather(own_part, "mp", axis=1, tiled=True)

    images = jnp.broadcast_to(image_rows[None], (phases,) + image_rows.shape)
    images = exchange(images, "phase")
    gain = lax.dynamic_slice_in_dim(norm_gain[0], lax.axis_index("dp") * depth, depth, 0)
    middle = depth // 2
    wq = [
        (query_weight[0, rows].astype(jnp.float32) * gain[rows, None]).astype(jnp.bfloat16)
        for rows in (slice(0, middle), slice(middle, depth))
    ]
    mine = lax.dynamic_slice_in_dim(text_rows, phase_index * part_rows, part_rows, 0)
    wo = jnp.concatenate([output_weight[0], mine], axis=0)
    wo = wo.reshape(-1, slots, mps, piece).transpose(2, 1, 0, 3).reshape(mps, -1, piece)
    images, wq = lax.optimization_barrier((images, wq))
    wq_parts = bring_near(*wq)
    wo = exchange(exchange(wo, "mp").reshape(dps, context_part + part_rows, piece), "dp")

    place = jnp.full((1,), phase_index, jnp.int32)
    images = lax.all_gather(images, "mp", axis=2, tiled=True)
    keyval = project_keyval(
        part_rows, place, sample_image, cross_gate, images, keyval_weight[0, :, 0, :]
    )
    wq = bring_across(wq_parts, *wq_parts[3:5])
    keyval, _ = lax.optimization_barrier((keyval, wq_parts[2:6]))
    keyval = [shift(keyval[k], k) if k else keyval[k] for k in range(phases)]
    wo, keyval = lax.optimization_barrier((wo, keyval))
    middle = dps // 2
    own = wo[:, context_part:].reshape(dps * part_rows, piece)
    wo = wo[:, :context_part]
    wo_parts = bring_near(wo[:middle].reshape(-1, piece), wo[middle:].reshape(-1, piece))
    carried = spread(own)


    packed_width = head_width + LANES
    packed = project(query_kernel, place, [carried], wq, 0, packed_width)
    packed = exchange(packed.reshape(dps, part_rows, packed_width), "dp")
    forward, _ = lax.optimization_barrier((wo_parts[3:5], packed))
    wo = bring_across(wo_parts, *forward)
    later = range(1, phases)
    wq_later, wo_later = arrange(place, wq, later), arrange(place, wo, later)
    states = []
    for section in range(phases):
        if section:
            carried = spread(own)
            weights = [wq_later[section - 1]]
            packed = project(query_kernel, place, [carried], weights, None, packed_width)
            packed = exchange(packed.reshape(dps, part_rows, packed_width), "dp")
        context = attend(
            place, sample_image, tile_counts, text_lengths, packed, keyval, section, width
        )
        context = spread(exchange(context, "dp").reshape(dps * part_rows, head_width))
        if section == 0:
            own = project(output_kernel, place, [context, own], wo, 0, piece)
        else:
            weights = [wo_later[section - 1]]
            own = project(output_kernel, place, [context, own], weights, None, piece)
        states.append(own)
    result = jnp.stack(states).reshape(phases * dps, part_rows, piece)
    result = exchange(result, ("phase", "dp")).reshape(phases, mps, slots, part_rows, piece)
    return assemble(exchange(result.transpose(1, 0, 2, 3, 4), "mp"))


def solution(mesh):
    placed = (
        P("dp", "mp"),
        P("dp", ("phase", "mp"), None),
        P("dp"),
        P("dp"),
        P("dp"),
        P("phase", None),
        P("phase", "dp", "mp"),
        P("phase", None, "mp", None),
        P("phase", "dp", "mp"),
        P("phase"),
    )
    return jax.shard_map(
        on_device, mesh=mesh, in_specs=placed, out_specs=P("phase", "dp", "mp"), check_vma=False
    )
```

```python
import functools

import jax
import jax.numpy as jnp
from jax import lax
from jax.experimental import pallas as pl
from jax.experimental.pallas import tpu as pltpu
from jax.sharding import PartitionSpec as P

HD = 128
HQ_DEV = 4
TROWS = 32
SAMP = 2
TXT = 64
LANES = 128

epsilon = 1e-05
IN_VMEM = pl.BlockSpec(memory_space=pltpu.VMEM)
IN_PLACE = pl.BlockSpec(memory_space=pl.ANY)
IN_SMEM = pl.BlockSpec(memory_space=pltpu.SMEM)
LIMIT = pltpu.CompilerParams(vmem_limit_bytes=24 * 2**20)


def cost(flops, bytes_accessed, transcendentals=0):
    return pl.CostEstimate(
        flops=flops, bytes_accessed=bytes_accessed, transcendentals=transcendentals
    )


def keyval_kernel(part_rows, place_ref, choice_ref, gate_ref, images_ref, weight_ref, *refs):
    *result_refs, held = refs
    phases, count, part = images_ref.shape[:3]
    factor = jnp.tanh(jnp.full((1, HD), gate_ref[0], jnp.float32))
    for image in range(count):
        rows = jnp.concatenate([images_ref[phase, image] for phase in range(phases)], axis=0)
        both = jnp.dot(rows, weight_ref[...], preferred_element_type=jnp.float32)
        keys = both[:, :HD].astype(jnp.bfloat16)
        values = (both[:, HD:] * factor).astype(jnp.bfloat16)
        for distance in range(phases):
            source = slice(distance * part, (distance + 1) * part)
            first = pl.multiple_of((place_ref[0] ^ distance) * part, part)
            held[image, pl.ds(first, part), :HD] = keys[source]
            held[image, pl.ds(first, part), HD:] = values[source]
    for distance, result_ref in enumerate(result_refs):
        sample = (place_ref[0] ^ distance) * part_rows // TXT
        result_ref[...] = held[choice_ref[sample]]


def project_keyval(part_rows, place, choice, gate, images, weight):
    phases, count, rows, depth = images.shape
    keys = phases * rows
    block = jax.ShapeDtypeStruct((keys, 2 * HD), jnp.bfloat16)
    return pl.pallas_call(
        functools.partial(keyval_kernel, part_rows),
        out_shape=[block] * phases,
        in_specs=[IN_SMEM, IN_SMEM, IN_SMEM, IN_VMEM, IN_VMEM],
        out_specs=[IN_VMEM] * phases,
        scratch_shapes=[pltpu.VMEM((count, keys, 2 * HD), jnp.bfloat16)],
        compiler_params=LIMIT,
        cost_estimate=cost(4 * count * keys * depth * HD, 2 * images.size + 2 * weight.size),
    )(place, choice, gate, images, weight)


def start_copy(distance, blocks, target, sems):
    half = target.shape[0] // 2
    for step in range(len(blocks) // 2):

        @pl.when(distance == step)
        def _():
            pltpu.make_async_copy(blocks[2 * step], target.at[:half], sems.at[0]).start()
            pltpu.make_async_copy(blocks[2 * step + 1], target.at[half:], sems.at[1]).start()


def wait_copy(blocks, target, sems):
    half = target.shape[0] // 2
    pltpu.make_async_copy(blocks[0], target.at[:half], sems.at[0]).wait()
    pltpu.make_async_copy(blocks[1], target.at[half:], sems.at[1]).wait()


def arrange_kernel(sections, place_ref, *refs):
    blocks, targets, sems = refs[: -len(sections) - 1], refs[-len(sections) - 1 : -1], refs[-1]
    for step, section in enumerate(sections):
        start_copy(place_ref[0] ^ section, blocks, targets[step], sems.at[step])
    for step in range(len(sections)):
        wait_copy(blocks, targets[step], sems.at[step])


def arrange(place, blocks, sections):
    half, columns = blocks[0].shape
    whole = jax.ShapeDtypeStruct((2 * half, columns), jnp.bfloat16)
    return pl.pallas_call(
        functools.partial(arrange_kernel, sections),
        out_shape=[whole] * len(sections),
        in_specs=[IN_SMEM] + [IN_PLACE] * len(blocks),
        out_specs=[IN_PLACE] * len(sections),
        scratch_shapes=[pltpu.SemaphoreType.DMA((len(sections), 2))],
        compiler_params=LIMIT,
        cost_estimate=cost(0, 8 * half * columns * len(sections)),
    )(place, *blocks)


def query_kernel(section, place_ref, x_ref, *refs):
    if section is None:
        weight_ref, packed_ref = refs
    else:
        *blocks, packed_ref, weight_ref, sems = refs
        start_copy(place_ref[0] ^ section, blocks, weight_ref, sems)
    width = weight_ref.shape[1]
    wide = x_ref[...].astype(jnp.float32)
    squares = jnp.sum(wide * wide, axis=-1, keepdims=True)
    high = squares.astype(jnp.bfloat16).astype(jnp.float32)
    lane = lax.broadcasted_iota(jnp.int32, (x_ref.shape[0], LANES), 1)
    extra = jnp.where(lane == 0, high, jnp.where(lane == 1, squares - high, 0.0))
    packed_ref[:, width:] = extra.astype(jnp.bfloat16)
    if section is not None:
        wait_copy(blocks, weight_ref, sems)
    total = jnp.dot(x_ref[...], weight_ref[...], preferred_element_type=jnp.float32)
    packed_ref[:, :width] = total.astype(jnp.bfloat16)


def output_kernel(section, place_ref, context_ref, own_ref, *refs):
    if section is None:
        weight_ref, result_ref = refs
    else:
        *blocks, result_ref, weight_ref, sems = refs
        start_copy(place_ref[0] ^ section, blocks, weight_ref, sems)
        wait_copy(blocks, weight_ref, sems)
    total = own_ref[...].astype(jnp.float32)
    total += jnp.dot(context_ref[...], weight_ref[...], preferred_element_type=jnp.float32)
    result_ref[...] = total.astype(jnp.bfloat16)


def project(kernel, place, operands, weights, section, columns):
    rows = operands[0].shape[0]
    fetch = section is not None
    depth = weights[0].shape[0] * (2 if fetch else 1)
    width = weights[0].shape[1]
    scratch = [pltpu.VMEM((depth, width), jnp.bfloat16), pltpu.SemaphoreType.DMA((2,))]
    return pl.pallas_call(
        functools.partial(kernel, section),
        out_shape=jax.ShapeDtypeStruct((rows, columns), jnp.bfloat16),
        in_specs=[IN_SMEM]
        + [IN_VMEM] * len(operands)
        + [IN_PLACE if fetch else IN_VMEM] * len(weights),
        out_specs=IN_VMEM,
        scratch_shapes=scratch if fetch else [],
        compiler_params=LIMIT,
        cost_estimate=cost(2 * rows * depth * width, 2 * depth * width),
    )(place, *operands, *weights)


def attend_kernel(width, section, place_ref, choice_ref, tiles_ref, length_ref, packed_ref, *refs):
    *blocks, result_ref, held = refs
    for distance, block_ref in enumerate(blocks):

        @pl.when(place_ref[0] ^ section == distance)
        def _():
            held[...] = block_ref[...]

    sources, rows, columns = packed_ref.shape
    heads = (columns - LANES) // HD
    keys = held.shape[0]
    first = place_ref[0] * rows
    sample = first // TXT
    key = lax.broadcasted_iota(jnp.int32, (1, keys), 1)
    valid = jnp.where(key < tiles_ref[choice_ref[sample]] * TROWS, 1.0, 0.0)
    position = first - sample * TXT + lax.broadcasted_iota(jnp.int32, (rows, 1), 0)
    live = jnp.where(position < length_ref[sample], 1.0, 0.0)
    summed = packed_ref[0].astype(jnp.float32)
    for source in range(1, sources):
        summed += packed_ref[source].astype(jnp.float32)
    squares = summed[:, heads * HD : heads * HD + 1] + summed[:, heads * HD + 1 : heads * HD + 2]
    inverse = lax.rsqrt(squares / width + epsilon) * (float(HD) ** (-0.5))
    queries = jnp.concatenate(
        [summed[:, head * HD : (head + 1) * HD] * inverse for head in range(heads)], axis=0
    ).astype(jnp.bfloat16)
    scores = lax.dot_general(
        queries,
        held[:, :HD],
        (((1,), (1,)), ((), ())),
        preferred_element_type=jnp.float32,
    )
    weighted = jnp.exp(scores) * valid
    weights = (weighted / jnp.sum(weighted, axis=-1, keepdims=True)).astype(jnp.bfloat16)
    context = jnp.dot(weights, held[:, HD:], preferred_element_type=jnp.float32)
    for head in range(heads):
        part = (context[head * rows : (head + 1) * rows] * live).astype(jnp.bfloat16)
        for target in range(result_ref.shape[0]):
            result_ref[target, :, head * HD : (head + 1) * HD] = part


def attend(place, choice, tiles, lengths, packed, keyval, section, width):
    sources, rows, columns = packed.shape
    keys = keyval[0].shape[0]
    heads = (columns - LANES) // HD
    return pl.pallas_call(
        functools.partial(attend_kernel, width, section),
        out_shape=jax.ShapeDtypeStruct((sources, rows, heads * HD), jnp.bfloat16),
        in_specs=[IN_SMEM] * 4 + [IN_VMEM] * (1 + len(keyval)),
        out_specs=IN_VMEM,
        scratch_shapes=[pltpu.VMEM(keyval[0].shape, jnp.bfloat16)],
        compiler_params=LIMIT,
        cost_estimate=cost(4 * heads * rows * keys * HD, packed.size * 2, heads * rows * keys),
    )(place, choice, tiles, lengths, packed, *keyval)


def assemble_kernel(received_ref, result_ref):
    cores, phases, slots, rows, piece = received_ref.shape
    for phase in range(phases):
        for slot in range(slots):
            for core in range(cores):
                column = (slot * cores + core) * piece
                result_ref[0, phase * rows : (phase + 1) * rows, column : column + piece] = (
                    received_ref[core, phase, slot]
                )


def assemble(received):
    cores, phases, slots, rows, piece = received.shape
    return pl.pallas_call(
        assemble_kernel,
        out_shape=jax.ShapeDtypeStruct((1, phases * rows, slots * cores * piece), received.dtype),
        in_specs=[IN_VMEM],
        out_specs=IN_VMEM,
        compiler_params=LIMIT,
        cost_estimate=cost(0, 4 * received.size),
    )(received)


def shift(part, distance):
    phases = lax.axis_size("phase")
    return lax.ppermute(part, "phase", [(i, i ^ distance) for i in range(phases)])


def bring_near(first, second):
    near_first, far_first = shift(first, 1), shift(first, 2)
    near_second, far_second = shift(second, 1), shift(second, 2)
    return first, second, near_first, near_second, far_first, far_second


def bring_across(parts, near_second, far_first):
    return *parts, shift(far_first, 1), shift(near_second, 2)


def exchange(block, axes):
    return lax.all_to_all(block, axes, 0, 0, tiled=True)


def on_device(
    text_rows,
    image_rows,
    tile_counts,
    text_lengths,
    sample_image,
    norm_gain,
    query_weight,
    keyval_weight,
    output_weight,
    cross_gate,
):
    phases, dps, mps = (lax.axis_size(name) for name in ("phase", "dp", "mp"))
    phase_index = lax.axis_index("phase")
    width = norm_gain.shape[1]
    own_rows = text_rows.shape[0]
    part_rows = own_rows // phases
    depth, head_width = query_weight.shape[1:]
    slots = dps // mps
    piece = depth // mps
    context_part = output_weight.shape[1]

    def spread(own_part):
        return lax.all_gather(own_part, "mp", axis=1, tiled=True)

    images = [shift(image_rows, k) if k else image_rows for k in range(phases)]
    gain = lax.dynamic_slice_in_dim(norm_gain[0], lax.axis_index("dp") * depth, depth, 0)
    middle = depth // 2
    wq = [
        (query_weight[0, rows].astype(jnp.float32) * gain[rows, None]).astype(jnp.bfloat16)
        for rows in (slice(0, middle), slice(middle, depth))
    ]
    mine = lax.dynamic_slice_in_dim(text_rows, phase_index * part_rows, part_rows, 0)
    wo = jnp.concatenate([output_weight[0], mine], axis=0)
    wo = wo.reshape(-1, slots, mps, piece).transpose(2, 1, 0, 3).reshape(mps, -1, piece)
    images, wq, wo = lax.optimization_barrier((images, wq, wo))
    wq_parts = bring_near(*wq)
    wo = exchange(exchange(wo, "mp").reshape(dps, context_part + part_rows, piece), "dp")

    place = jnp.full((1,), phase_index, jnp.int32)
    images = lax.all_gather(jnp.stack(images), "mp", axis=2, tiled=True)
    keyval = project_keyval(
        part_rows, place, sample_image, cross_gate, images, keyval_weight[0, :, 0, :]
    )
    wq = bring_across(wq_parts, *wq_parts[3:5])
    keyval, _ = lax.optimization_barrier((keyval, wq_parts[2:6]))
    keyval = [shift(keyval[k], k) if k else keyval[k] for k in range(phases)]
    wo, keyval = lax.optimization_barrier((wo, keyval))
    middle = dps // 2
    own = wo[:, context_part:].reshape(dps * part_rows, piece)
    wo = wo[:, :context_part]
    wo_parts = bring_near(wo[:middle].reshape(-1, piece), wo[middle:].reshape(-1, piece))
    carried = spread(own)


    packed_width = head_width + LANES
    packed = project(query_kernel, place, [carried], wq, 0, packed_width)
    packed = exchange(packed.reshape(dps, part_rows, packed_width), "dp")
    forward, _ = lax.optimization_barrier((wo_parts[3:5], packed))
    wo = bring_across(wo_parts, *forward)
    later = range(1, phases)
    wq_later, wo_later = arrange(place, wq, later), arrange(place, wo, later)
    states = []
    for section in range(phases):
        if section:
            carried = spread(own)
            weights = [wq_later[section - 1]]
            packed = project(query_kernel, place, [carried], weights, None, packed_width)
            packed = exchange(packed.reshape(dps, part_rows, packed_width), "dp")
        context = attend(
            place, sample_image, tile_counts, text_lengths, packed, keyval, section, width
        )
        context = spread(exchange(context, "dp").reshape(dps * part_rows, head_width))
        if section == 0:
            own = project(output_kernel, place, [context, own], wo, 0, piece)
        else:
            weights = [wo_later[section - 1]]
            own = project(output_kernel, place, [context, own], weights, None, piece)
        states.append(own)
    result = jnp.stack(states).reshape(phases * dps, part_rows, piece)
    result = exchange(result, ("phase", "dp")).reshape(phases, mps, slots, part_rows, piece)
    return assemble(exchange(result.transpose(1, 0, 2, 3, 4), "mp"))


def solution(mesh):
    placed = (
        P("dp", "mp"),
        P("dp", ("phase", "mp"), None),
        P("dp"),
        P("dp"),
        P("dp"),
        P("phase", None),
        P("phase", "dp", "mp"),
        P("phase", None, "mp", None),
        P("phase", "dp", "mp"),
        P("phase"),
    )
    return jax.shard_map(
        on_device, mesh=mesh, in_specs=placed, out_specs=P("phase", "dp", "mp"), check_vma=False
    )
```

```python
import functools

import jax
import jax.numpy as jnp
from jax import lax
from jax.experimental import pallas as pl
from jax.experimental.pallas import tpu as pltpu
from jax.sharding import PartitionSpec as P

HD = 128
HQ_DEV = 4
TROWS = 32
SAMP = 2
TXT = 64
LANES = 128

epsilon = 1e-05
IN_VMEM = pl.BlockSpec(memory_space=pltpu.VMEM)
IN_PLACE = pl.BlockSpec(memory_space=pl.ANY)
IN_SMEM = pl.BlockSpec(memory_space=pltpu.SMEM)
LIMIT = pltpu.CompilerParams(vmem_limit_bytes=24 * 2**20)


def cost(flops, bytes_accessed, transcendentals=0):
    return pl.CostEstimate(
        flops=flops, bytes_accessed=bytes_accessed, transcendentals=transcendentals
    )


def keyval_kernel(part_rows, place_ref, choice_ref, gate_ref, images_ref, weight_ref, *refs):
    *result_refs, held = refs
    phases, count, part = images_ref.shape[:3]
    factor = jnp.tanh(jnp.full((1, HD), gate_ref[0], jnp.float32))
    for image in range(count):
        rows = jnp.concatenate([images_ref[phase, image] for phase in range(phases)], axis=0)
        both = jnp.dot(rows, weight_ref[...], preferred_element_type=jnp.float32)
        keys = both[:, :HD].astype(jnp.bfloat16)
        values = (both[:, HD:] * factor).astype(jnp.bfloat16)
        for distance in range(phases):
            source = slice(distance * part, (distance + 1) * part)
            first = pl.multiple_of((place_ref[0] ^ distance) * part, part)
            held[image, pl.ds(first, part), :HD] = keys[source]
            held[image, pl.ds(first, part), HD:] = values[source]
    for distance, result_ref in enumerate(result_refs):
        sample = (place_ref[0] ^ distance) * part_rows // TXT
        result_ref[...] = held[choice_ref[sample]]


def project_keyval(part_rows, place, choice, gate, images, weight):
    phases, count, rows, depth = images.shape
    keys = phases * rows
    block = jax.ShapeDtypeStruct((keys, 2 * HD), jnp.bfloat16)
    return pl.pallas_call(
        functools.partial(keyval_kernel, part_rows),
        out_shape=[block] * phases,
        in_specs=[IN_SMEM, IN_SMEM, IN_SMEM, IN_VMEM, IN_VMEM],
        out_specs=[IN_VMEM] * phases,
        scratch_shapes=[pltpu.VMEM((count, keys, 2 * HD), jnp.bfloat16)],
        compiler_params=LIMIT,
        cost_estimate=cost(4 * count * keys * depth * HD, 2 * images.size + 2 * weight.size),
    )(place, choice, gate, images, weight)


def start_copy(distance, blocks, target, sems):
    half = target.shape[0] // 2
    for step in range(len(blocks) // 2):

        @pl.when(distance == step)
        def _():
            pltpu.make_async_copy(blocks[2 * step], target.at[:half], sems.at[0]).start()
            pltpu.make_async_copy(blocks[2 * step + 1], target.at[half:], sems.at[1]).start()


def wait_copy(blocks, target, sems):
    half = target.shape[0] // 2
    pltpu.make_async_copy(blocks[0], target.at[:half], sems.at[0]).wait()
    pltpu.make_async_copy(blocks[1], target.at[half:], sems.at[1]).wait()


def arrange_kernel(sections, place_ref, *refs):
    blocks, targets, sems = refs[: -len(sections) - 1], refs[-len(sections) - 1 : -1], refs[-1]
    for step, section in enumerate(sections):
        start_copy(place_ref[0] ^ section, blocks, targets[step], sems.at[step])
    for step in range(len(sections)):
        wait_copy(blocks, targets[step], sems.at[step])


def arrange(place, blocks, sections):
    half, columns = blocks[0].shape
    whole = jax.ShapeDtypeStruct((2 * half, columns), jnp.bfloat16)
    return pl.pallas_call(
        functools.partial(arrange_kernel, sections),
        out_shape=[whole] * len(sections),
        in_specs=[IN_SMEM] + [IN_PLACE] * len(blocks),
        out_specs=[IN_PLACE] * len(sections),
        scratch_shapes=[pltpu.SemaphoreType.DMA((len(sections), 2))],
        compiler_params=LIMIT,
        cost_estimate=cost(0, 8 * half * columns * len(sections)),
    )(place, *blocks)


def query_kernel(section, place_ref, x_ref, *refs):
    if section is None:
        weight_ref, packed_ref = refs
    else:
        *blocks, packed_ref, weight_ref, sems = refs
        start_copy(place_ref[0] ^ section, blocks, weight_ref, sems)
    width = weight_ref.shape[1]
    wide = x_ref[...].astype(jnp.float32)
    squares = jnp.sum(wide * wide, axis=-1, keepdims=True)
    high = squares.astype(jnp.bfloat16).astype(jnp.float32)
    lane = lax.broadcasted_iota(jnp.int32, (x_ref.shape[0], LANES), 1)
    extra = jnp.where(lane == 0, high, jnp.where(lane == 1, squares - high, 0.0))
    packed_ref[:, width:] = extra.astype(jnp.bfloat16)
    if section is not None:
        wait_copy(blocks, weight_ref, sems)
    total = jnp.dot(x_ref[...], weight_ref[...], preferred_element_type=jnp.float32)
    packed_ref[:, :width] = total.astype(jnp.bfloat16)


def output_kernel(section, place_ref, context_ref, own_ref, *refs):
    if section is None:
        weight_ref, result_ref = refs
    else:
        *blocks, result_ref, weight_ref, sems = refs
        start_copy(place_ref[0] ^ section, blocks, weight_ref, sems)
        wait_copy(blocks, weight_ref, sems)
    total = own_ref[...].astype(jnp.float32)
    total += jnp.dot(context_ref[...], weight_ref[...], preferred_element_type=jnp.float32)
    result_ref[...] = total.astype(jnp.bfloat16)


def project(kernel, place, operands, weights, section, columns):
    rows = operands[0].shape[0]
    fetch = section is not None
    depth = weights[0].shape[0] * (2 if fetch else 1)
    width = weights[0].shape[1]
    scratch = [pltpu.VMEM((depth, width), jnp.bfloat16), pltpu.SemaphoreType.DMA((2,))]
    return pl.pallas_call(
        functools.partial(kernel, section),
        out_shape=jax.ShapeDtypeStruct((rows, columns), jnp.bfloat16),
        in_specs=[IN_SMEM]
        + [IN_VMEM] * len(operands)
        + [IN_PLACE if fetch else IN_VMEM] * len(weights),
        out_specs=IN_VMEM,
        scratch_shapes=scratch if fetch else [],
        compiler_params=LIMIT,
        cost_estimate=cost(2 * rows * depth * width, 2 * depth * width),
    )(place, *operands, *weights)


def attend_kernel(width, section, place_ref, choice_ref, tiles_ref, length_ref, packed_ref, *refs):
    *blocks, result_ref, held = refs
    for distance, block_ref in enumerate(blocks):

        @pl.when(place_ref[0] ^ section == distance)
        def _():
            held[...] = block_ref[...]

    sources, rows, columns = packed_ref.shape
    heads = (columns - LANES) // HD
    keys = held.shape[0]
    first = place_ref[0] * rows
    sample = first // TXT
    key = lax.broadcasted_iota(jnp.int32, (1, keys), 1)
    valid = jnp.where(key < tiles_ref[choice_ref[sample]] * TROWS, 1.0, 0.0)
    position = first - sample * TXT + lax.broadcasted_iota(jnp.int32, (rows, 1), 0)
    live = jnp.where(position < length_ref[sample], 1.0, 0.0)
    summed = packed_ref[0].astype(jnp.float32)
    for source in range(1, sources):
        summed += packed_ref[source].astype(jnp.float32)
    squares = summed[:, heads * HD : heads * HD + 1] + summed[:, heads * HD + 1 : heads * HD + 2]
    inverse = lax.rsqrt(squares / width + epsilon) * (float(HD) ** (-0.5))
    queries = jnp.concatenate(
        [summed[:, head * HD : (head + 1) * HD] * inverse for head in range(heads)], axis=0
    ).astype(jnp.bfloat16)
    scores = lax.dot_general(
        queries,
        held[:, :HD],
        (((1,), (1,)), ((), ())),
        preferred_element_type=jnp.float32,
    )
    weighted = jnp.exp(scores) * valid
    weights = (weighted / jnp.sum(weighted, axis=-1, keepdims=True)).astype(jnp.bfloat16)
    context = jnp.dot(weights, held[:, HD:], preferred_element_type=jnp.float32)
    for head in range(heads):
        part = (context[head * rows : (head + 1) * rows] * live).astype(jnp.bfloat16)
        for target in range(result_ref.shape[0]):
            result_ref[target, :, head * HD : (head + 1) * HD] = part


def attend(place, choice, tiles, lengths, packed, keyval, section, width):
    sources, rows, columns = packed.shape
    keys = keyval[0].shape[0]
    heads = (columns - LANES) // HD
    return pl.pallas_call(
        functools.partial(attend_kernel, width, section),
        out_shape=jax.ShapeDtypeStruct((sources, rows, heads * HD), jnp.bfloat16),
        in_specs=[IN_SMEM] * 4 + [IN_VMEM] * (1 + len(keyval)),
        out_specs=IN_VMEM,
        scratch_shapes=[pltpu.VMEM(keyval[0].shape, jnp.bfloat16)],
        compiler_params=LIMIT,
        cost_estimate=cost(4 * heads * rows * keys * HD, packed.size * 2, heads * rows * keys),
    )(place, choice, tiles, lengths, packed, *keyval)


def assemble_kernel(received_ref, result_ref):
    cores, phases, slots, rows, piece = received_ref.shape
    for phase in range(phases):
        for slot in range(slots):
            for core in range(cores):
                column = (slot * cores + core) * piece
                result_ref[0, phase * rows : (phase + 1) * rows, column : column + piece] = (
                    received_ref[core, phase, slot]
                )


def assemble(received):
    cores, phases, slots, rows, piece = received.shape
    return pl.pallas_call(
        assemble_kernel,
        out_shape=jax.ShapeDtypeStruct((1, phases * rows, slots * cores * piece), received.dtype),
        in_specs=[IN_VMEM],
        out_specs=IN_VMEM,
        compiler_params=LIMIT,
        cost_estimate=cost(0, 4 * received.size),
    )(received)


def shift(part, distance):
    phases = lax.axis_size("phase")
    return lax.ppermute(part, "phase", [(i, i ^ distance) for i in range(phases)])


def bring_near(first, second):
    near_first, far_first = shift(first, 1), shift(first, 2)
    near_second, far_second = shift(second, 1), shift(second, 2)
    return first, second, near_first, near_second, far_first, far_second


def bring_across(parts, near_second, far_first):
    return *parts, shift(far_first, 1), shift(near_second, 2)


def split_kernel(slots, weight_ref, text_ref, result_ref):
    cores, _, piece = result_ref.shape
    rows, more = weight_ref.shape[0], text_ref.shape[0]
    for core in range(cores):
        for slot in range(slots):
            column, first = (slot * cores + core) * piece, slot * (rows + more)
            result_ref[core, first : first + rows] = weight_ref[:, column : column + piece]
            first += rows
            result_ref[core, first : first + more] = text_ref[:, column : column + piece]


def split_columns(weight, text, cores, slots, piece):
    rows = slots * (weight.shape[0] + text.shape[0])
    return pl.pallas_call(
        functools.partial(split_kernel, slots),
        out_shape=jax.ShapeDtypeStruct((cores, rows, piece), weight.dtype),
        in_specs=[IN_VMEM, IN_VMEM],
        out_specs=IN_VMEM,
        compiler_params=LIMIT,
        cost_estimate=cost(0, 4 * (weight.size + text.size)),
    )(weight, text)


def exchange(block, axes):
    return lax.all_to_all(block, axes, 0, 0, tiled=True)


def on_device(
    text_rows,
    image_rows,
    tile_counts,
    text_lengths,
    sample_image,
    norm_gain,
    query_weight,
    keyval_weight,
    output_weight,
    cross_gate,
):
    phases, dps, mps = (lax.axis_size(name) for name in ("phase", "dp", "mp"))
    phase_index = lax.axis_index("phase")
    width = norm_gain.shape[1]
    own_rows = text_rows.shape[0]
    part_rows = own_rows // phases
    depth, head_width = query_weight.shape[1:]
    slots = dps // mps
    piece = depth // mps
    context_part = output_weight.shape[1]

    def spread(own_part):
        return lax.all_gather(own_part, "mp", axis=1, tiled=True)

    images = [shift(image_rows, k) if k else image_rows for k in range(phases)]
    gain = lax.dynamic_slice_in_dim(norm_gain[0], lax.axis_index("dp") * depth, depth, 0)
    middle = depth // 2
    wq = [
        (query_weight[0, rows].astype(jnp.float32) * gain[rows, None]).astype(jnp.bfloat16)
        for rows in (slice(0, middle), slice(middle, depth))
    ]
    mine = lax.dynamic_slice_in_dim(text_rows, phase_index * part_rows, part_rows, 0)
    wo = split_columns(output_weight[0], mine, mps, slots, piece)
    images, wq, wo = lax.optimization_barrier((images, wq, wo))
    wq_parts = bring_near(*wq)
    wo = exchange(exchange(wo, "mp").reshape(dps, context_part + part_rows, piece), "dp")

    place = jnp.full((1,), phase_index, jnp.int32)
    images = lax.all_gather(jnp.stack(images), "mp", axis=2, tiled=True)
    keyval = project_keyval(
        part_rows, place, sample_image, cross_gate, images, keyval_weight[0, :, 0, :]
    )
    wq = bring_across(wq_parts, *wq_parts[3:5])
    keyval, _ = lax.optimization_barrier((keyval, wq_parts[2:6]))
    keyval = [shift(keyval[k], k) if k else keyval[k] for k in range(phases)]
    wo, keyval = lax.optimization_barrier((wo, keyval))
    middle = dps // 2
    own = wo[:, context_part:].reshape(dps * part_rows, piece)
    wo = wo[:, :context_part]
    wo_parts = bring_near(wo[:middle].reshape(-1, piece), wo[middle:].reshape(-1, piece))
    carried = spread(own)


    packed_width = head_width + LANES
    packed = project(query_kernel, place, [carried], wq, 0, packed_width)
    packed = exchange(packed.reshape(dps, part_rows, packed_width), "dp")
    forward, _ = lax.optimization_barrier((wo_parts[3:5], packed))
    wo = bring_across(wo_parts, *forward)
    later = range(1, phases)
    wq_later, wo_later = arrange(place, wq, later), arrange(place, wo, later)
    states = []
    for section in range(phases):
        if section:
            carried = spread(own)
            weights = [wq_later[section - 1]]
            packed = project(query_kernel, place, [carried], weights, None, packed_width)
            packed = exchange(packed.reshape(dps, part_rows, packed_width), "dp")
        context = attend(
            place, sample_image, tile_counts, text_lengths, packed, keyval, section, width
        )
        context = spread(exchange(context, "dp").reshape(dps * part_rows, head_width))
        if section == 0:
            own = project(output_kernel, place, [context, own], wo, 0, piece)
        else:
            weights = [wo_later[section - 1]]
            own = project(output_kernel, place, [context, own], weights, None, piece)
        states.append(own)
    result = jnp.stack(states).reshape(phases * dps, part_rows, piece)
    result = exchange(result, ("phase", "dp")).reshape(phases, mps, slots, part_rows, piece)
    return assemble(exchange(result.transpose(1, 0, 2, 3, 4), "mp"))


def solution(mesh):
    placed = (
        P("dp", "mp"),
        P("dp", ("phase", "mp"), None),
        P("dp"),
        P("dp"),
        P("dp"),
        P("phase", None),
        P("phase", "dp", "mp"),
        P("phase", None, "mp", None),
        P("phase", "dp", "mp"),
        P("phase"),
    )
    return jax.shard_map(
        on_device, mesh=mesh, in_specs=placed, out_specs=P("phase", "dp", "mp"), check_vma=False
    )
```
